32 devices in a mesh: gx: 4 (over x, core), gy: 2 (over y), gz: 4 (over z).
Axes of the slice: x: 2, y: 2, z: 4, core: 2. Of those that a mesh axis runs over, the one named last changes fastest.
Arguments:
- load: float32 [3, 128, 64, 512], P(None, 'gz', 'gy', 'gx'), may hold values from -6 to 6
- labels: int32 [128, 64, 512], P('gz', 'gy', 'gx'), may hold values from 0 to 15
- mask: int32 [128, 64, 512], P('gz', 'gy', 'gx'), may hold values 0 or 1
- table: float32 [16], replicated, may hold values from 0.25 to 2
Outputs:
- displacement: float32 [3, 128, 64, 512], P(None, 'gz', 'gy', 'gx')
- residual: float32 [3, 128, 64, 512], P(None, 'gz', 'gy', 'gx')
The draws below stay inside these ranges and needn't reach their ends.
All inputs are finite; a program needn't handle non-finite values. No bound on the sum of `mask` on one device may be relied on, other than what follows from the above.
Results may differ from the reference program's by a relative error of at most 0.0003.
Values sent between devices are 32-bit elements; how exact they have to be, the bound alone decides.
No kernel may reach another device: no remote copies, remote signals or barrier semaphores. Data moves between devices by JAX's collectives and lax.ppermute only.
A program may use at most 128 MiB of HBM per device.

```python
import math
import jax
import jax.numpy as jnp
from jax import lax

BRICK = 32
INTERSECTION = 4
MATERIALS = 16
SWEEPS = 2
NZ = 128
NY = 64
NX = 512


def draw_load(key, part):
    shape = (3, NZ, NY, NX)
    first = jax.random.fold_in(jax.random.fold_in(key, 11), 0)
    return jnp.clip(jax.random.normal(first, shape, jnp.float32), -6.0, 6.0)


def place_ends(values, stream_key, smallest, largest):
    spot = [jax.random.randint(jax.random.fold_in(stream_key, axis), (), 0, length) for axis, length in enumerate(values.shape)]
    longest = values.shape.index(max(values.shape))
    neighbour = spot[:longest] + [(spot[longest] + 1) % values.shape[longest]] + spot[longest + 1:]
    return values.at[tuple(spot)].set(smallest).at[tuple(neighbour)].set(largest)


def setup_inputs(seed: int = 0) -> dict:
    splits = jax.random.split(jax.random.key(seed), 5)
    load = draw_load(jax.random.fold_in(splits[4], 71), 0)
    labels = place_ends(jax.random.randint(splits[1], (NZ, NY, NX), 0, MATERIALS), jax.random.fold_in(splits[1], 1), 0, MATERIALS - 1).astype(jnp.int32)
    mask = place_ends((jax.random.randint(splits[2], (NZ, NY, NX), 0, 4) < 3).astype(jnp.int32), jax.random.fold_in(splits[2], 1), 0, 1)
    table = jnp.clip(jnp.exp(jax.random.uniform(splits[3], (MATERIALS,), jnp.float32, math.log(0.25), math.log(2.0))), 0.25, 2.0)
    return dict(load=load, labels=labels, mask=mask, table=table)


LAMBDA_RATIO = 2.0
SIGMA_SHIFT = 0.1
REF_MODULUS = 1.5
VOID_MODULUS = 0.1
HIGHEST = lax.Precision.HIGHEST

def stiffness_ratio(component, direction):
    return LAMBDA_RATIO if component == direction else 1.0

def sine_table(length):
    grid = jnp.arange(1, length + 1, dtype=jnp.float32)
    return jnp.sqrt(2.0 / (length + 1)) * jnp.sin(jnp.pi * grid[:, None] * grid[None, :] / (length + 1))

def eigen_values(length):
    grid = jnp.arange(1, length + 1, dtype=jnp.float32)
    return 2.0 - 2.0 * jnp.cos(jnp.pi * grid / (length + 1))

def ramp_weights(length, margin):
    position = jnp.arange(length, dtype=jnp.float32)
    rising = (position + 0.5) / (2 * margin)
    falling = (length - 0.5 - position) / (2 * margin)
    return jnp.minimum(jnp.minimum(rising, falling), 1.0)

def operator_core(padded_field, padded_modulus):
    centre_modulus = padded_modulus[1:-1, 1:-1, 1:-1]
    centre = padded_field[:, 1:-1, 1:-1, 1:-1]
    results = []
    for component in range(3):
        total = SIGMA_SHIFT * centre_modulus * centre[component]
        for direction in range(3):
            for offset in (0, 2):
                window = [slice(1, -1), slice(1, -1), slice(1, -1)]
                window[direction] = slice(offset, offset + centre_modulus.shape[direction])
                window = tuple(window)
                face = 0.5 * (centre_modulus + padded_modulus[window])
                total = total + stiffness_ratio(component, direction) * face * (centre[component] - padded_field[component][window])
        results.append(total)
    return jnp.stack(results)

def apply_operator(field, modulus):
    padded_field = jnp.pad(field, ((0, 0), (1, 1), (1, 1), (1, 1)))
    padded_modulus = jnp.pad(modulus, 1)
    return operator_core(padded_field, padded_modulus)

def transform_all(values, along_x, along_rest):
    values = jnp.einsum('czyx,xk->czyk', values, along_x, precision=HIGHEST)
    values = jnp.einsum('czyx,yk->czkx', values, along_rest, precision=HIGHEST)
    return jnp.einsum('czyx,zk->ckyx', values, along_rest, precision=HIGHEST)

def reference(load, labels, mask, table):
    modulus = jnp.where(mask == 1, jnp.take(table, labels), VOID_MODULUS)
    length = BRICK + 2 * INTERSECTION
    sine = sine_table(length)
    eigen = eigen_values(length)
    denominators = jnp.stack([REF_MODULUS * (stiffness_ratio(component, 0) * eigen[:, None, None] + stiffness_ratio(component, 1) * eigen[None, :, None] + stiffness_ratio(component, 2) * eigen[None, None, :] + SIGMA_SHIFT) for component in range(3)])
    ramp = ramp_weights(length, INTERSECTION)
    weight_cube = ramp[:, None, None] * ramp[None, :, None] * ramp[None, None, :]
    rows_y = NY // BRICK
    rows_x = NX // BRICK
    number_bricks = NZ // BRICK * rows_y * rows_x
    solution = jnp.zeros_like(load)
    residual = load
    for sweep in range(SWEEPS):
        padded = jnp.pad(residual, ((0, 0), (INTERSECTION, INTERSECTION), (INTERSECTION, INTERSECTION), (INTERSECTION, INTERSECTION)))

        def add_brick(total, number, padded=padded):
            layer = number // (rows_y * rows_x)
            column_y = number // rows_x % rows_y
            column_x = number % rows_x
            starts = (jnp.int32(0), (layer * BRICK).astype(jnp.int32), (column_y * BRICK).astype(jnp.int32), (column_x * BRICK).astype(jnp.int32))
            piece = lax.dynamic_slice(padded, starts, (3, length, length, length))
            solved = transform_all(transform_all(piece * weight_cube, sine, sine) / denominators, sine, sine)
            current = lax.dynamic_slice(total, starts, (3, length, length, length))
            return (lax.dynamic_update_slice(total, current + solved, starts), None)
        summed, _ = lax.scan(add_brick, jnp.zeros_like(padded), jnp.arange(number_bricks, dtype=jnp.int32))
        correction = summed[:, INTERSECTION:-INTERSECTION, INTERSECTION:-INTERSECTION, INTERSECTION:-INTERSECTION]
        solution = solution + correction
        residual = residual - apply_operator(correction, modulus)
    return (solution, residual)
```

```python
import functools

import jax
import jax.numpy as jnp
import ml_dtypes
import numpy as np
from jax import lax
from jax.experimental import pallas as pl
from jax.experimental.pallas import tpu as pltpu
from jax.sharding import PartitionSpec as P

BRICK = 32
INTERSECTION = 4
LENGTH = BRICK + 2 * INTERSECTION
REACH = INTERSECTION + 1
WIDE = BRICK + 2 * REACH
LANES = 128
PAD = 8
FOLD = 2 * INTERSECTION + 1

LAMBDA_RATIO = 2.0
SIGMA_SHIFT = 0.1
REF_MODULUS = 1.5
VOID_MODULUS = 0.1

F32 = jnp.float32
BF16 = jnp.bfloat16
VMEM = pl.BlockSpec(memory_space=pltpu.VMEM)
SMEM = pl.BlockSpec(memory_space=pltpu.SMEM)


def halves(values):
    values = np.asarray(values, np.float32)
    high = values.astype(ml_dtypes.bfloat16)
    low = (values - high.astype(np.float32)).astype(ml_dtypes.bfloat16)
    return high, low


def right_table(values):
    high, low = halves(values)
    return np.block([[high, low], [high, np.zeros_like(low)]]).astype(ml_dtypes.bfloat16)


def left_table(values):
    high, low = halves(values)
    return np.concatenate([high, high, low], axis=1)


def tables(count_x):
    grid = np.arange(1, LENGTH + 1, dtype=np.float64)
    sine = np.sqrt(2.0 / (LENGTH + 1)) * np.sin(np.pi * np.outer(grid, grid) / (LENGTH + 1))
    eigen = 2.0 - 2.0 * np.cos(np.pi * grid / (LENGTH + 1))
    position = np.arange(LENGTH, dtype=np.float64)
    margin = 2 * INTERSECTION
    ramp = np.minimum(
        np.minimum((position + 0.5) / margin, (LENGTH - 0.5 - position) / margin), 1.0
    )
    rows = count_x * BRICK + 2 * PAD
    ramped = ramp[:, None] * sine
    along_y = np.zeros((LANES, LANES))
    back_y = np.zeros((LANES, LANES))
    for c in range(3):
        lane = c * WIDE + 1
        along_y[lane : lane + LENGTH, c * LENGTH : (c + 1) * LENGTH] = ramped
        back_y[c * LENGTH : (c + 1) * LENGTH, lane : lane + LENGTH] = sine
    along_x = np.zeros((count_x * LENGTH, rows))
    back_x = np.zeros((rows, count_x * LENGTH))
    for b in range(count_x):
        row = b * BRICK + PAD - INTERSECTION
        along_x[b * LENGTH : (b + 1) * LENGTH, row : row + LENGTH] = ramped.T
        back_x[row : row + LENGTH, b * LENGTH : (b + 1) * LENGTH] = sine
    half = LENGTH // 2
    eye = np.eye(8)
    even = left_table(np.kron(ramped[:half, 0::2].T, eye))
    odd = left_table(np.kron(ramped[:half, 1::2].T, eye))
    back_even = left_table(np.kron(sine[0::2, :half].T, eye))
    back_odd = left_table(np.kron(sine[1::2, :half].T, eye))
    ratio = lambda c, d: LAMBDA_RATIO if c == d else 1.0
    base = np.ones((count_x * LENGTH, LANES))
    steps = np.zeros((LENGTH, 8, LANES))
    order = np.concatenate([np.arange(0, LENGTH, 2), np.arange(1, LENGTH, 2)])
    for c in range(3):
        part = slice(c * LENGTH, (c + 1) * LENGTH)
        base[:, part] = REF_MODULUS * (
            ratio(c, 1) * eigen[None, :]
            + ratio(c, 2) * np.tile(eigen, count_x)[:, None]
            + SIGMA_SHIFT
        )
        steps[:, :, part] = REF_MODULUS * ratio(c, 0) * eigen[order][:, None, None]
    return [
        right_table(along_y),
        left_table(along_x),
        even,
        odd,
        back_even,
        back_odd,
        left_table(back_x),
        right_table(back_y),
        base.astype(np.float32),
        steps.astype(np.float32),
    ]


def phases(count):
    return 1 if count <= 2 else 2


def partners(count, phase):
    found = [i + 1 if (i + phase) % 2 == 0 else i - 1 for i in range(count)]
    return [j if 0 <= j < count else i for i, j in enumerate(found)]


def swap(value, axis, phase):
    target = partners(lax.axis_size(axis), phase)
    return lax.ppermute(value, axis, list(enumerate(target)))


def swap_both(value, first, phase_first, second, phase_second):
    rows = lax.axis_size(first)
    columns = lax.axis_size(second)
    one = partners(rows, phase_first)
    two = partners(columns, phase_second)
    pairs = []
    for i in range(rows):
        for j in range(columns):
            moved = one[i] != i and two[j] != j
            to = one[i] * columns + two[j] if moved else i * columns + j
            pairs.append((i * columns + j, to))
    return lax.ppermute(value, (first, second), pairs)


def spots(shape):
    lane = lax.broadcasted_iota(jnp.int32, shape, len(shape) - 1)
    region = jnp.where(lane >= 3 * WIDE, 3, jnp.where(lane >= 2 * WIDE, 2, jnp.where(lane >= WIDE, 1, 0)))
    spot = jnp.where(region == 3, 4 * LANES, lane - region * WIDE)
    return spot, region


def turn(values, shift):
    return pltpu.roll(values, lax.rem(shift + 2 * LANES, LANES), values.ndim - 1)


def pack(planes, width, start, spot, groups):
    total = jnp.zeros(spot.shape, F32)
    for g, plane in enumerate(planes):
        inside = (spot >= g * width) & (spot < (g + 1) * width)
        total = jnp.where(inside, turn(plane, g * width - start), total)
    return total


def unpack(packed, g, width, start, spot, use):
    inside = (spot >= start) & (spot < start + width) & use
    return jnp.where(inside, turn(packed, start - g * width), 0.0)


def side(pos_ref, dim, phase, count):
    place = pos_ref[dim]
    up = lax.rem(place + phase, 2) == 0
    use = jnp.where(up, place < count - 1, place > 0)
    return up, use


def pick(up, high, low):
    return jnp.where(up, high, low)


def two_terms(values):
    high = values.astype(BF16)
    low = (values - high.astype(F32)).astype(BF16)
    return high, low


def right_product(values, table):
    high, low = two_terms(values)
    product = jnp.dot(jnp.concatenate([high, low], axis=1), table, preferred_element_type=F32)
    return product[:, :LANES] + product[:, LANES:]


def left_product(table, values):
    high, low = two_terms(values)
    return jnp.dot(
        table, jnp.concatenate([high, low, high], axis=0), preferred_element_type=F32
    )


def solve(source, mid, target, consts):
    along_y, along_x, even, odd, back_even, back_odd, back_x, back_y, base, steps = consts
    rows = source.shape[1]
    half = LENGTH // 2

    def forward(t, _):
        both = jnp.concatenate([source[2 * t], source[2 * t + 1]], axis=0)
        turned = right_product(both, along_y[...])
        pair = jnp.concatenate([turned[:rows], turned[rows:]], axis=1)
        done = left_product(along_x[...], pair)
        mid[2 * t] = done[:, :LANES]
        mid[2 * t + 1] = done[:, LANES:]
        return 0

    lax.fori_loop(0, half, forward, 0)

    def across(g, _):
        start = pl.multiple_of(g * 16, 16)

        def plane(z):
            return jnp.concatenate(
                [mid[z, pl.ds(start, 8), :], mid[z, pl.ds(start + 8, 8), :]], axis=1
            )

        planes = [plane(z) for z in range(LENGTH)]
        sums = jnp.concatenate([planes[z] + planes[LENGTH - 1 - z] for z in range(half)], axis=0)
        gaps = jnp.concatenate([planes[z] - planes[LENGTH - 1 - z] for z in range(half)], axis=0)
        ground = jnp.concatenate(
            [base[pl.ds(start, 8), :], base[pl.ds(start + 8, 8), :]], axis=1
        )

        def divisors(first):
            return jnp.concatenate(
                [
                    ground + jnp.concatenate([steps[first + k], steps[first + k]], axis=1)
                    for k in range(half)
                ],
                axis=0,
            )

        near = left_product(back_even[...], left_product(even[...], sums) / divisors(0))
        far = left_product(back_odd[...], left_product(odd[...], gaps) / divisors(half))
        lower = near + far
        upper = near - far
        for z in range(half):
            for h in range(2):
                lanes = slice(h * LANES, (h + 1) * LANES)
                mid[z, pl.ds(start + 8 * h, 8), :] = lower[8 * z : 8 * z + 8, lanes]
                mid[LENGTH - 1 - z, pl.ds(start + 8 * h, 8), :] = upper[8 * z : 8 * z + 8, lanes]
        return 0

    lax.fori_loop(0, mid.shape[1] // 16, across, 0)

    def backward(t, _):
        pair = jnp.concatenate([mid[2 * t], mid[2 * t + 1]], axis=1)
        done = left_product(back_x[...], pair)
        both = jnp.concatenate([done[:, :LANES], done[:, LANES:]], axis=0)
        turned = right_product(both, back_y[...])
        target[2 * t] = turned[:rows]
        target[2 * t + 1] = turned[rows:]
        return 0

    lax.fori_loop(0, half, backward, 0)


def write_messages(pos_ref, solved, width, counts, outs_y, outs_z, outs_yz):
    rows = solved.shape[1]
    spot, _ = spots((rows, LANES))
    groups = WIDE // width
    _, count_y, count_z = counts
    for phase, out in enumerate(outs_z):
        up, _ = side(pos_ref, 0, phase, count_z)
        first = pick(up, LENGTH - width, 0)
        for i in range(width):
            out[i] = solved[first + i]
    for phase, out in enumerate(outs_y):
        up, _ = side(pos_ref, 1, phase, count_y)
        start = pick(up, WIDE - 1 - width, 1)
        many = LENGTH // groups

        def one(k, _, out=out, start=start, many=many):
            out[k] = pack(
                [solved[g * many + k] for g in range(groups)], width, start, spot, groups
            )
            return 0

        lax.fori_loop(0, many, one, 0)
    for number, out in enumerate(outs_yz):
        phase_y, phase_z = divmod(number, len(outs_z))
        up_y, _ = side(pos_ref, 1, phase_y, count_y)
        up_z, _ = side(pos_ref, 0, phase_z, count_z)
        start = pick(up_y, WIDE - 1 - width, 1)
        first = pick(up_z, LENGTH - width, 0)
        many = out.shape[0]
        for k in range(many):
            planes = [
                solved[first + g * many + k] for g in range(groups) if g * many + k < width
            ]
            out[k] = pack(planes, width, start, spot, groups)


def add_messages(pos_ref, solved, width, counts, ins_y, ins_z, ins_yz, field):
    rows = solved.shape[1]
    spot, _ = spots((rows, LANES))
    groups = WIDE // width
    _, count_y, count_z = counts
    first_y = [side(pos_ref, 1, phase, count_y) for phase in range(len(ins_y))]
    first_z = [side(pos_ref, 0, phase, count_z) for phase in range(len(ins_z))]
    many = LENGTH // groups

    def one(k, _):
        for g in range(groups):
            total = solved[g * many + k]
            for (up, use), ref in zip(first_y, ins_y):
                start = pick(up, WIDE - FOLD, FOLD - width)
                total = total + unpack(ref[k], g, width, start, spot, use)
            field[g * many + k + 1] = total
        return 0

    lax.fori_loop(0, many, one, 0)
    field[0] = jnp.zeros((rows, LANES), F32)
    field[WIDE - 1] = jnp.zeros((rows, LANES), F32)
    for phase_z, ((up_z, use_z), ref_z) in enumerate(zip(first_z, ins_z)):
        first = pick(up_z, WIDE - FOLD, FOLD - width)
        for i in range(width):
            total = ref_z[i]
            for phase_y, (up_y, use_y) in enumerate(first_y):
                ref = ins_yz[phase_y * len(ins_z) + phase_z]
                g, k = divmod(i, ref.shape[0])
                start = pick(up_y, WIDE - FOLD, FOLD - width)
                total = total + unpack(ref[k], g, width, start, spot, use_y)
            field[first + i] = field[first + i] + jnp.where(use_z, total, 0.0)


def grid_masks(pos_ref, rows, counts):
    count_x, count_y, count_z = counts
    spot, _ = spots((rows, LANES))
    row = lax.broadcasted_iota(jnp.int32, (rows, LANES), 0)
    low_y = pick(pos_ref[1] > 0, 0, REACH)
    high_y = pick(pos_ref[1] < count_y - 1, WIDE, REACH + BRICK)
    low_x = pick(pos_ref[2] > 0, 0, PAD)
    high_x = pick(pos_ref[2] < count_x - 1, rows, rows - PAD)
    inside = (spot >= low_y) & (spot < high_y) & (row >= low_x) & (row < high_x)
    low_z = pick(pos_ref[0] > 0, 0, REACH)
    high_z = pick(pos_ref[0] < count_z - 1, WIDE, REACH + BRICK)
    return inside, low_z, high_z


def complete(pos_ref, counts, partial, ins_x, field, first, last):
    rows = field.shape[1]
    inside, low_z, high_z = grid_masks(pos_ref, rows, counts)
    sides = [side(pos_ref, 2, phase, counts[0]) for phase in range(len(ins_x))]

    def one(z, _):
        on = inside & (z >= low_z) & (z < high_z)
        field[z] = partial[z]
        for (up, use), ref in zip(sides, ins_x):
            start = pl.multiple_of(pick(up, rows - 2 * PAD, 0), 2 * PAD)
            part = field[z, pl.ds(start, 2 * PAD), :]
            field[z, pl.ds(start, 2 * PAD), :] = part + jnp.where(use, ref[z], 0.0)
        field[z] = jnp.where(on, field[z], 0.0)
        return 0

    lax.fori_loop(first, last + 1, one, 0)


def stiffness(field, modulus, first, last, store):
    rows = field.shape[1]
    _, region = spots((rows, LANES))
    scale = [
        jnp.where(region == c, 0.5 * LAMBDA_RATIO, 0.5) for c in range(3)
    ]

    def rise(z):
        return (modulus[z] + modulus[z + 1]) * (field[z + 1] - field[z])

    def one(z, below):
        v = field[z]
        m = modulus[z]
        above = rise(z)
        gx = (m + pltpu.roll(m, rows - 1, 0)) * (pltpu.roll(v, rows - 1, 0) - v)
        gy = (m + pltpu.roll(m, LANES - 1, 1)) * (pltpu.roll(v, LANES - 1, 1) - v)
        total = SIGMA_SHIFT * m * v + scale[0] * (below - above)
        total = total + scale[1] * (pltpu.roll(gy, 1, 1) - gy)
        total = total + scale[2] * (pltpu.roll(gx, 1, 0) - gx)
        store(z, total)
        return above

    lax.fori_loop(first, last + 1, one, rise(first - 1))


def groups_of(refs, sizes):
    found = []
    at = 0
    for size in sizes:
        found.append(refs[at : at + size])
        at += size
    return found


def prepare_kernel(counts, sizes, pos_ref, table_ref, load, labels, mask, *refs):
    (load_out, modulus_out), outs_y, outs_z, outs_yz, (wide_load, wide_modulus) = groups_of(
        refs, (2,) + sizes[:3] + (2,)
    )
    columns = load.shape[3]
    wide_load[...] = jnp.zeros(wide_load.shape, F32)
    wide_modulus[...] = jnp.zeros(wide_modulus.shape, F32)

    def one(z, _):
        label = labels[z]
        looked = jnp.zeros(label.shape, F32)
        for k in range(table_ref.shape[0]):
            looked = jnp.where(label == k, table_ref[k], looked)
        value = jnp.where(mask[z] == 1, looked, VOID_MODULUS)
        for c in range(3):
            lane = c * WIDE + REACH
            wide_load[lane : lane + BRICK, :] = load[c, z]
            wide_modulus[lane : lane + BRICK, :] = value
        load_out[z] = wide_load[...].T
        modulus_out[z] = wide_modulus[...].T
        return 0

    lax.fori_loop(0, BRICK, one, 0)

    spot, region = spots((columns, LANES))
    _, count_y, count_z = counts
    groups = WIDE // REACH
    many = BRICK // groups
    for phase, out in enumerate(outs_z):
        up, _ = side(pos_ref, 0, phase, count_z)
        first = pick(up, BRICK - INTERSECTION, 0)
        for i in range(INTERSECTION):
            out[i] = load_out[first + i]
        first = pick(up, BRICK - REACH, 0)
        for k in range(2):
            total = modulus_out[first + k]
            for c in (1, 2):
                i = min(2 * c + k, REACH - 1)
                total = jnp.where(region == c, modulus_out[first + i], total)
            out[INTERSECTION + k] = total
    for phase, out in enumerate(outs_y):
        up, _ = side(pos_ref, 1, phase, count_y)
        start = pick(up, BRICK, REACH)
        for k in range(many):
            out[k] = pack(
                [load_out[g * many + k] for g in range(groups)], REACH, start, spot, groups
            )
        for k in range(2):
            total = jnp.zeros((columns, LANES), F32)
            for g in range(groups):
                turned = [
                    turn(modulus_out[(c * groups + g) * 2 + k], g * REACH - start)
                    for c in range(2)
                ]
                chosen = jnp.where(region == 0, turned[0], turned[1])
                inside = (spot >= g * REACH) & (spot < (g + 1) * REACH)
                total = jnp.where(inside, chosen, total)
            out[many + k] = total
    for number, out in enumerate(outs_yz):
        phase_y, phase_z = divmod(number, len(outs_z))
        up_y, _ = side(pos_ref, 1, phase_y, count_y)
        up_z, _ = side(pos_ref, 0, phase_z, count_z)
        start = pick(up_y, BRICK, REACH)
        first = pick(up_z, BRICK - INTERSECTION, 0)
        out[0] = pack(
            [load_out[first + i] for i in range(INTERSECTION)], REACH, start, spot, groups
        )
        first = pick(up_z, BRICK - REACH, 0)
        out[1] = pack([modulus_out[first + i] for i in range(REACH)], REACH, start, spot, groups)


def spread(values, region, source):
    total = jnp.zeros(values.shape, F32)
    for c in range(3):
        total = jnp.where(region == c, turn(values, (c - source) * WIDE), total)
    return total


def gather_kernel(counts, sizes, pos_ref, load, modulus, *refs):
    ins_y, ins_z, ins_yz, (load_out, modulus_out), outs_x = groups_of(
        refs, sizes[:3] + (2, sizes[3])
    )
    columns = load.shape[1]
    rows = columns + 2 * PAD
    core = slice(PAD, PAD + columns)
    spot, region = spots((columns, LANES))
    count_x, count_y, count_z = counts
    groups = WIDE // REACH
    many = BRICK // groups
    sides_y = [side(pos_ref, 1, phase, count_y) for phase in range(len(ins_y))]
    sides_z = [side(pos_ref, 0, phase, count_z) for phase in range(len(ins_z))]
    blank = jnp.zeros((PAD, LANES), F32)

    def store(out, z, value):
        out[z, :PAD, :] = blank
        out[z, core, :] = value
        out[z, rows - PAD :, :] = blank

    for z in range(BRICK):
        g, k = divmod(z, many)
        total = load[z]
        for (up, use), ref in zip(sides_y, ins_y):
            start = pick(up, REACH + BRICK, 0)
            total = total + unpack(ref[k], g, REACH, start, spot, use)
        store(load_out, z + INTERSECTION, total)
        c, rest = divmod(z, 2 * groups)
        g, k = divmod(rest, 2)
        total = modulus[z]
        for (up, use), ref in zip(sides_y, ins_y):
            start = pick(up, REACH + BRICK, 0)
            whole = spread(ref[many + k], region, c)
            total = total + unpack(whole, g, REACH, start, spot, use)
        store(modulus_out, z + REACH, total)
    zero = jnp.zeros((columns, LANES), F32)
    for i in range(INTERSECTION):
        store(load_out, i, zero)
        store(load_out, LENGTH - 1 - i, zero)
    for i in range(REACH):
        store(modulus_out, i, zero)
        store(modulus_out, WIDE - 1 - i, zero)
    for phase_z, ((up_z, use_z), ref_z) in enumerate(zip(sides_z, ins_z)):
        first = pick(up_z, INTERSECTION + BRICK, 0)
        for i in range(INTERSECTION):
            total = ref_z[i]
            for phase_y, (up_y, use_y) in enumerate(sides_y):
                ref = ins_yz[phase_y * len(ins_z) + phase_z]
                start = pick(up_y, REACH + BRICK, 0)
                total = total + unpack(ref[0], i, REACH, start, spot, use_y)
            load_out[first + i, core, :] = load_out[first + i, core, :] + jnp.where(
                use_z, total, 0.0
            )
        first = pick(up_z, REACH + BRICK, 0)
        for i in range(REACH):
            c, k = divmod(i, 2)
            total = spread(ref_z[INTERSECTION + k], region, c)
            for phase_y, (up_y, use_y) in enumerate(sides_y):
                ref = ins_yz[phase_y * len(ins_z) + phase_z]
                start = pick(up_y, REACH + BRICK, 0)
                total = total + unpack(ref[1], i, REACH, start, spot, use_y)
            modulus_out[first + i, core, :] = modulus_out[first + i, core, :] + jnp.where(
                use_z, total, 0.0
            )
    _, edge_region = spots((PAD, LANES))
    third = WIDE // 3
    for phase, out in enumerate(outs_x):
        up, _ = side(pos_ref, 2, phase, count_x)
        start = pl.multiple_of(pick(up, rows - 2 * PAD, PAD), PAD)
        for z in range(LENGTH):
            out[z] = load_out[z, pl.ds(start, PAD), :]
        for k in range(third):
            total = modulus_out[k, pl.ds(start, PAD), :]
            for c in (1, 2):
                part = modulus_out[k + c * third, pl.ds(start, PAD), :]
                total = jnp.where(edge_region == c, part, total)
            out[LENGTH + k] = total


def first_kernel(counts, sizes, pos_ref, load, modulus, *refs):
    ins_x, consts, (field_out, modulus_out, solved), outs_y, outs_z, outs_yz, (mid,) = groups_of(
        refs, (sizes[3], 10, 3) + sizes[:3] + (1,)
    )
    rows = load.shape[1]
    _, region = spots((PAD, LANES))
    sides = [side(pos_ref, 2, phase, counts[0]) for phase in range(len(ins_x))]
    third = WIDE // 3

    def copy(z, _):
        field_out[z] = load[z]
        modulus_out[z] = modulus[z]
        return 0

    lax.fori_loop(0, LENGTH, copy, 0)
    for z in range(LENGTH, WIDE):
        modulus_out[z] = modulus[z]
    for (up, use), ref in zip(sides, ins_x):
        start = pl.multiple_of(pick(up, rows - PAD, 0), PAD)
        for z in range(LENGTH):
            part = field_out[z, pl.ds(start, PAD), :]
            field_out[z, pl.ds(start, PAD), :] = part + jnp.where(use, ref[z], 0.0)
        for z in range(WIDE):
            c, k = divmod(z, third)
            part = modulus_out[z, pl.ds(start, PAD), :]
            modulus_out[z, pl.ds(start, PAD), :] = part + jnp.where(
                use, spread(ref[LENGTH + k], region, c), 0.0
            )
    solve(field_out, mid, solved, consts)
    write_messages(pos_ref, solved, FOLD, counts, outs_y, outs_z, outs_yz)


def fold_kernel(width, counts, sizes, pos_ref, solved, *refs):
    ins_y, ins_z, ins_yz, (field,), outs_x = groups_of(refs, sizes[:3] + (1, sizes[3]))
    rows = solved.shape[1]
    add_messages(pos_ref, solved, width, counts, ins_y, ins_z, ins_yz, field)
    for phase, out in enumerate(outs_x):
        up, _ = side(pos_ref, 2, phase, counts[0])
        start = pl.multiple_of(pick(up, rows - 2 * PAD, 0), 2 * PAD)
        for z in range(WIDE):
            out[z] = field[z, pl.ds(start, 2 * PAD), :]


def second_kernel(counts, sizes, pos_ref, partial, residual, modulus, *refs):
    (
        ins_x,
        consts,
        (solved, moved, left),
        outs_y,
        outs_z,
        outs_yz,
        (mid, field, renewed),
    ) = groups_of(refs, (sizes[3], 10, 3) + sizes[:3] + (3,))
    rows = partial.shape[1]
    complete(pos_ref, counts, partial, ins_x, field, 0, WIDE - 1)
    inside, low_z, high_z = grid_masks(pos_ref, rows, counts)

    def store(z, product):
        on = inside & (z >= low_z) & (z < high_z)
        renewed[z - 1] = jnp.where(on, residual[z - 1] - product, 0.0)

    stiffness(field, modulus, 1, WIDE - 2, store)

    def keep(z, _):
        moved[z] = field[z + REACH, PAD : rows - PAD, :]
        left[z] = renewed[z + INTERSECTION, PAD : rows - PAD, :]
        return 0

    lax.fori_loop(0, BRICK, keep, 0)
    solve(renewed, mid, solved, consts)
    write_messages(pos_ref, solved, REACH, counts, outs_y, outs_z, outs_yz)


def last_kernel(counts, sizes, pos_ref, partial, modulus, moved, left, *refs):
    ins_x, (displacement, residual), (field, turned_one, turned_two) = groups_of(
        refs, (sizes[3], 2, 3)
    )
    rows = partial.shape[1]
    complete(pos_ref, counts, partial, ins_x, field, INTERSECTION, REACH + BRICK)
    core = slice(PAD, rows - PAD)

    def store(z, product):
        at = z - REACH
        turned_one[...] = (moved[at] + field[z, core, :]).T
        turned_two[...] = (left[at] - product[core]).T
        for c in range(3):
            lane = c * WIDE + REACH
            displacement[c, at] = turned_one[lane : lane + BRICK, :]
            residual[c, at] = turned_two[lane : lane + BRICK, :]

    stiffness(field, modulus, REACH, REACH + BRICK - 1, store)


def call(kernel, inputs, outs, scratch=(), smem=1):
    return pl.pallas_call(
        kernel,
        out_shape=[jax.ShapeDtypeStruct(shape, F32) for shape in outs],
        in_specs=[SMEM] * smem + [VMEM] * (len(inputs) - smem),
        out_specs=[VMEM] * len(outs),
        scratch_shapes=[pltpu.VMEM(shape, F32) for shape in scratch],
        compiler_params=pltpu.CompilerParams(vmem_limit_bytes=48 * 1024 * 1024),
    )(*inputs)


def local(load, labels, mask, table):
    columns = load.shape[3]
    rows = columns + 2 * PAD
    counts = tuple(lax.axis_size(axis) for axis in ("gx", "gy", "gz"))
    ways = tuple(phases(count) for count in counts)
    sizes = (ways[1], ways[2], ways[1] * ways[2], ways[0])
    pos = jnp.stack([lax.axis_index(axis) for axis in ("gz", "gy", "gx")]).astype(jnp.int32)
    consts = [jnp.asarray(value) for value in tables(columns // BRICK)]
    spectral = (LENGTH, columns // BRICK * LENGTH, LANES)

    def exchange_yz(values):
        y, z, yz = groups_of(values, sizes[:3])
        z = [swap(value, "gz", phase) for phase, value in enumerate(z)]
        y = [swap(value, "gy", phase) for phase, value in enumerate(y)]
        yz = [
            swap_both(value, "gy", number // ways[2], "gz", number % ways[2])
            for number, value in enumerate(yz)
        ]
        return [*y, *z, *yz]

    def exchange_x(values):
        return [swap(value, "gx", phase) for phase, value in enumerate(values)]

    def message_shapes(width, height):
        groups = WIDE // width
        return (
            [(LENGTH // groups, height, LANES)] * sizes[0]
            + [(width, height, LANES)] * sizes[1]
            + [(-(-width // groups), height, LANES)] * sizes[2]
        )

    bind = lambda kernel, *first: functools.partial(kernel, *first, counts, sizes)
    core = (BRICK, columns, LANES)
    tall = (LENGTH, rows, LANES)
    wide = (WIDE, rows, LANES)
    many = BRICK // (WIDE // REACH)

    load_core, modulus_core, *out = call(
        bind(prepare_kernel),
        [pos, table, load, labels, mask],
        [core, core]
        + [(many + 2, columns, LANES)] * sizes[0]
        + [(INTERSECTION + 2, columns, LANES)] * sizes[1]
        + [(2, columns, LANES)] * sizes[2],
        [(LANES, columns)] * 2,
        smem=2,
    )
    residual, modulus, *out = call(
        bind(gather_kernel),
        [pos, load_core, modulus_core, *exchange_yz(out)],
        [tall, wide] + [(LENGTH + WIDE // 3, PAD, LANES)] * sizes[3],
    )
    residual, modulus, solved, *out = call(
        bind(first_kernel),
        [pos, residual, modulus, *exchange_x(out), *consts],
        [tall, wide, tall] + message_shapes(FOLD, rows),
        [spectral],
    )
    partial, *out = call(
        bind(fold_kernel, FOLD),
        [pos, solved, *exchange_yz(out)],
        [wide] + [(WIDE, 2 * PAD, LANES)] * sizes[3],
    )
    solved, moved, left, *out = call(
        bind(second_kernel),
        [pos, partial, residual, modulus, *exchange_x(out), *consts],
        [tall, core, core] + message_shapes(REACH, rows),
        [spectral, wide, tall],
    )
    partial, *out = call(
        bind(fold_kernel, REACH),
        [pos, solved, *exchange_yz(out)],
        [wide] + [(WIDE, 2 * PAD, LANES)] * sizes[3],
    )
    displacement, residual = call(
        bind(last_kernel),
        [pos, partial, modulus, moved, left, *exchange_x(out)],
        [load.shape, load.shape],
        [wide] + [(LANES, columns)] * 2,
    )
    return displacement, residual


def solution(mesh):
    placed = (P(None, "gz", "gy", "gx"), P("gz", "gy", "gx"), P("gz", "gy", "gx"), P())
    return jax.shard_map(
        local,
        mesh=mesh,
        in_specs=placed,
        out_specs=(P(None, "gz", "gy", "gx"), P(None, "gz", "gy", "gx")),
        check_vma=False,
    )
```

```python
import functools

import jax
import jax.numpy as jnp
import ml_dtypes
import numpy as np
from jax import lax
from jax.experimental import pallas as pl
from jax.experimental.pallas import tpu as pltpu
from jax.sharding import PartitionSpec as P

BRICK = 32
INTERSECTION = 4
LENGTH = BRICK + 2 * INTERSECTION
REACH = INTERSECTION + 1
WIDE = BRICK + 2 * REACH
LANES = 128
PAD = 8
FOLD = 2 * INTERSECTION + 1

LAMBDA_RATIO = 2.0
SIGMA_SHIFT = 0.1
REF_MODULUS = 1.5
VOID_MODULUS = 0.1

F32 = jnp.float32
BF16 = jnp.bfloat16
VMEM = pl.BlockSpec(memory_space=pltpu.VMEM)
SMEM = pl.BlockSpec(memory_space=pltpu.SMEM)


def halves(values):
    values = np.asarray(values, np.float32)
    high = values.astype(ml_dtypes.bfloat16)
    low = (values - high.astype(np.float32)).astype(ml_dtypes.bfloat16)
    return high, low


def right_table(values):
    high, low = halves(values)
    return np.block([[high, low], [high, np.zeros_like(low)]]).astype(ml_dtypes.bfloat16)


def left_table(values):
    high, low = halves(values)
    return np.concatenate([high, high, low], axis=1)


def tables(count_x):
    grid = np.arange(1, LENGTH + 1, dtype=np.float64)
    sine = np.sqrt(2.0 / (LENGTH + 1)) * np.sin(np.pi * np.outer(grid, grid) / (LENGTH + 1))
    eigen = 2.0 - 2.0 * np.cos(np.pi * grid / (LENGTH + 1))
    position = np.arange(LENGTH, dtype=np.float64)
    margin = 2 * INTERSECTION
    ramp = np.minimum(
        np.minimum((position + 0.5) / margin, (LENGTH - 0.5 - position) / margin), 1.0
    )
    rows = count_x * BRICK + 2 * PAD
    ramped = ramp[:, None] * sine
    along_y = np.zeros((LANES, LANES))
    back_y = np.zeros((LANES, LANES))
    for c in range(3):
        lane = c * WIDE + 1
        along_y[lane : lane + LENGTH, c * LENGTH : (c + 1) * LENGTH] = ramped
        back_y[c * LENGTH : (c + 1) * LENGTH, lane : lane + LENGTH] = sine
    along_x = np.zeros((count_x * LENGTH, rows))
    back_x = np.zeros((rows, count_x * LENGTH))
    for b in range(count_x):
        row = b * BRICK + PAD - INTERSECTION
        along_x[b * LENGTH : (b + 1) * LENGTH, row : row + LENGTH] = ramped.T
        back_x[row : row + LENGTH, b * LENGTH : (b + 1) * LENGTH] = sine
    half = LENGTH // 2
    eye = np.eye(8)
    even = left_table(np.kron(ramped[:half, 0::2].T, eye))
    odd = left_table(np.kron(ramped[:half, 1::2].T, eye))
    back_even = left_table(np.kron(sine[0::2, :half].T, eye))
    back_odd = left_table(np.kron(sine[1::2, :half].T, eye))
    ratio = lambda c, d: LAMBDA_RATIO if c == d else 1.0
    base = np.ones((count_x * LENGTH, LANES))
    steps = np.zeros((LENGTH, 8, LANES))
    order = np.concatenate([np.arange(0, LENGTH, 2), np.arange(1, LENGTH, 2)])
    for c in range(3):
        part = slice(c * LENGTH, (c + 1) * LENGTH)
        base[:, part] = REF_MODULUS * (
            ratio(c, 1) * eigen[None, :]
            + ratio(c, 2) * np.tile(eigen, count_x)[:, None]
            + SIGMA_SHIFT
        )
        steps[:, :, part] = REF_MODULUS * ratio(c, 0) * eigen[order][:, None, None]
    return [
        right_table(along_y),
        left_table(along_x),
        even,
        odd,
        back_even,
        back_odd,
        left_table(back_x),
        right_table(back_y),
        base.astype(np.float32),
        steps.astype(np.float32),
    ]


def phases(count):
    return 1 if count <= 2 else 2


def partners(count, phase):
    found = [i + 1 if (i + phase) % 2 == 0 else i - 1 for i in range(count)]
    return [j if 0 <= j < count else i for i, j in enumerate(found)]


def swap(value, axis, phase):
    target = partners(lax.axis_size(axis), phase)
    return lax.ppermute(value, axis, list(enumerate(target)))


def swap_both(value, first, phase_first, second, phase_second):
    rows = lax.axis_size(first)
    columns = lax.axis_size(second)
    one = partners(rows, phase_first)
    two = partners(columns, phase_second)
    pairs = []
    for i in range(rows):
        for j in range(columns):
            moved = one[i] != i and two[j] != j
            to = one[i] * columns + two[j] if moved else i * columns + j
            pairs.append((i * columns + j, to))
    return lax.ppermute(value, (first, second), pairs)


def spots(shape):
    lane = lax.broadcasted_iota(jnp.int32, shape, len(shape) - 1)
    region = jnp.where(lane >= 3 * WIDE, 3, jnp.where(lane >= 2 * WIDE, 2, jnp.where(lane >= WIDE, 1, 0)))
    spot = jnp.where(region == 3, 4 * LANES, lane - region * WIDE)
    return spot, region


def turn(values, shift):
    return pltpu.roll(values, lax.rem(shift + 2 * LANES, LANES), values.ndim - 1)


def pack(planes, width, start, spot, groups):
    total = jnp.zeros(spot.shape, F32)
    for g, plane in enumerate(planes):
        inside = (spot >= g * width) & (spot < (g + 1) * width)
        total = jnp.where(inside, turn(plane, g * width - start), total)
    return total


def unpack(packed, g, width, start, spot, use):
    inside = (spot >= start) & (spot < start + width) & use
    return jnp.where(inside, turn(packed, start - g * width), 0.0)


def side(pos_ref, dim, phase, count):
    place = pos_ref[dim]
    up = lax.rem(place + phase, 2) == 0
    use = jnp.where(up, place < count - 1, place > 0)
    return up, use


def pick(up, high, low):
    return jnp.where(up, high, low)


def two_terms(values):
    high = values.astype(BF16)
    low = (values - high.astype(F32)).astype(BF16)
    return high, low


def right_product(values, table):
    high, low = two_terms(values)
    product = jnp.dot(jnp.concatenate([high, low], axis=1), table, preferred_element_type=F32)
    return product[:, :LANES] + product[:, LANES:]


def left_product(table, values):
    high, low = two_terms(values)
    return jnp.dot(
        table, jnp.concatenate([high, low, high], axis=0), preferred_element_type=F32
    )


def solve(source, mid, target, consts):
    along_y, along_x, even, odd, back_even, back_odd, back_x, back_y, base, steps = consts
    rows = source.shape[1]
    half = LENGTH // 2

    def forward(t, _):
        both = jnp.concatenate([source[2 * t], source[2 * t + 1]], axis=0)
        turned = right_product(both, along_y[...])
        pair = jnp.concatenate([turned[:rows], turned[rows:]], axis=1)
        done = left_product(along_x[...], pair)
        mid[2 * t] = done[:, :LANES]
        mid[2 * t + 1] = done[:, LANES:]
        return 0

    lax.fori_loop(0, half, forward, 0, unroll=10)

    def across(g, _):
        start = pl.multiple_of(g * 16, 16)

        def plane(z):
            return jnp.concatenate(
                [mid[z, pl.ds(start, 8), :], mid[z, pl.ds(start + 8, 8), :]], axis=1
            )

        planes = [plane(z) for z in range(LENGTH)]
        sums = jnp.concatenate([planes[z] + planes[LENGTH - 1 - z] for z in range(half)], axis=0)
        gaps = jnp.concatenate([planes[z] - planes[LENGTH - 1 - z] for z in range(half)], axis=0)
        ground = jnp.concatenate(
            [base[pl.ds(start, 8), :], base[pl.ds(start + 8, 8), :]], axis=1
        )

        def divisors(first):
            return jnp.concatenate(
                [
                    ground + jnp.concatenate([steps[first + k], steps[first + k]], axis=1)
                    for k in range(half)
                ],
                axis=0,
            )

        near = left_product(back_even[...], left_product(even[...], sums) / divisors(0))
        far = left_product(back_odd[...], left_product(odd[...], gaps) / divisors(half))
        lower = near + far
        upper = near - far
        for z in range(half):
            for h in range(2):
                lanes = slice(h * LANES, (h + 1) * LANES)
                mid[z, pl.ds(start + 8 * h, 8), :] = lower[8 * z : 8 * z + 8, lanes]
                mid[LENGTH - 1 - z, pl.ds(start + 8 * h, 8), :] = upper[8 * z : 8 * z + 8, lanes]
        return 0

    lax.fori_loop(0, mid.shape[1] // 16, across, 0, unroll=5)

    def backward(t, _):
        pair = jnp.concatenate([mid[2 * t], mid[2 * t + 1]], axis=1)
        done = left_product(back_x[...], pair)
        both = jnp.concatenate([done[:, :LANES], done[:, LANES:]], axis=0)
        turned = right_product(both, back_y[...])
        target[2 * t] = turned[:rows]
        target[2 * t + 1] = turned[rows:]
        return 0

    lax.fori_loop(0, half, backward, 0, unroll=10)


def write_messages(pos_ref, solved, width, counts, outs_y, outs_z, outs_yz):
    rows = solved.shape[1]
    spot, _ = spots((rows, LANES))
    groups = WIDE // width
    _, count_y, count_z = counts
    for phase, out in enumerate(outs_z):
        up, _ = side(pos_ref, 0, phase, count_z)
        first = pick(up, LENGTH - width, 0)
        for i in range(width):
            out[i] = solved[first + i]
    for phase, out in enumerate(outs_y):
        up, _ = side(pos_ref, 1, phase, count_y)
        start = pick(up, WIDE - 1 - width, 1)
        many = LENGTH // groups

        def one(k, _, out=out, start=start, many=many):
            out[k] = pack(
                [solved[g * many + k] for g in range(groups)], width, start, spot, groups
            )
            return 0

        lax.fori_loop(0, many, one, 0, unroll=5)
    for number, out in enumerate(outs_yz):
        phase_y, phase_z = divmod(number, len(outs_z))
        up_y, _ = side(pos_ref, 1, phase_y, count_y)
        up_z, _ = side(pos_ref, 0, phase_z, count_z)
        start = pick(up_y, WIDE - 1 - width, 1)
        first = pick(up_z, LENGTH - width, 0)
        many = out.shape[0]
        for k in range(many):
            planes = [
                solved[first + g * many + k] for g in range(groups) if g * many + k < width
            ]
            out[k] = pack(planes, width, start, spot, groups)


def add_messages(pos_ref, solved, width, counts, ins_y, ins_z, ins_yz, field):
    rows = solved.shape[1]
    spot, _ = spots((rows, LANES))
    groups = WIDE // width
    _, count_y, count_z = counts
    first_y = [side(pos_ref, 1, phase, count_y) for phase in range(len(ins_y))]
    first_z = [side(pos_ref, 0, phase, count_z) for phase in range(len(ins_z))]
    many = LENGTH // groups

    def one(k, _):
        for g in range(groups):
            total = solved[g * many + k]
            for (up, use), ref in zip(first_y, ins_y):
                start = pick(up, WIDE - FOLD, FOLD - width)
                total = total + unpack(ref[k], g, width, start, spot, use)
            field[g * many + k + 1] = total
        return 0

    lax.fori_loop(0, many, one, 0, unroll=5)
    field[0] = jnp.zeros((rows, LANES), F32)
    field[WIDE - 1] = jnp.zeros((rows, LANES), F32)
    for phase_z, ((up_z, use_z), ref_z) in enumerate(zip(first_z, ins_z)):
        first = pick(up_z, WIDE - FOLD, FOLD - width)
        for i in range(width):
            total = ref_z[i]
            for phase_y, (up_y, use_y) in enumerate(first_y):
                ref = ins_yz[phase_y * len(ins_z) + phase_z]
                g, k = divmod(i, ref.shape[0])
                start = pick(up_y, WIDE - FOLD, FOLD - width)
                total = total + unpack(ref[k], g, width, start, spot, use_y)
            field[first + i] = field[first + i] + jnp.where(use_z, total, 0.0)


def grid_masks(pos_ref, rows, counts):
    count_x, count_y, count_z = counts
    spot, _ = spots((rows, LANES))
    row = lax.broadcasted_iota(jnp.int32, (rows, LANES), 0)
    low_y = pick(pos_ref[1] > 0, 0, REACH)
    high_y = pick(pos_ref[1] < count_y - 1, WIDE, REACH + BRICK)
    low_x = pick(pos_ref[2] > 0, 0, PAD)
    high_x = pick(pos_ref[2] < count_x - 1, rows, rows - PAD)
    inside = (spot >= low_y) & (spot < high_y) & (row >= low_x) & (row < high_x)
    low_z = pick(pos_ref[0] > 0, 0, REACH)
    high_z = pick(pos_ref[0] < count_z - 1, WIDE, REACH + BRICK)
    return inside, low_z, high_z


def complete(pos_ref, counts, partial, ins_x, field, first, last):
    rows = field.shape[1]
    inside, low_z, high_z = grid_masks(pos_ref, rows, counts)
    sides = [side(pos_ref, 2, phase, counts[0]) for phase in range(len(ins_x))]

    def one(z, _):
        on = inside & (z >= low_z) & (z < high_z)
        field[z] = partial[z]
        for (up, use), ref in zip(sides, ins_x):
            start = pl.multiple_of(pick(up, rows - 2 * PAD, 0), 2 * PAD)
            part = field[z, pl.ds(start, 2 * PAD), :]
            field[z, pl.ds(start, 2 * PAD), :] = part + jnp.where(use, ref[z], 0.0)
        field[z] = jnp.where(on, field[z], 0.0)
        return 0

    lax.fori_loop(first, last + 1, one, 0, unroll=2)


def stiffness(field, modulus, first, last, store):
    rows = field.shape[1]
    _, region = spots((rows, LANES))
    scale = [
        jnp.where(region == c, 0.5 * LAMBDA_RATIO, 0.5) for c in range(3)
    ]

    def rise(z):
        return (modulus[z] + modulus[z + 1]) * (field[z + 1] - field[z])

    def one(z, below):
        v = field[z]
        m = modulus[z]
        above = rise(z)
        gx = (m + pltpu.roll(m, rows - 1, 0)) * (pltpu.roll(v, rows - 1, 0) - v)
        gy = (m + pltpu.roll(m, LANES - 1, 1)) * (pltpu.roll(v, LANES - 1, 1) - v)
        total = SIGMA_SHIFT * m * v + scale[0] * (below - above)
        total = total + scale[1] * (pltpu.roll(gy, 1, 1) - gy)
        total = total + scale[2] * (pltpu.roll(gx, 1, 0) - gx)
        store(z, total)
        return above

    lax.fori_loop(first, last + 1, one, rise(first - 1), unroll=4)


def groups_of(refs, sizes):
    found = []
    at = 0
    for size in sizes:
        found.append(refs[at : at + size])
        at += size
    return found


def prepare_kernel(counts, sizes, pos_ref, table_ref, load, labels, mask, *refs):
    (load_out, modulus_out), outs_y, outs_z, outs_yz, (wide_load, wide_modulus) = groups_of(
        refs, (2,) + sizes[:3] + (2,)
    )
    columns = load.shape[3]
    wide_load[...] = jnp.zeros(wide_load.shape, F32)
    wide_modulus[...] = jnp.zeros(wide_modulus.shape, F32)

    def one(z, _):
        label = labels[z]
        looked = jnp.zeros(label.shape, F32)
        for k in range(table_ref.shape[0]):
            looked = jnp.where(label == k, table_ref[k], looked)
        value = jnp.where(mask[z] == 1, looked, VOID_MODULUS)
        for c in range(3):
            lane = c * WIDE + REACH
            wide_load[lane : lane + BRICK, :] = load[c, z]
            wide_modulus[lane : lane + BRICK, :] = value
        load_out[z] = wide_load[...].T
        modulus_out[z] = wide_modulus[...].T
        return 0

    lax.fori_loop(0, BRICK, one, 0, unroll=4)

    spot, region = spots((columns, LANES))
    _, count_y, count_z = counts
    groups = WIDE // REACH
    many = BRICK // groups
    for phase, out in enumerate(outs_z):
        up, _ = side(pos_ref, 0, phase, count_z)
        first = pick(up, BRICK - INTERSECTION, 0)
        for i in range(INTERSECTION):
            out[i] = load_out[first + i]
        first = pick(up, BRICK - REACH, 0)
        for k in range(2):
            total = modulus_out[first + k]
            for c in (1, 2):
                i = min(2 * c + k, REACH - 1)
                total = jnp.where(region == c, modulus_out[first + i], total)
            out[INTERSECTION + k] = total
    for phase, out in enumerate(outs_y):
        up, _ = side(pos_ref, 1, phase, count_y)
        start = pick(up, BRICK, REACH)
        for k in range(many):
            out[k] = pack(
                [load_out[g * many + k] for g in range(groups)], REACH, start, spot, groups
            )
        for k in range(2):
            total = jnp.zeros((columns, LANES), F32)
            for g in range(groups):
                turned = [
                    turn(modulus_out[(c * groups + g) * 2 + k], g * REACH - start)
                    for c in range(2)
                ]
                chosen = jnp.where(region == 0, turned[0], turned[1])
                inside = (spot >= g * REACH) & (spot < (g + 1) * REACH)
                total = jnp.where(inside, chosen, total)
            out[many + k] = total
    for number, out in enumerate(outs_yz):
        phase_y, phase_z = divmod(number, len(outs_z))
        up_y, _ = side(pos_ref, 1, phase_y, count_y)
        up_z, _ = side(pos_ref, 0, phase_z, count_z)
        start = pick(up_y, BRICK, REACH)
        first = pick(up_z, BRICK - INTERSECTION, 0)
        out[0] = pack(
            [load_out[first + i] for i in range(INTERSECTION)], REACH, start, spot, groups
        )
        first = pick(up_z, BRICK - REACH, 0)
        out[1] = pack([modulus_out[first + i] for i in range(REACH)], REACH, start, spot, groups)


def spread(values, region, source):
    total = jnp.zeros(values.shape, F32)
    for c in range(3):
        total = jnp.where(region == c, turn(values, (c - source) * WIDE), total)
    return total


def gather_kernel(counts, sizes, pos_ref, load, modulus, *refs):
    ins_y, ins_z, ins_yz, (load_out, modulus_out), outs_x = groups_of(
        refs, sizes[:3] + (2, sizes[3])
    )
    columns = load.shape[1]
    rows = columns + 2 * PAD
    core = slice(PAD, PAD + columns)
    spot, region = spots((columns, LANES))
    count_x, count_y, count_z = counts
    groups = WIDE // REACH
    many = BRICK // groups
    sides_y = [side(pos_ref, 1, phase, count_y) for phase in range(len(ins_y))]
    sides_z = [side(pos_ref, 0, phase, count_z) for phase in range(len(ins_z))]
    blank = jnp.zeros((PAD, LANES), F32)

    def store(out, z, value):
        out[z, :PAD, :] = blank
        out[z, core, :] = value
        out[z, rows - PAD :, :] = blank

    for z in range(BRICK):
        g, k = divmod(z, many)
        total = load[z]
        for (up, use), ref in zip(sides_y, ins_y):
            start = pick(up, REACH + BRICK, 0)
            total = total + unpack(ref[k], g, REACH, start, spot, use)
        store(load_out, z + INTERSECTION, total)
        c, rest = divmod(z, 2 * groups)
        g, k = divmod(rest, 2)
        total = modulus[z]
        for (up, use), ref in zip(sides_y, ins_y):
            start = pick(up, REACH + BRICK, 0)
            whole = spread(ref[many + k], region, c)
            total = total + unpack(whole, g, REACH, start, spot, use)
        store(modulus_out, z + REACH, total)
    zero = jnp.zeros((columns, LANES), F32)
    for i in range(INTERSECTION):
        store(load_out, i, zero)
        store(load_out, LENGTH - 1 - i, zero)
    for i in range(REACH):
        store(modulus_out, i, zero)
        store(modulus_out, WIDE - 1 - i, zero)
    for phase_z, ((up_z, use_z), ref_z) in enumerate(zip(sides_z, ins_z)):
        first = pick(up_z, INTERSECTION + BRICK, 0)
        for i in range(INTERSECTION):
            total = ref_z[i]
            for phase_y, (up_y, use_y) in enumerate(sides_y):
                ref = ins_yz[phase_y * len(ins_z) + phase_z]
                start = pick(up_y, REACH + BRICK, 0)
                total = total + unpack(ref[0], i, REACH, start, spot, use_y)
            load_out[first + i, core, :] = load_out[first + i, core, :] + jnp.where(
                use_z, total, 0.0
            )
        first = pick(up_z, REACH + BRICK, 0)
        for i in range(REACH):
            c, k = divmod(i, 2)
            total = spread(ref_z[INTERSECTION + k], region, c)
            for phase_y, (up_y, use_y) in enumerate(sides_y):
                ref = ins_yz[phase_y * len(ins_z) + phase_z]
                start = pick(up_y, REACH + BRICK, 0)
                total = total + unpack(ref[1], i, REACH, start, spot, use_y)
            modulus_out[first + i, core, :] = modulus_out[first + i, core, :] + jnp.where(
                use_z, total, 0.0
            )
    _, edge_region = spots((PAD, LANES))
    third = WIDE // 3
    for phase, out in enumerate(outs_x):
        up, _ = side(pos_ref, 2, phase, count_x)
        start = pl.multiple_of(pick(up, rows - 2 * PAD, PAD), PAD)
        for z in range(LENGTH):
            out[z] = load_out[z, pl.ds(start, PAD), :]
        for k in range(third):
            total = modulus_out[k, pl.ds(start, PAD), :]
            for c in (1, 2):
                part = modulus_out[k + c * third, pl.ds(start, PAD), :]
                total = jnp.where(edge_region == c, part, total)
            out[LENGTH + k] = total


def first_kernel(counts, sizes, pos_ref, load, modulus, *refs):
    ins_x, consts, (field_out, modulus_out, solved), outs_y, outs_z, outs_yz, (mid,) = groups_of(
        refs, (sizes[3], 10, 3) + sizes[:3] + (1,)
    )
    rows = load.shape[1]
    _, region = spots((PAD, LANES))
    sides = [side(pos_ref, 2, phase, counts[0]) for phase in range(len(ins_x))]
    third = WIDE // 3

    def copy(z, _):
        field_out[z] = load[z]
        modulus_out[z] = modulus[z]
        return 0

    lax.fori_loop(0, LENGTH, copy, 0, unroll=4)
    for z in range(LENGTH, WIDE):
        modulus_out[z] = modulus[z]
    for (up, use), ref in zip(sides, ins_x):
        start = pl.multiple_of(pick(up, rows - PAD, 0), PAD)
        for z in range(LENGTH):
            part = field_out[z, pl.ds(start, PAD), :]
            field_out[z, pl.ds(start, PAD), :] = part + jnp.where(use, ref[z], 0.0)
        for z in range(WIDE):
            c, k = divmod(z, third)
            part = modulus_out[z, pl.ds(start, PAD), :]
            modulus_out[z, pl.ds(start, PAD), :] = part + jnp.where(
                use, spread(ref[LENGTH + k], region, c), 0.0
            )
    solve(field_out, mid, solved, consts)
    write_messages(pos_ref, solved, FOLD, counts, outs_y, outs_z, outs_yz)


def fold_kernel(width, counts, sizes, pos_ref, solved, *refs):
    ins_y, ins_z, ins_yz, (field,), outs_x = groups_of(refs, sizes[:3] + (1, sizes[3]))
    rows = solved.shape[1]
    add_messages(pos_ref, solved, width, counts, ins_y, ins_z, ins_yz, field)
    for phase, out in enumerate(outs_x):
        up, _ = side(pos_ref, 2, phase, counts[0])
        start = pl.multiple_of(pick(up, rows - 2 * PAD, 0), 2 * PAD)
        for z in range(WIDE):
            out[z] = field[z, pl.ds(start, 2 * PAD), :]


def second_kernel(counts, sizes, pos_ref, partial, residual, modulus, *refs):
    (
        ins_x,
        consts,
        (solved, moved, left),
        outs_y,
        outs_z,
        outs_yz,
        (mid, field, renewed),
    ) = groups_of(refs, (sizes[3], 10, 3) + sizes[:3] + (3,))
    rows = partial.shape[1]
    complete(pos_ref, counts, partial, ins_x, field, 0, WIDE - 1)
    inside, low_z, high_z = grid_masks(pos_ref, rows, counts)

    def store(z, product):
        on = inside & (z >= low_z) & (z < high_z)
        renewed[z - 1] = jnp.where(on, residual[z - 1] - product, 0.0)

    stiffness(field, modulus, 1, WIDE - 2, store)

    def keep(z, _):
        moved[z] = field[z + REACH, PAD : rows - PAD, :]
        left[z] = renewed[z + INTERSECTION, PAD : rows - PAD, :]
        return 0

    lax.fori_loop(0, BRICK, keep, 0, unroll=4)
    solve(renewed, mid, solved, consts)
    write_messages(pos_ref, solved, REACH, counts, outs_y, outs_z, outs_yz)


def last_kernel(counts, sizes, pos_ref, partial, modulus, moved, left, *refs):
    ins_x, (displacement, residual), (field, turned_one, turned_two) = groups_of(
        refs, (sizes[3], 2, 3)
    )
    rows = partial.shape[1]
    complete(pos_ref, counts, partial, ins_x, field, INTERSECTION, REACH + BRICK)
    core = slice(PAD, rows - PAD)

    def store(z, product):
        at = z - REACH
        turned_one[...] = (moved[at] + field[z, core, :]).T
        turned_two[...] = (left[at] - product[core]).T
        for c in range(3):
            lane = c * WIDE + REACH
            displacement[c, at] = turned_one[lane : lane + BRICK, :]
            residual[c, at] = turned_two[lane : lane + BRICK, :]

    stiffness(field, modulus, REACH, REACH + BRICK - 1, store)


def call(kernel, inputs, outs, scratch=(), smem=1):
    return pl.pallas_call(
        kernel,
        out_shape=[jax.ShapeDtypeStruct(shape, F32) for shape in outs],
        in_specs=[SMEM] * smem + [VMEM] * (len(inputs) - smem),
        out_specs=[VMEM] * len(outs),
        scratch_shapes=[pltpu.VMEM(shape, F32) for shape in scratch],
        compiler_params=pltpu.CompilerParams(vmem_limit_bytes=48 * 1024 * 1024),
    )(*inputs)


def local(load, labels, mask, table):
    columns = load.shape[3]
    rows = columns + 2 * PAD
    counts = tuple(lax.axis_size(axis) for axis in ("gx", "gy", "gz"))
    ways = tuple(phases(count) for count in counts)
    sizes = (ways[1], ways[2], ways[1] * ways[2], ways[0])
    pos = jnp.stack([lax.axis_index(axis) for axis in ("gz", "gy", "gx")]).astype(jnp.int32)
    consts = [jnp.asarray(value) for value in tables(columns // BRICK)]
    spectral = (LENGTH, columns // BRICK * LENGTH, LANES)

    def exchange_yz(values):
        y, z, yz = groups_of(values, sizes[:3])
        z = [swap(value, "gz", phase) for phase, value in enumerate(z)]
        y = [swap(value, "gy", phase) for phase, value in enumerate(y)]
        yz = [
            swap_both(value, "gy", number // ways[2], "gz", number % ways[2])
            for number, value in enumerate(yz)
        ]
        return [*y, *z, *yz]

    def exchange_x(values):
        return [swap(value, "gx", phase) for phase, value in enumerate(values)]

    def message_shapes(width, height):
        groups = WIDE // width
        return (
            [(LENGTH // groups, height, LANES)] * sizes[0]
            + [(width, height, LANES)] * sizes[1]
            + [(-(-width // groups), height, LANES)] * sizes[2]
        )

    bind = lambda kernel, *first: functools.partial(kernel, *first, counts, sizes)
    core = (BRICK, columns, LANES)
    tall = (LENGTH, rows, LANES)
    wide = (WIDE, rows, LANES)
    many = BRICK // (WIDE // REACH)

    load_core, modulus_core, *out = call(
        bind(prepare_kernel),
        [pos, table, load, labels, mask],
        [core, core]
        + [(many + 2, columns, LANES)] * sizes[0]
        + [(INTERSECTION + 2, columns, LANES)] * sizes[1]
        + [(2, columns, LANES)] * sizes[2],
        [(LANES, columns)] * 2,
        smem=2,
    )
    residual, modulus, *out = call(
        bind(gather_kernel),
        [pos, load_core, modulus_core, *exchange_yz(out)],
        [tall, wide] + [(LENGTH + WIDE // 3, PAD, LANES)] * sizes[3],
    )
    residual, modulus, solved, *out = call(
        bind(first_kernel),
        [pos, residual, modulus, *exchange_x(out), *consts],
        [tall, wide, tall] + message_shapes(FOLD, rows),
        [spectral],
    )
    partial, *out = call(
        bind(fold_kernel, FOLD),
        [pos, solved, *exchange_yz(out)],
        [wide] + [(WIDE, 2 * PAD, LANES)] * sizes[3],
    )
    solved, moved, left, *out = call(
        bind(second_kernel),
        [pos, partial, residual, modulus, *exchange_x(out), *consts],
        [tall, core, core] + message_shapes(REACH, rows),
        [spectral, wide, tall],
    )
    partial, *out = call(
        bind(fold_kernel, REACH),
        [pos, solved, *exchange_yz(out)],
        [wide] + [(WIDE, 2 * PAD, LANES)] * sizes[3],
    )
    displacement, residual = call(
        bind(last_kernel),
        [pos, partial, modulus, moved, left, *exchange_x(out)],
        [load.shape, load.shape],
        [wide] + [(LANES, columns)] * 2,
    )
    return displacement, residual


def solution(mesh):
    placed = (P(None, "gz", "gy", "gx"), P("gz", "gy", "gx"), P("gz", "gy", "gx"), P())
    return jax.shard_map(
        local,
        mesh=mesh,
        in_specs=placed,
        out_specs=(P(None, "gz", "gy", "gx"), P(None, "gz", "gy", "gx")),
        check_vma=False,
    )
```

```python
import functools

import jax
import jax.numpy as jnp
import ml_dtypes
import numpy as np
from jax import lax
from jax.experimental import pallas as pl
from jax.experimental.pallas import tpu as pltpu
from jax.sharding import PartitionSpec as P

BRICK = 32
INTERSECTION = 4
LENGTH = BRICK + 2 * INTERSECTION
REACH = INTERSECTION + 1
WIDE = BRICK + 2 * REACH
LANES = 128
PAD = 8
FOLD = 2 * INTERSECTION + 1

LAMBDA_RATIO = 2.0
SIGMA_SHIFT = 0.1
REF_MODULUS = 1.5
VOID_MODULUS = 0.1

F32 = jnp.float32
BF16 = jnp.bfloat16
VMEM = pl.BlockSpec(memory_space=pltpu.VMEM)
SMEM = pl.BlockSpec(memory_space=pltpu.SMEM)


def halves(values):
    values = np.asarray(values, np.float32)
    high = values.astype(ml_dtypes.bfloat16)
    low = (values - high.astype(np.float32)).astype(ml_dtypes.bfloat16)
    return high, low


def right_table(values):
    high, low = halves(values)
    return np.block([[high, low], [high, np.zeros_like(low)]]).astype(ml_dtypes.bfloat16)


def left_table(values):
    high, low = halves(values)
    return np.concatenate([high, high, low], axis=1)


def tables(count_x):
    grid = np.arange(1, LENGTH + 1, dtype=np.float64)
    sine = np.sqrt(2.0 / (LENGTH + 1)) * np.sin(np.pi * np.outer(grid, grid) / (LENGTH + 1))
    eigen = 2.0 - 2.0 * np.cos(np.pi * grid / (LENGTH + 1))
    position = np.arange(LENGTH, dtype=np.float64)
    margin = 2 * INTERSECTION
    ramp = np.minimum(
        np.minimum((position + 0.5) / margin, (LENGTH - 0.5 - position) / margin), 1.0
    )
    rows = count_x * BRICK + 2 * PAD
    ramped = ramp[:, None] * sine
    along_y = np.zeros((LANES, LANES))
    back_y = np.zeros((LANES, LANES))
    for c in range(3):
        lane = c * WIDE + 1
        along_y[lane : lane + LENGTH, c * LENGTH : (c + 1) * LENGTH] = ramped
        back_y[c * LENGTH : (c + 1) * LENGTH, lane : lane + LENGTH] = sine
    along_x = np.zeros((count_x * LENGTH, rows))
    back_x = np.zeros((rows - 2 * INTERSECTION, count_x * LENGTH))
    for b in range(count_x):
        row = b * BRICK + PAD - INTERSECTION
        along_x[b * LENGTH : (b + 1) * LENGTH, row : row + LENGTH] = ramped.T
        back_x[b * BRICK : b * BRICK + LENGTH, b * LENGTH : (b + 1) * LENGTH] = sine
    half = LENGTH // 2
    eye = np.eye(8)
    even = left_table(np.kron(ramped[:half, 0::2].T, eye))
    odd = left_table(np.kron(ramped[:half, 1::2].T, eye))
    back_even = left_table(np.kron(sine[0::2, :half].T, eye))
    back_odd = left_table(np.kron(sine[1::2, :half].T, eye))
    ratio = lambda c, d: LAMBDA_RATIO if c == d else 1.0
    base = np.ones((count_x * LENGTH, LANES))
    steps = np.zeros((LENGTH, 8, LANES))
    order = np.concatenate([np.arange(0, LENGTH, 2), np.arange(1, LENGTH, 2)])
    for c in range(3):
        part = slice(c * LENGTH, (c + 1) * LENGTH)
        base[:, part] = REF_MODULUS * (
            ratio(c, 1) * eigen[None, :]
            + ratio(c, 2) * np.tile(eigen, count_x)[:, None]
            + SIGMA_SHIFT
        )
        steps[:, :, part] = REF_MODULUS * ratio(c, 0) * eigen[order][:, None, None]
    return [
        right_table(along_y),
        left_table(along_x),
        even,
        odd,
        back_even,
        back_odd,
        left_table(back_x),
        right_table(back_y),
        base.astype(np.float32),
        steps.astype(np.float32),
    ]


def phases(count):
    return 1 if count <= 2 else 2


def partners(count, phase):
    found = [i + 1 if (i + phase) % 2 == 0 else i - 1 for i in range(count)]
    return [j if 0 <= j < count else i for i, j in enumerate(found)]


def swap(value, axis, phase):
    target = partners(lax.axis_size(axis), phase)
    return lax.ppermute(value, axis, list(enumerate(target)))


def swap_both(value, first, phase_first, second, phase_second):
    rows = lax.axis_size(first)
    columns = lax.axis_size(second)
    one = partners(rows, phase_first)
    two = partners(columns, phase_second)
    pairs = []
    for i in range(rows):
        for j in range(columns):
            moved = one[i] != i and two[j] != j
            to = one[i] * columns + two[j] if moved else i * columns + j
            pairs.append((i * columns + j, to))
    return lax.ppermute(value, (first, second), pairs)


def spots(shape):
    lane = lax.broadcasted_iota(jnp.int32, shape, len(shape) - 1)
    region = jnp.where(lane >= 3 * WIDE, 3, jnp.where(lane >= 2 * WIDE, 2, jnp.where(lane >= WIDE, 1, 0)))
    spot = jnp.where(region == 3, 4 * LANES, lane - region * WIDE)
    return spot, region


def turn(values, shift):
    return pltpu.roll(values, lax.rem(shift + 2 * LANES, LANES), values.ndim - 1)


def pack(planes, width, start, spot, groups):
    total = jnp.zeros(spot.shape, F32)
    for g, plane in enumerate(planes):
        inside = (spot >= g * width) & (spot < (g + 1) * width)
        total = jnp.where(inside, turn(plane, g * width - start), total)
    return total


def unpack(packed, g, width, start, spot, use):
    inside = (spot >= start) & (spot < start + width) & use
    return jnp.where(inside, turn(packed, start - g * width), 0.0)


def side(pos_ref, dim, phase, count):
    place = pos_ref[dim]
    up = lax.rem(place + phase, 2) == 0
    use = jnp.where(up, place < count - 1, place > 0)
    return up, use


def pick(up, high, low):
    return jnp.where(up, high, low)


def two_terms(values):
    high = values.astype(BF16)
    low = (values - high.astype(F32)).astype(BF16)
    return high, low


def right_product(values, table):
    high, low = two_terms(values)
    product = jnp.dot(jnp.concatenate([high, low], axis=1), table, preferred_element_type=F32)
    return product[:, :LANES] + product[:, LANES:]


def left_product(table, values):
    high, low = two_terms(values)
    return jnp.dot(
        table, jnp.concatenate([high, low, high], axis=0), preferred_element_type=F32
    )


def along(columns):
    return columns + 2 * INTERSECTION


def solve(source, mid, target, consts):
    along_y, along_x, even, odd, back_even, back_odd, back_x, back_y, base, steps = consts
    rows = target.shape[1]
    half = LENGTH // 2

    def forward(t, _):
        both = jnp.concatenate([source(2 * t), source(2 * t + 1)], axis=0)
        turned = right_product(both, along_y[...])
        height = both.shape[0] // 2
        pair = jnp.concatenate([turned[:height], turned[height:]], axis=1)
        done = left_product(along_x[...], pair)
        mid[2 * t] = done[:, :LANES]
        mid[2 * t + 1] = done[:, LANES:]
        return 0

    lax.fori_loop(0, half, forward, 0, unroll=10)

    def across(g, _):
        start = pl.multiple_of(g * 16, 16)

        def plane(z):
            return jnp.concatenate(
                [mid[z, pl.ds(start, 8), :], mid[z, pl.ds(start + 8, 8), :]], axis=1
            )

        planes = [plane(z) for z in range(LENGTH)]
        sums = jnp.concatenate([planes[z] + planes[LENGTH - 1 - z] for z in range(half)], axis=0)
        gaps = jnp.concatenate([planes[z] - planes[LENGTH - 1 - z] for z in range(half)], axis=0)
        ground = jnp.concatenate(
            [base[pl.ds(start, 8), :], base[pl.ds(start + 8, 8), :]], axis=1
        )

        def divisors(first):
            return jnp.concatenate(
                [
                    ground + jnp.concatenate([steps[first + k], steps[first + k]], axis=1)
                    for k in range(half)
                ],
                axis=0,
            )

        near = left_product(back_even[...], left_product(even[...], sums) / divisors(0))
        far = left_product(back_odd[...], left_product(odd[...], gaps) / divisors(half))
        lower = near + far
        upper = near - far
        for z in range(half):
            for h in range(2):
                lanes = slice(h * LANES, (h + 1) * LANES)
                mid[z, pl.ds(start + 8 * h, 8), :] = lower[8 * z : 8 * z + 8, lanes]
                mid[LENGTH - 1 - z, pl.ds(start + 8 * h, 8), :] = upper[8 * z : 8 * z + 8, lanes]
        return 0

    lax.fori_loop(0, mid.shape[1] // 16, across, 0, unroll=5)

    def backward(t, _):
        pair = jnp.concatenate([mid[2 * t], mid[2 * t + 1]], axis=1)
        done = left_product(back_x[...], pair)
        both = jnp.concatenate([done[:, :LANES], done[:, LANES:]], axis=0)
        turned = right_product(both, back_y[...])
        target[2 * t] = turned[:rows]
        target[2 * t + 1] = turned[rows:]
        return 0

    lax.fori_loop(0, half, backward, 0, unroll=10)


def write_messages(pos_ref, solved, width, counts, outs_y, outs_z, outs_yz):
    rows = solved.shape[1]
    spot, _ = spots((rows, LANES))
    groups = WIDE // width
    _, count_y, count_z = counts
    for phase, out in enumerate(outs_z):
        up, _ = side(pos_ref, 0, phase, count_z)
        first = pick(up, LENGTH - width, 0)
        for i in range(width):
            out[i] = solved[first + i]
    for phase, out in enumerate(outs_y):
        up, _ = side(pos_ref, 1, phase, count_y)
        start = pick(up, WIDE - 1 - width, 1)
        many = LENGTH // groups

        def one(k, _, out=out, start=start, many=many):
            out[k] = pack(
                [solved[g * many + k] for g in range(groups)], width, start, spot, groups
            )
            return 0

        lax.fori_loop(0, many, one, 0, unroll=5)
    for number, out in enumerate(outs_yz):
        phase_y, phase_z = divmod(number, len(outs_z))
        up_y, _ = side(pos_ref, 1, phase_y, count_y)
        up_z, _ = side(pos_ref, 0, phase_z, count_z)
        start = pick(up_y, WIDE - 1 - width, 1)
        first = pick(up_z, LENGTH - width, 0)
        many = out.shape[0]
        for k in range(many):
            planes = [
                solved[first + g * many + k] for g in range(groups) if g * many + k < width
            ]
            out[k] = pack(planes, width, start, spot, groups)


def planes_of(width):
    return range(FOLD - width, WIDE - FOLD + width)


def add_messages(pos_ref, solved, width, counts, ins_y, ins_z, ins_yz, window, put, get):
    height = solved.shape[1] if window is None else window.size
    rows = slice(None) if window is None else window
    spot, _ = spots((height, LANES))
    groups = WIDE // width
    _, count_y, count_z = counts
    sides_y = [side(pos_ref, 1, phase, count_y) for phase in range(len(ins_y))]
    sides_z = [side(pos_ref, 0, phase, count_z) for phase in range(len(ins_z))]
    many = LENGTH // groups
    wanted = planes_of(width)
    for z in range(LENGTH):
        if z + 1 not in wanted:
            continue
        g, k = divmod(z, many)
        total = solved[z, rows, :]
        for (up, use), ref in zip(sides_y, ins_y):
            start = pick(up, WIDE - FOLD, FOLD - width)
            total = total + unpack(ref[k, rows, :], g, width, start, spot, use)
        put(z + 1 - wanted[0], total)
    for plane in (0, WIDE - 1):
        if plane in wanted:
            put(plane - wanted[0], jnp.zeros((height, LANES), F32))
    for phase_z, ((up_z, use_z), ref_z) in enumerate(zip(sides_z, ins_z)):
        first = pick(up_z, WIDE - FOLD - wanted[0], 0)
        for i in range(width):
            total = ref_z[i, rows, :]
            for phase_y, (up_y, use_y) in enumerate(sides_y):
                ref = ins_yz[phase_y * len(ins_z) + phase_z]
                g, k = divmod(i, ref.shape[0])
                start = pick(up_y, WIDE - FOLD, FOLD - width)
                total = total + unpack(ref[k, rows, :], g, width, start, spot, use_y)
            put(first + i, get(first + i) + jnp.where(use_z, total, 0.0))


def grid_masks(pos_ref, rows, counts):
    count_x, count_y, count_z = counts
    spot, _ = spots((rows, LANES))
    row = lax.broadcasted_iota(jnp.int32, (rows, LANES), 0)
    low_y = pick(pos_ref[1] > 0, 0, REACH)
    high_y = pick(pos_ref[1] < count_y - 1, WIDE, REACH + BRICK)
    low_x = pick(pos_ref[2] > 0, 0, PAD)
    high_x = pick(pos_ref[2] < count_x - 1, rows, rows - PAD)
    inside = (spot >= low_y) & (spot < high_y) & (row >= low_x) & (row < high_x)
    low_z = pick(pos_ref[0] > 0, 0, REACH)
    high_z = pick(pos_ref[0] < count_z - 1, WIDE, REACH + BRICK)
    return inside, low_z, high_z


def from_sides(sides, refs, index):
    low = high = None
    for (up, use), ref in zip(sides, refs):
        value = index(ref)
        one = jnp.where(use & jnp.logical_not(up), value, 0.0)
        two = jnp.where(use & up, value, 0.0)
        low = one if low is None else low + one
        high = two if high is None else high + two
    return low, high


def complete(pos_ref, counts, partial, ins_x, height, field, first):
    rows = field.shape[1]
    inside, low_z, high_z = grid_masks(pos_ref, rows, counts)
    sides = [side(pos_ref, 2, phase, counts[0]) for phase in range(len(ins_x))]
    row = lax.broadcasted_iota(jnp.int32, (16, LANES), 0)
    blank = jnp.zeros((8, LANES), F32)

    def one(z, _):
        low, high = from_sides(sides, ins_x, lambda ref: ref[z])
        if height == 16:
            low = jnp.where(row < 12, pltpu.roll(low, 12, 0), 0.0)
            high = jnp.where(row < 4, 0.0, pltpu.roll(high, 4, 0))
        else:
            low = pltpu.roll(jnp.concatenate([low, blank], axis=0), 4, 0)
            high = pltpu.roll(jnp.concatenate([high, blank], axis=0), 4, 0)
        on = inside & (z + first >= low_z) & (z + first < high_z)
        whole = jnp.concatenate(
            [
                partial[z, :16, :] + low,
                partial[z, 16 : rows - 16, :],
                partial[z, rows - 16 :, :] + high,
            ],
            axis=0,
        )
        field[z] = jnp.where(on, whole, 0.0)
        return 0

    lax.fori_loop(0, field.shape[0], one, 0, unroll=2)


def widened(pos_ref, counts, modulus, ins_x):
    rows = modulus.shape[1]
    sides = [side(pos_ref, 2, phase, counts[0]) for phase in range(len(ins_x))]
    _, region = spots((PAD, LANES))
    third = WIDE // 3

    def plane(z):
        c = z // third
        k = z - c * third
        row = pl.multiple_of(k % 2 * PAD, PAD)
        low, high = from_sides(sides, ins_x, lambda ref: ref[WIDE + k // 2, pl.ds(row, PAD), :])
        edges = []
        for value in (low, high):
            total = turn(value, (2 * WIDE - c * WIDE))
            for target in (0, 1):
                total = jnp.where(region == target, turn(value, (target - c) * WIDE), total)
            edges.append(total)
        return jnp.concatenate([edges[0], modulus[z, PAD : rows - PAD, :], edges[1]], axis=0)

    return plane


def stiffness(field, modulus, first, last, shift, store):
    rows = field.shape[1]
    _, region = spots((rows, LANES))
    scale = [
        jnp.where(region == c, 0.5 * LAMBDA_RATIO, 0.5) for c in range(3)
    ]

    def one(z, carry):
        below, m = carry
        v = field[z - shift]
        next_m = modulus(z + 1)
        above = (m + next_m) * (field[z + 1 - shift] - v)
        gx = (m + pltpu.roll(m, rows - 1, 0)) * (pltpu.roll(v, rows - 1, 0) - v)
        gy = (m + pltpu.roll(m, LANES - 1, 1)) * (pltpu.roll(v, LANES - 1, 1) - v)
        total = SIGMA_SHIFT * m * v + scale[0] * (below - above)
        total = total + scale[1] * (pltpu.roll(gy, 1, 1) - gy)
        total = total + scale[2] * (pltpu.roll(gx, 1, 0) - gx)
        store(z, total)
        return above, next_m

    m = modulus(first)
    below = (modulus(first - 1) + m) * (field[first - shift] - field[first - 1 - shift])
    lax.fori_loop(first, last + 1, one, (below, m), unroll=4)


def groups_of(refs, sizes):
    found = []
    at = 0
    for size in sizes:
        found.append(refs[at : at + size])
        at += size
    return found


def prepare_kernel(counts, sizes, pos_ref, table_ref, load, labels, mask, *refs):
    (modulus_out,), outs_y, outs_z, outs_yz = groups_of(refs, (1,) + sizes[:3])
    _, count_y, count_z = counts

    def one(z, _):
        label = labels[z]
        looked = jnp.zeros(label.shape, F32)
        for k in range(table_ref.shape[0]):
            looked = jnp.where(label == k, table_ref[k], looked)
        modulus_out[z] = jnp.where(mask[z] == 1, looked, VOID_MODULUS)
        return 0

    lax.fori_loop(0, BRICK, one, 0, unroll=4)
    thin = INTERSECTION
    pairs = BRICK // 2

    def ends(plane, up, count):
        return jnp.where(up, plane[BRICK - count :, :], plane[:count, :])

    for phase, out in enumerate(outs_z):
        up, _ = side(pos_ref, 0, phase, count_z)
        first = pick(up, BRICK - thin, 0)
        for c in range(3):
            for i in range(thin):
                out[c * thin + i] = load[c, first + i]
        first = pick(up, BRICK - REACH, 0)
        for i in range(REACH):
            out[3 * thin + i] = modulus_out[first + i]
    for phase, out in enumerate(outs_y):
        up, _ = side(pos_ref, 1, phase, count_y)
        for c in range(4):
            for z in range(BRICK):
                plane = load[c, z] if c < 3 else modulus_out[z]
                row = z % 2 * thin
                out[c * pairs + z // 2, row : row + thin, :] = ends(plane, up, thin)
        for z in range(BRICK):
            plane = modulus_out[z]
            fifth = jnp.where(
                up, plane[BRICK - REACH : BRICK - thin, :], plane[thin:REACH, :]
            )
            out[4 * pairs + z // 8, z % 8 : z % 8 + 1, :] = fifth
    for number, out in enumerate(outs_yz):
        phase_y, phase_z = divmod(number, len(outs_z))
        up_y, _ = side(pos_ref, 1, phase_y, count_y)
        up_z, _ = side(pos_ref, 0, phase_z, count_z)
        first = pick(up_z, BRICK - thin, 0)
        for c in range(3):
            for i in range(thin):
                row = i % 2 * thin
                out[c * 2 + i // 2, row : row + thin, :] = ends(load[c, first + i], up_y, thin)
        first = pick(up_z, BRICK - REACH, 0)
        for i in range(REACH):
            out[6 + i] = ends(modulus_out[first + i], up_y, 8)


def gather_kernel(counts, sizes, pos_ref, load, *refs):
    ins_y, ins_z, ins_yz, (load_out,), outs_x, (wide,) = groups_of(
        refs, sizes[:3] + (1, sizes[3], 1)
    )
    columns = load.shape[3]
    rows = columns + 2 * PAD
    count_x, count_y, count_z = counts
    thin = INTERSECTION
    pairs = BRICK // 2
    sides_y = [side(pos_ref, 1, phase, count_y) for phase in range(len(ins_y))]
    sides_z = [side(pos_ref, 0, phase, count_z) for phase in range(len(ins_z))]
    blank = jnp.zeros((PAD, LANES), F32)

    def place(slot, c, centre, low, high):
        lane = c * WIDE + REACH
        wide[slot, lane : lane + BRICK, :] = centre
        wide[slot, lane - thin : lane, :] = low
        wide[slot, lane + BRICK : lane + BRICK + thin, :] = high

    def finish(z):
        load_out[z, :PAD, :] = blank
        load_out[z, PAD : PAD + columns, :] = wide[z].T
        load_out[z, rows - PAD :, :] = blank

    def clear(z, _):
        wide[z] = jnp.zeros((LANES, columns), F32)
        return 0

    lax.fori_loop(0, LENGTH, clear, 0, unroll=4)

    def pair(t, _):
        for h in range(2):
            z = 2 * t + h
            for c in range(3):
                low, high = from_sides(
                    sides_y, ins_y, lambda ref: ref[c * pairs + t, h * thin : (h + 1) * thin, :]
                )
                place(z + thin, c, load[c, z], low, high)
        for h in range(2):
            finish(2 * t + h + thin)
        return 0

    lax.fori_loop(0, pairs, pair, 0, unroll=2)
    for i in range(thin):
        row = i % 2 * thin
        for c in range(3):
            centre = from_sides(sides_z, ins_z, lambda ref: ref[c * thin + i])
            corner = [[], []]
            for phase_y in range(len(ins_y)):
                refs_z = ins_yz[phase_y * len(ins_z) : (phase_y + 1) * len(ins_z)]
                found = from_sides(
                    sides_z, refs_z, lambda ref: ref[c * 2 + i // 2, row : row + thin, :]
                )
                corner[0].append(found[0])
                corner[1].append(found[1])
            for which, slot in ((0, i), (1, thin + BRICK + i)):
                low, high = from_sides(sides_y, corner[which], lambda value: value)
                place(slot, c, centre[which], low, high)
        finish(i)
        finish(thin + BRICK + i)
    for phase, out in enumerate(outs_x):
        up, _ = side(pos_ref, 2, phase, count_x)
        start = pl.multiple_of(pick(up, rows - 2 * PAD, PAD), PAD)
        for z in range(LENGTH):
            out[z] = load_out[z, pl.ds(start, PAD), :]


def modulus_kernel(counts, sizes, pos_ref, modulus, *refs):
    ins_y, ins_z, ins_yz, (modulus_out,), (wide,) = groups_of(refs, sizes[:3] + (1, 1))
    columns = modulus.shape[2]
    rows = columns + 2 * PAD
    count_x, count_y, count_z = counts
    thin = INTERSECTION
    pairs = BRICK // 2
    sides_y = [side(pos_ref, 1, phase, count_y) for phase in range(len(ins_y))]
    sides_z = [side(pos_ref, 0, phase, count_z) for phase in range(len(ins_z))]
    blank = jnp.zeros((PAD, LANES), F32)

    def finish(z, centre, low, high, low_end, high_end):
        for c in range(3):
            lane = c * WIDE + REACH
            wide[z, lane : lane + BRICK, :] = centre
            wide[z, lane - thin : lane, :] = low
            wide[z, lane + BRICK : lane + BRICK + thin, :] = high
            wide[z, lane - REACH : lane - thin, :] = low_end
            wide[z, lane + BRICK + thin : lane + BRICK + REACH, :] = high_end
        wide[z, 3 * WIDE :, :] = jnp.zeros((LANES - 3 * WIDE, columns), F32)
        modulus_out[z, :PAD, :] = blank
        modulus_out[z, PAD : PAD + columns, :] = wide[z].T
        modulus_out[z, rows - PAD :, :] = blank

    for z in range(BRICK):
        row = z % 2 * thin
        low, high = from_sides(
            sides_y, ins_y, lambda ref: ref[3 * pairs + z // 2, row : row + thin, :]
        )
        low_end, high_end = from_sides(
            sides_y, ins_y, lambda ref: ref[4 * pairs + z // 8, z % 8 : z % 8 + 1, :]
        )
        finish(z + REACH, modulus[z], low, high, low_end, high_end)
    for i in range(REACH):
        centre = from_sides(sides_z, ins_z, lambda ref: ref[3 * thin + i])
        corner = [[], []]
        for phase_y in range(len(ins_y)):
            refs_z = ins_yz[phase_y * len(ins_z) : (phase_y + 1) * len(ins_z)]
            found = from_sides(sides_z, refs_z, lambda ref: ref[6 + i])
            corner[0].append(found[0])
            corner[1].append(found[1])
        for which, slot in ((0, i), (1, REACH + BRICK + i)):
            low, high = from_sides(sides_y, corner[which], lambda value: value)
            finish(
                slot,
                centre[which],
                low[8 - thin :, :],
                high[:thin, :],
                low[8 - REACH : 8 - thin, :],
                high[thin:REACH, :],
            )


def patched(pos_ref, counts, residual, ins_x):
    rows = residual.shape[1]
    sides = [side(pos_ref, 2, phase, counts[0]) for phase in range(len(ins_x))]

    def plane(z):
        low, high = from_sides(sides, ins_x, lambda ref: ref[z])
        return jnp.concatenate([low, residual[z, PAD : rows - PAD, :], high], axis=0)

    return plane


def first_kernel(counts, sizes, pos_ref, residual, *refs):
    ins_x, consts, (solved,), outs_y, outs_z, outs_yz, (mid,) = groups_of(
        refs, (sizes[3], 10, 1) + sizes[:3] + (1,)
    )
    solve(patched(pos_ref, counts, residual, ins_x), mid, solved, consts)
    write_messages(pos_ref, solved, FOLD, counts, outs_y, outs_z, outs_yz)


def edge_kernel(width, height, counts, sizes, pos_ref, solved, *refs):
    extra = 1 if width == FOLD else 0
    ins_y, ins_z, ins_yz, modulus, outs_x = groups_of(refs, sizes[:3] + (extra, sizes[3]))
    rows = solved.shape[1]
    _, region = spots((PAD, LANES))
    third = WIDE // 3
    for phase, out in enumerate(outs_x):
        up, _ = side(pos_ref, 2, phase, counts[0])
        window = pl.ds(pl.multiple_of(pick(up, rows - height, 0), 8), height)

        def put(plane, value, out=out):
            out[plane] = value

        def get(plane, out=out):
            return out[plane]

        add_messages(pos_ref, solved, width, counts, ins_y, ins_z, ins_yz, window, put, get)
        for ref in modulus:
            place = pl.ds(pl.multiple_of(pick(up, ref.shape[1] - 2 * PAD, PAD), PAD), PAD)
            for k in range(third):
                total = ref[k, place, :]
                for c in (1, 2):
                    total = jnp.where(region == c, ref[k + c * third, place, :], total)
                row = k % 2 * PAD
                out[WIDE + k // 2, row : row + PAD, :] = total


def fold_kernel(width, counts, sizes, pos_ref, solved, *refs):
    ins_y, ins_z, ins_yz, (field,) = groups_of(refs, sizes[:3] + (1,))
    rows = solved.shape[1]
    thin = INTERSECTION
    core = slice(thin, thin + rows)
    blank = jnp.zeros((thin, LANES), F32)

    def put(plane, value):
        field[plane, core, :] = value

    def get(plane):
        return field[plane, core, :]

    for z in range(field.shape[0]):
        field[z, :thin, :] = blank
        field[z, thin + rows :, :] = blank
    add_messages(pos_ref, solved, width, counts, ins_y, ins_z, ins_yz, None, put, get)


def second_kernel(counts, sizes, pos_ref, partial, residual, modulus, *refs):
    (
        ins_load,
        ins_x,
        consts,
        (solved, field, renewed),
        outs_y,
        outs_z,
        outs_yz,
        (mid,),
    ) = groups_of(refs, (sizes[3], sizes[3], 10, 3) + sizes[:3] + (1,))
    rows = partial.shape[1]
    complete(pos_ref, counts, partial, ins_x, 16, field, 0)
    inside, low_z, high_z = grid_masks(pos_ref, rows, counts)
    before = patched(pos_ref, counts, residual, ins_load)

    def store(z, product):
        on = inside & (z >= low_z) & (z < high_z)
        renewed[z - 1] = jnp.where(on, before(z - 1) - product, 0.0)

    stiffness(field, widened(pos_ref, counts, modulus, ins_x), 1, WIDE - 2, 0, store)
    solve(lambda z: renewed[z], mid, solved, consts)
    write_messages(pos_ref, solved, REACH, counts, outs_y, outs_z, outs_yz)


def last_kernel(counts, sizes, pos_ref, partial, modulus, moved, left, *refs):
    ins_x, ins_modulus, (displacement, residual), (field,) = groups_of(
        refs, (sizes[3], sizes[3], 2, 1)
    )
    rows = partial.shape[1]
    first = planes_of(REACH)[0]
    complete(pos_ref, counts, partial, ins_x, 8, field, first)
    core = slice(PAD, rows - PAD)

    def store(z, product):
        at = z - REACH
        one = (moved[z, core, :] + field[z - first, core, :]).T
        two = (left[z - 1, core, :] - product[core]).T
        for c in range(3):
            lane = c * WIDE + REACH
            displacement[c, at] = one[lane : lane + BRICK, :]
            residual[c, at] = two[lane : lane + BRICK, :]

    stiffness(
        field,
        widened(pos_ref, counts, modulus, ins_modulus),
        REACH,
        REACH + BRICK - 1,
        first,
        store,
    )


def call(kernel, inputs, outs, scratch=(), smem=1, limit=24, work=0):
    return pl.pallas_call(
        kernel,
        out_shape=[jax.ShapeDtypeStruct(shape, F32) for shape in outs],
        in_specs=[SMEM] * smem + [VMEM] * (len(inputs) - smem),
        out_specs=[VMEM] * len(outs),
        scratch_shapes=[pltpu.VMEM(shape, F32) for shape in scratch],
        compiler_params=pltpu.CompilerParams(vmem_limit_bytes=limit * 1024 * 1024),
        cost_estimate=pl.CostEstimate(flops=work, bytes_accessed=work, transcendentals=0),
    )(*inputs)


def local(load, labels, mask, table):
    columns = load.shape[3]
    rows = columns + 2 * PAD
    counts = tuple(lax.axis_size(axis) for axis in ("gx", "gy", "gz"))
    ways = tuple(phases(count) for count in counts)
    sizes = (ways[1], ways[2], ways[1] * ways[2], ways[0])
    pos = jnp.stack([lax.axis_index(axis) for axis in ("gz", "gy", "gx")]).astype(jnp.int32)
    consts = [jnp.asarray(value) for value in tables(columns // BRICK)]
    spectral = (LENGTH, columns // BRICK * LENGTH, LANES)

    def exchange_yz(values):
        y, z, yz = groups_of(values, sizes[:3])
        z = [swap(value, "gz", phase) for phase, value in enumerate(z)]
        y = [swap(value, "gy", phase) for phase, value in enumerate(y)]
        yz = [
            swap_both(value, "gy", number // ways[2], "gz", number % ways[2])
            for number, value in enumerate(yz)
        ]
        return [*y, *z, *yz]

    def exchange_x(values):
        return [swap(value, "gx", phase) for phase, value in enumerate(values)]

    def message_shapes(width, height):
        groups = WIDE // width
        return (
            [(LENGTH // groups, height, LANES)] * sizes[0]
            + [(width, height, LANES)] * sizes[1]
            + [(-(-width // groups), height, LANES)] * sizes[2]
        )

    bind = lambda kernel, *first: functools.partial(kernel, *first, counts, sizes)
    thick = along(columns)
    thin = (LENGTH, thick, LANES)
    tall = (LENGTH, rows, LANES)
    wide = (WIDE, rows, LANES)
    near = len(planes_of(REACH))

    modulus_core, *out = call(
        bind(prepare_kernel),
        [pos, table, load, labels, mask],
        [(BRICK, BRICK, columns)]
        + [(2 * BRICK + BRICK // 8, 8, columns)] * sizes[0]
        + [(3 * INTERSECTION + REACH, BRICK, columns)] * sizes[1]
        + [(6 + REACH, 8, columns)] * sizes[2],
        smem=2,
    )
    margins = exchange_yz(out)
    residual, *out = call(
        bind(gather_kernel),
        [pos, load, *margins],
        [tall] + [(LENGTH, PAD, LANES)] * sizes[3],
        [(LENGTH, LANES, columns)],
    )
    from_x = exchange_x(out)
    (modulus,) = call(
        bind(modulus_kernel),
        [pos, modulus_core, *margins],
        [wide],
        [(WIDE, LANES, columns)],
        work=8000000,
    )
    solved, *out = call(
        bind(first_kernel),
        [pos, residual, *from_x, *consts],
        [thin] + message_shapes(FOLD, thick),
        [spectral],
    )
    margins = exchange_yz(out)
    first_edges = exchange_x(
        call(
            bind(edge_kernel, FOLD, 16),
            [pos, solved, *margins, modulus],
            [(WIDE + WIDE // 6, 16, LANES)] * sizes[3],
        )
    )
    (partial,) = call(
        bind(fold_kernel, FOLD), [pos, solved, *margins], [wide], work=8000000
    )
    solved, moved, left, *out = call(
        bind(second_kernel),
        [pos, partial, residual, modulus, *from_x, *first_edges, *consts],
        [thin, wide, tall] + message_shapes(REACH, thick),
        [spectral],
        limit=32,
    )
    margins = exchange_yz(out)
    edges = exchange_x(
        call(
            bind(edge_kernel, REACH, 8), [pos, solved, *margins], [(near, 8, LANES)] * sizes[3]
        )
    )
    (partial,) = call(
        bind(fold_kernel, REACH), [pos, solved, *margins], [(near, rows, LANES)], work=8000000
    )
    displacement, residual = call(
        bind(last_kernel),
        [pos, partial, modulus, moved, left, *edges, *first_edges],
        [load.shape, load.shape],
        [(near, rows, LANES)],
        limit=32,
    )
    return displacement, residual


def solution(mesh):
    placed = (P(None, "gz", "gy", "gx"), P("gz", "gy", "gx"), P("gz", "gy", "gx"), P())
    return jax.shard_map(
        local,
        mesh=mesh,
        in_specs=placed,
        out_specs=(P(None, "gz", "gy", "gx"), P(None, "gz", "gy", "gx")),
        check_vma=False,
    )
```

```python
import functools

import jax
import jax.numpy as jnp
import ml_dtypes
import numpy as np
from jax import lax
from jax.experimental import pallas as pl
from jax.experimental.pallas import tpu as pltpu
from jax.sharding import PartitionSpec as P

BRICK = 32
INTERSECTION = 4
LENGTH = BRICK + 2 * INTERSECTION
REACH = INTERSECTION + 1
WIDE = BRICK + 2 * REACH
LANES = 128
PAD = 8
FOLD = 2 * INTERSECTION + 1

LAMBDA_RATIO = 2.0
SIGMA_SHIFT = 0.1
REF_MODULUS = 1.5
VOID_MODULUS = 0.1

F32 = jnp.float32
BF16 = jnp.bfloat16
VMEM = pl.BlockSpec(memory_space=pltpu.VMEM)
SMEM = pl.BlockSpec(memory_space=pltpu.SMEM)
HBM = pl.BlockSpec(memory_space=pltpu.HBM)


def halves(values):
    values = np.asarray(values, np.float32)
    high = values.astype(ml_dtypes.bfloat16)
    low = (values - high.astype(np.float32)).astype(ml_dtypes.bfloat16)
    return high, low


def right_table(values):
    high, low = halves(values)
    return np.block([[high, low], [high, np.zeros_like(low)]]).astype(ml_dtypes.bfloat16)


def left_table(values):
    high, low = halves(values)
    return np.concatenate([high, high, low], axis=1)


def tables(count_x):
    grid = np.arange(1, LENGTH + 1, dtype=np.float64)
    sine = np.sqrt(2.0 / (LENGTH + 1)) * np.sin(np.pi * np.outer(grid, grid) / (LENGTH + 1))
    eigen = 2.0 - 2.0 * np.cos(np.pi * grid / (LENGTH + 1))
    position = np.arange(LENGTH, dtype=np.float64)
    margin = 2 * INTERSECTION
    ramp = np.minimum(
        np.minimum((position + 0.5) / margin, (LENGTH - 0.5 - position) / margin), 1.0
    )
    rows = count_x * BRICK + 2 * PAD
    ramped = ramp[:, None] * sine
    along_y = np.zeros((LANES, LANES))
    back_y = np.zeros((LANES, LANES))
    for c in range(3):
        lane = c * WIDE + 1
        along_y[lane : lane + LENGTH, c * LENGTH : (c + 1) * LENGTH] = ramped
        back_y[c * LENGTH : (c + 1) * LENGTH, lane : lane + LENGTH] = sine
    along_x = np.zeros((count_x * LENGTH, rows))
    back_x = np.zeros((rows - 2 * INTERSECTION, count_x * LENGTH))
    for b in range(count_x):
        row = b * BRICK + PAD - INTERSECTION
        along_x[b * LENGTH : (b + 1) * LENGTH, row : row + LENGTH] = ramped.T
        back_x[b * BRICK : b * BRICK + LENGTH, b * LENGTH : (b + 1) * LENGTH] = sine
    half = LENGTH // 2
    eye = np.eye(8)
    even = left_table(np.kron(ramped[:half, 0::2].T, eye))
    odd = left_table(np.kron(ramped[:half, 1::2].T, eye))
    back_even = left_table(np.kron(sine[0::2, :half].T, eye))
    back_odd = left_table(np.kron(sine[1::2, :half].T, eye))
    ratio = lambda c, d: LAMBDA_RATIO if c == d else 1.0
    base = np.ones((count_x * LENGTH, LANES))
    steps = np.zeros((LENGTH, 8, LANES))
    order = np.concatenate([np.arange(0, LENGTH, 2), np.arange(1, LENGTH, 2)])
    for c in range(3):
        part = slice(c * LENGTH, (c + 1) * LENGTH)
        base[:, part] = REF_MODULUS * (
            ratio(c, 1) * eigen[None, :]
            + ratio(c, 2) * np.tile(eigen, count_x)[:, None]
            + SIGMA_SHIFT
        )
        steps[:, :, part] = REF_MODULUS * ratio(c, 0) * eigen[order][:, None, None]
    return [
        right_table(along_y),
        left_table(along_x),
        even,
        odd,
        back_even,
        back_odd,
        left_table(back_x),
        right_table(back_y),
        base.astype(np.float32),
        steps.astype(np.float32),
    ]


def phases(count):
    return 1 if count <= 2 else 2


def partners(count, phase):
    found = [i + 1 if (i + phase) % 2 == 0 else i - 1 for i in range(count)]
    return [j if 0 <= j < count else i for i, j in enumerate(found)]


def swap(value, mesh, moves, filler):
    names = mesh.axis_names
    shape = [mesh.shape[name] for name in names]
    found = {name: partners(mesh.shape[name], phase) for name, phase in moves.items()}
    spare = None if filler is None else partners(mesh.shape[filler], 0)
    pairs = []
    for place in np.ndindex(*shape):
        target = list(place)
        for name, other in found.items():
            target[names.index(name)] = other[place[names.index(name)]]
        if any(target[names.index(name)] == place[names.index(name)] for name in found):
            target = list(place)
            if filler is not None:
                target[names.index(filler)] = spare[place[names.index(filler)]]
        pairs.append(tuple(int(np.ravel_multi_index(at, shape)) for at in (place, target)))
    if filler is None and len(found) == 1:
        ((name, other),) = found.items()
        return lax.ppermute(value, name, list(enumerate(other)))
    return lax.ppermute(value, names, pairs)


def spots(shape):
    lane = lax.broadcasted_iota(jnp.int32, shape, len(shape) - 1)
    region = jnp.where(lane >= 3 * WIDE, 3, jnp.where(lane >= 2 * WIDE, 2, jnp.where(lane >= WIDE, 1, 0)))
    spot = jnp.where(region == 3, 4 * LANES, lane - region * WIDE)
    return spot, region


def turn(values, shift):
    return pltpu.roll(values, lax.rem(shift + 2 * LANES, LANES), values.ndim - 1)


def pack(planes, width, start, spot, groups):
    total = jnp.zeros(spot.shape, F32)
    for g, plane in enumerate(planes):
        inside = (spot >= g * width) & (spot < (g + 1) * width)
        total = jnp.where(inside, turn(plane, g * width - start), total)
    return total


def unpack(packed, g, width, start, spot, use):
    inside = (spot >= start) & (spot < start + width) & use
    return jnp.where(inside, turn(packed, start - g * width), 0.0)


def side(pos_ref, dim, phase, count):
    place = pos_ref[dim]
    up = lax.rem(place + phase, 2) == 0
    use = jnp.where(up, place < count - 1, place > 0)
    return up, use


def pick(up, high, low):
    return jnp.where(up, high, low)


def two_terms(values):
    high = values.astype(BF16)
    low = (values - high.astype(F32)).astype(BF16)
    return high, low


def right_product(values, table):
    high, low = two_terms(values)
    product = jnp.dot(jnp.concatenate([high, low], axis=1), table, preferred_element_type=F32)
    return product[:, :LANES] + product[:, LANES:]


def left_product(table, values):
    high, low = two_terms(values)
    return jnp.dot(
        table, jnp.concatenate([high, low, high], axis=0), preferred_element_type=F32
    )


def along(columns):
    return columns + 2 * INTERSECTION


def solve(source, mid, target, consts):
    along_y, along_x, even, odd, back_even, back_odd, back_x, back_y, base, steps = consts
    rows = target.shape[1]
    half = LENGTH // 2

    def forward(t, _):
        both = jnp.concatenate([source(2 * t), source(2 * t + 1)], axis=0)
        turned = right_product(both, along_y[...])
        height = both.shape[0] // 2
        pair = jnp.concatenate([turned[:height], turned[height:]], axis=1)
        done = left_product(along_x[...], pair)
        mid[2 * t] = done[:, :LANES]
        mid[2 * t + 1] = done[:, LANES:]
        return 0

    lax.fori_loop(0, half, forward, 0, unroll=10)

    def across(g, _):
        start = pl.multiple_of(g * 16, 16)

        def plane(z):
            return jnp.concatenate(
                [mid[z, pl.ds(start, 8), :], mid[z, pl.ds(start + 8, 8), :]], axis=1
            )

        planes = [plane(z) for z in range(LENGTH)]
        sums = jnp.concatenate([planes[z] + planes[LENGTH - 1 - z] for z in range(half)], axis=0)
        gaps = jnp.concatenate([planes[z] - planes[LENGTH - 1 - z] for z in range(half)], axis=0)
        ground = jnp.concatenate(
            [base[pl.ds(start, 8), :], base[pl.ds(start + 8, 8), :]], axis=1
        )

        def divisors(first):
            return jnp.concatenate(
                [
                    ground + jnp.concatenate([steps[first + k], steps[first + k]], axis=1)
                    for k in range(half)
                ],
                axis=0,
            )

        near = left_product(back_even[...], left_product(even[...], sums) / divisors(0))
        far = left_product(back_odd[...], left_product(odd[...], gaps) / divisors(half))
        lower = near + far
        upper = near - far
        for z in range(half):
            for h in range(2):
                lanes = slice(h * LANES, (h + 1) * LANES)
                mid[z, pl.ds(start + 8 * h, 8), :] = lower[8 * z : 8 * z + 8, lanes]
                mid[LENGTH - 1 - z, pl.ds(start + 8 * h, 8), :] = upper[8 * z : 8 * z + 8, lanes]
        return 0

    lax.fori_loop(0, mid.shape[1] // 16, across, 0, unroll=5)

    def backward(t, _):
        pair = jnp.concatenate([mid[2 * t], mid[2 * t + 1]], axis=1)
        done = left_product(back_x[...], pair)
        both = jnp.concatenate([done[:, :LANES], done[:, LANES:]], axis=0)
        turned = right_product(both, back_y[...])
        target[2 * t] = turned[:rows]
        target[2 * t + 1] = turned[rows:]
        return 0

    lax.fori_loop(0, half, backward, 0, unroll=10)


def write_messages(pos_ref, solved, width, counts, outs_y, outs_z, outs_yz):
    rows = solved.shape[1]
    spot, _ = spots((rows, LANES))
    lane = lax.broadcasted_iota(jnp.int32, (rows, LANES), 1)
    groups = WIDE // width
    _, count_y, count_z = counts
    for phase, out in enumerate(outs_z):
        up, _ = side(pos_ref, 0, phase, count_z)
        first = pick(up, LENGTH - width, 0)
        for i in range(width):
            out[i] = solved[first + i]
    for phase, out in enumerate(outs_y):
        up, _ = side(pos_ref, 1, phase, count_y)
        start = pick(up, WIDE - 1 - width, 1)
        many = LENGTH // groups

        def one(k, _, out=out, start=start, many=many):
            out[k] = pack(
                [solved[g * many + k] for g in range(groups)], width, start, spot, groups
            )
            return 0

        lax.fori_loop(0, many, one, 0, unroll=5)
    for number, out in enumerate(outs_yz):
        phase_y, phase_z = divmod(number, len(outs_z))
        up_y, _ = side(pos_ref, 1, phase_y, count_y)
        up_z, _ = side(pos_ref, 0, phase_z, count_z)
        start = pick(up_y, WIDE - 1 - width, 1)
        first = pick(up_z, LENGTH - width, 0)
        slots = LANES // width
        for k in range(out.shape[0]):
            total = jnp.zeros((rows, LANES), F32)
            for j in range(slots):
                i, c = divmod(k * slots + j, 3)
                if i < width:
                    inside = (lane >= j * width) & (lane < (j + 1) * width)
                    moved = turn(solved[first + i], j * width - c * WIDE - start)
                    total = jnp.where(inside, moved, total)
            out[k] = total


def planes_of(width):
    return range(FOLD - width, WIDE - FOLD + width)


def add_messages(pos_ref, solved, width, counts, ins_y, ins_z, ins_yz, window, put, get):
    height = solved.shape[1] if window is None else window.size
    rows = slice(None) if window is None else window
    spot, region = spots((height, LANES))
    groups = WIDE // width
    _, count_y, count_z = counts
    sides_y = [side(pos_ref, 1, phase, count_y) for phase in range(len(ins_y))]
    sides_z = [side(pos_ref, 0, phase, count_z) for phase in range(len(ins_z))]
    many = LENGTH // groups
    wanted = planes_of(width)
    for z in range(LENGTH):
        if z + 1 not in wanted:
            continue
        g, k = divmod(z, many)
        total = solved[z, rows, :]
        for (up, use), ref in zip(sides_y, ins_y):
            start = pick(up, WIDE - FOLD, FOLD - width)
            total = total + unpack(ref[k, rows, :], g, width, start, spot, use)
        put(z + 1 - wanted[0], total)
    for plane in (0, WIDE - 1):
        if plane in wanted:
            put(plane - wanted[0], jnp.zeros((height, LANES), F32))
    for phase_z, ((up_z, use_z), ref_z) in enumerate(zip(sides_z, ins_z)):
        first = pick(up_z, WIDE - FOLD - wanted[0], 0)
        for i in range(width):
            total = ref_z[i, rows, :]
            for phase_y, (up_y, use_y) in enumerate(sides_y):
                ref = ins_yz[phase_y * len(ins_z) + phase_z]
                start = pick(up_y, WIDE - FOLD, FOLD - width)
                part = jnp.zeros((height, LANES), F32)
                for c in range(3):
                    k, j = divmod(3 * i + c, LANES // width)
                    moved = turn(ref[k, rows, :], start + c * WIDE - j * width)
                    part = jnp.where(region == c, moved, part)
                inside = (spot >= start) & (spot < start + width) & use_y
                total = total + jnp.where(inside, part, 0.0)
            put(first + i, get(first + i) + jnp.where(use_z, total, 0.0))


def grid_masks(pos_ref, rows, counts):
    count_x, count_y, count_z = counts
    spot, _ = spots((rows, LANES))
    row = lax.broadcasted_iota(jnp.int32, (rows, LANES), 0)
    low_y = pick(pos_ref[1] > 0, 0, REACH)
    high_y = pick(pos_ref[1] < count_y - 1, WIDE, REACH + BRICK)
    low_x = pick(pos_ref[2] > 0, 0, PAD)
    high_x = pick(pos_ref[2] < count_x - 1, rows, rows - PAD)
    inside = (spot >= low_y) & (spot < high_y) & (row >= low_x) & (row < high_x)
    low_z = pick(pos_ref[0] > 0, 0, REACH)
    high_z = pick(pos_ref[0] < count_z - 1, WIDE, REACH + BRICK)
    return inside, low_z, high_z


def from_sides(sides, refs, index):
    low = high = None
    for (up, use), ref in zip(sides, refs):
        value = index(ref)
        one = jnp.where(use & jnp.logical_not(up), value, 0.0)
        two = jnp.where(use & up, value, 0.0)
        low = one if low is None else low + one
        high = two if high is None else high + two
    return low, high


def complete(pos_ref, counts, partial, ins_x, ninth, field, first):
    rows = field.shape[1]
    inside, low_z, high_z = grid_masks(pos_ref, rows, counts)
    sides = [side(pos_ref, 2, phase, counts[0]) for phase in range(len(ins_x))]
    row = lax.broadcasted_iota(jnp.int32, (16, LANES), 0)
    blank = jnp.zeros((8, LANES), F32)

    def one(z, _):
        low, high = from_sides(sides, ins_x, lambda ref: ref[z])
        low = pltpu.roll(jnp.concatenate([low, blank], axis=0), 4, 0)
        high = pltpu.roll(jnp.concatenate([high, blank], axis=0), 4, 0)
        if ninth:
            at = z % 8
            under, over = from_sides(
                sides, ins_x, lambda ref: ref[NINTH + z // 8, at : at + 1, :]
            )
            low = jnp.where(row == 3, under, low)
            high = jnp.where(row == 12, over, high)
        on = inside & (z + first >= low_z) & (z + first < high_z)
        whole = jnp.concatenate(
            [
                partial[z, :16, :] + low,
                partial[z, 16 : rows - 16, :],
                partial[z, rows - 16 :, :] + high,
            ],
            axis=0,
        )
        field[z] = jnp.where(on, whole, 0.0)
        return 0

    if ninth:
        for z in range(field.shape[0]):
            one(z, 0)
    else:
        lax.fori_loop(0, field.shape[0], one, 0, unroll=2)


def widened(pos_ref, counts, modulus, ins_x):
    rows = modulus.shape[1]
    sides = [side(pos_ref, 2, phase, counts[0]) for phase in range(len(ins_x))]
    _, region = spots((PAD, LANES))
    third = WIDE // 3

    def plane(z):
        c = z // third
        low, high = from_sides(sides, ins_x, lambda ref: ref[THIRD + z - c * third])
        edges = []
        for value in (low, high):
            total = turn(value, (2 * WIDE - c * WIDE))
            for target in (0, 1):
                total = jnp.where(region == target, turn(value, (target - c) * WIDE), total)
            edges.append(total)
        return jnp.concatenate([edges[0], modulus[z, PAD : rows - PAD, :], edges[1]], axis=0)

    return plane


def stiffness(field, modulus, first, last, shift, store):
    rows = field.shape[1]
    _, region = spots((rows, LANES))
    scale = [
        jnp.where(region == c, 0.5 * LAMBDA_RATIO, 0.5) for c in range(3)
    ]

    def one(z, carry):
        below, m = carry
        v = field[z - shift]
        next_m = modulus(z + 1)
        above = (m + next_m) * (field[z + 1 - shift] - v)
        gx = (m + pltpu.roll(m, rows - 1, 0)) * (pltpu.roll(v, rows - 1, 0) - v)
        gy = (m + pltpu.roll(m, LANES - 1, 1)) * (pltpu.roll(v, LANES - 1, 1) - v)
        total = SIGMA_SHIFT * m * v + scale[0] * (below - above)
        total = total + scale[1] * (pltpu.roll(gy, 1, 1) - gy)
        total = total + scale[2] * (pltpu.roll(gx, 1, 0) - gx)
        store(z, total)
        return above, next_m

    m = modulus(first)
    below = (modulus(first - 1) + m) * (field[first - shift] - field[first - 1 - shift])
    lax.fori_loop(first, last + 1, one, (below, m), unroll=4)


def groups_of(refs, sizes):
    found = []
    at = 0
    for size in sizes:
        found.append(refs[at : at + size])
        at += size
    return found


def prepare_kernel(counts, sizes, pos_ref, table_in, load_in, labels_in, mask_in, *refs):
    (modulus_out,), outs_y, outs_z, outs_yz, fetched = groups_of(refs, (1,) + sizes[:3] + (5,))
    table_ref, labels, mask, load, arrived = fetched
    _, count_y, count_z = counts
    copies = [
        pltpu.make_async_copy(source, target, arrived.at[number])
        for number, (source, target) in enumerate(
            [(table_in, table_ref), (labels_in, labels), (mask_in, mask), (load_in, load)]
        )
    ]
    for copy in copies:
        copy.start()
    for copy in copies[:3]:
        copy.wait()

    def one(z, _):
        label = labels[z]
        looked = jnp.zeros(label.shape, F32)
        for k in range(table_ref.shape[0]):
            looked = jnp.where(label == k, table_ref[k], looked)
        modulus_out[z] = jnp.where(mask[z] == 1, looked, VOID_MODULUS)
        return 0

    lax.fori_loop(0, BRICK, one, 0, unroll=4)
    copies[3].wait()
    thin = INTERSECTION
    pairs = BRICK // 2

    def ends(plane, up, count):
        return jnp.where(up, plane[BRICK - count :, :], plane[:count, :])

    for phase, out in enumerate(outs_z):
        up, _ = side(pos_ref, 0, phase, count_z)
        first = pick(up, BRICK - thin, 0)
        for c in range(3):
            for i in range(thin):
                out[c * thin + i] = load[c, first + i]
        first = pick(up, BRICK - REACH, 0)
        for i in range(REACH):
            out[3 * thin + i] = modulus_out[first + i]
    for phase, out in enumerate(outs_y):
        up, _ = side(pos_ref, 1, phase, count_y)
        for c in range(4):
            for z in range(BRICK):
                plane = load[c, z] if c < 3 else modulus_out[z]
                row = z % 2 * thin
                out[c * pairs + z // 2, row : row + thin, :] = ends(plane, up, thin)
        for z in range(BRICK):
            plane = modulus_out[z]
            fifth = jnp.where(
                up, plane[BRICK - REACH : BRICK - thin, :], plane[thin:REACH, :]
            )
            out[4 * pairs + z // 8, z % 8 : z % 8 + 1, :] = fifth
    for number, out in enumerate(outs_yz):
        phase_y, phase_z = divmod(number, len(outs_z))
        up_y, _ = side(pos_ref, 1, phase_y, count_y)
        up_z, _ = side(pos_ref, 0, phase_z, count_z)
        first = pick(up_z, BRICK - thin, 0)
        for c in range(3):
            for i in range(thin):
                row = i % 2 * thin
                out[c * 2 + i // 2, row : row + thin, :] = ends(load[c, first + i], up_y, thin)
        first = pick(up_z, BRICK - REACH, 0)
        for i in range(REACH):
            out[6 + i] = ends(modulus_out[first + i], up_y, 8)


def gather_kernel(counts, sizes, pos_ref, load, *refs):
    ins_y, ins_z, ins_yz, (load_out,), outs_x, (wide,) = groups_of(
        refs, sizes[:3] + (1, sizes[3], 1)
    )
    columns = load.shape[3]
    rows = columns + 2 * PAD
    count_x, count_y, count_z = counts
    thin = INTERSECTION
    pairs = BRICK // 2
    sides_y = [side(pos_ref, 1, phase, count_y) for phase in range(len(ins_y))]
    sides_z = [side(pos_ref, 0, phase, count_z) for phase in range(len(ins_z))]
    blank = jnp.zeros((PAD, LANES), F32)

    def place(slot, c, centre, low, high):
        lane = c * WIDE + REACH
        wide[slot, lane : lane + BRICK, :] = centre
        wide[slot, lane - thin : lane, :] = low
        wide[slot, lane + BRICK : lane + BRICK + thin, :] = high

    def finish(z):
        load_out[z, :PAD, :] = blank
        load_out[z, PAD : PAD + columns, :] = wide[z].T
        load_out[z, rows - PAD :, :] = blank

    def clear(z, _):
        wide[z] = jnp.zeros((LANES, columns), F32)
        return 0

    lax.fori_loop(0, LENGTH, clear, 0, unroll=4)

    def pair(t, _):
        for h in range(2):
            z = 2 * t + h
            for c in range(3):
                low, high = from_sides(
                    sides_y, ins_y, lambda ref: ref[c * pairs + t, h * thin : (h + 1) * thin, :]
                )
                place(z + thin, c, load[c, z], low, high)
        for h in range(2):
            finish(2 * t + h + thin)
        return 0

    lax.fori_loop(0, pairs, pair, 0, unroll=2)
    for i in range(thin):
        row = i % 2 * thin
        for c in range(3):
            centre = from_sides(sides_z, ins_z, lambda ref: ref[c * thin + i])
            corner = [[], []]
            for phase_y in range(len(ins_y)):
                refs_z = ins_yz[phase_y * len(ins_z) : (phase_y + 1) * len(ins_z)]
                found = from_sides(
                    sides_z, refs_z, lambda ref: ref[c * 2 + i // 2, row : row + thin, :]
                )
                corner[0].append(found[0])
                corner[1].append(found[1])
            for which, slot in ((0, i), (1, thin + BRICK + i)):
                low, high = from_sides(sides_y, corner[which], lambda value: value)
                place(slot, c, centre[which], low, high)
        finish(i)
        finish(thin + BRICK + i)
    for phase, out in enumerate(outs_x):
        up, _ = side(pos_ref, 2, phase, count_x)
        start = pl.multiple_of(pick(up, rows - 2 * PAD, PAD), PAD)
        for z in range(LENGTH):
            out[z] = load_out[z, pl.ds(start, PAD), :]


def modulus_kernel(counts, sizes, pos_ref, modulus, *refs):
    ins_y, ins_z, ins_yz, (modulus_out,), (wide,) = groups_of(refs, sizes[:3] + (1, 1))
    columns = modulus.shape[2]
    rows = columns + 2 * PAD
    count_x, count_y, count_z = counts
    thin = INTERSECTION
    pairs = BRICK // 2
    sides_y = [side(pos_ref, 1, phase, count_y) for phase in range(len(ins_y))]
    sides_z = [side(pos_ref, 0, phase, count_z) for phase in range(len(ins_z))]
    blank = jnp.zeros((PAD, LANES), F32)

    def finish(z, centre, low, high, low_end, high_end):
        for c in range(3):
            lane = c * WIDE + REACH
            wide[z, lane : lane + BRICK, :] = centre
            wide[z, lane - thin : lane, :] = low
            wide[z, lane + BRICK : lane + BRICK + thin, :] = high
            wide[z, lane - REACH : lane - thin, :] = low_end
            wide[z, lane + BRICK + thin : lane + BRICK + REACH, :] = high_end
        wide[z, 3 * WIDE :, :] = jnp.zeros((LANES - 3 * WIDE, columns), F32)
        modulus_out[z, :PAD, :] = blank
        modulus_out[z, PAD : PAD + columns, :] = wide[z].T
        modulus_out[z, rows - PAD :, :] = blank

    for z in range(BRICK):
        row = z % 2 * thin
        low, high = from_sides(
            sides_y, ins_y, lambda ref: ref[3 * pairs + z // 2, row : row + thin, :]
        )
        low_end, high_end = from_sides(
            sides_y, ins_y, lambda ref: ref[4 * pairs + z // 8, z % 8 : z % 8 + 1, :]
        )
        finish(z + REACH, modulus[z], low, high, low_end, high_end)
    for i in range(REACH):
        centre = from_sides(sides_z, ins_z, lambda ref: ref[3 * thin + i])
        corner = [[], []]
        for phase_y in range(len(ins_y)):
            refs_z = ins_yz[phase_y * len(ins_z) : (phase_y + 1) * len(ins_z)]
            found = from_sides(sides_z, refs_z, lambda ref: ref[6 + i])
            corner[0].append(found[0])
            corner[1].append(found[1])
        for which, slot in ((0, i), (1, REACH + BRICK + i)):
            low, high = from_sides(sides_y, corner[which], lambda value: value)
            finish(
                slot,
                centre[which],
                low[8 - thin :, :],
                high[:thin, :],
                low[8 - REACH : 8 - thin, :],
                high[thin:REACH, :],
            )


def patched(pos_ref, counts, residual, ins_x):
    rows = residual.shape[1]
    sides = [side(pos_ref, 2, phase, counts[0]) for phase in range(len(ins_x))]

    def plane(z):
        low, high = from_sides(sides, ins_x, lambda ref: ref[z])
        return jnp.concatenate([low, residual[z, PAD : rows - PAD, :], high], axis=0)

    return plane


def first_kernel(counts, sizes, pos_ref, residual, *refs):
    ins_x, consts, (solved,), outs_y, outs_z, outs_yz, (mid,) = groups_of(
        refs, (sizes[3], 10, 1) + sizes[:3] + (1,)
    )
    solve(patched(pos_ref, counts, residual, ins_x), mid, solved, consts)
    write_messages(pos_ref, solved, FOLD, counts, outs_y, outs_z, outs_yz)


NINTH = WIDE
THIRD = NINTH + -(-WIDE // 8)


def edge_kernel(width, counts, sizes, pos_ref, solved, *refs):
    extra = 1 if width == FOLD else 0
    ins_y, ins_z, ins_yz, modulus, outs_x, scratch = groups_of(
        refs, sizes[:3] + (extra, sizes[3], extra)
    )
    rows = solved.shape[1]
    height = 16 if extra else 8
    _, region = spots((PAD, LANES))
    third = WIDE // 3
    for phase, out in enumerate(outs_x):
        up, _ = side(pos_ref, 2, phase, counts[0])
        window = pl.ds(pl.multiple_of(pick(up, rows - height, 0), 8), height)

        found = scratch[0] if extra else out

        def put(plane, value, found=found):
            found[plane] = value

        def get(plane, found=found):
            return found[plane]

        add_messages(pos_ref, solved, width, counts, ins_y, ins_z, ins_yz, window, put, get)
        if extra:
            for z in range(WIDE):
                outer = found[z]
                out[z] = jnp.where(up, outer[8:], outer[:8])
                ninth = jnp.where(up, outer[7:8], outer[8:9])
                out[NINTH + z // 8, z % 8 : z % 8 + 1, :] = ninth
        for ref in modulus:
            place = pl.ds(pl.multiple_of(pick(up, ref.shape[1] - 2 * PAD, PAD), PAD), PAD)
            for k in range(third):
                total = ref[k, place, :]
                for c in (1, 2):
                    total = jnp.where(region == c, ref[k + c * third, place, :], total)
                out[THIRD + k] = total


def fold_kernel(width, counts, sizes, pos_ref, solved, *refs):
    ins_y, ins_z, ins_yz, (field,) = groups_of(refs, sizes[:3] + (1,))
    rows = solved.shape[1]
    thin = INTERSECTION
    core = slice(thin, thin + rows)
    blank = jnp.zeros((thin, LANES), F32)

    def put(plane, value):
        field[plane, core, :] = value

    def get(plane):
        return field[plane, core, :]

    for z in range(field.shape[0]):
        field[z, :thin, :] = blank
        field[z, thin + rows :, :] = blank
    add_messages(pos_ref, solved, width, counts, ins_y, ins_z, ins_yz, None, put, get)


def second_kernel(counts, sizes, pos_ref, partial, residual, modulus, *refs):
    (
        ins_load,
        ins_x,
        consts,
        (solved, field, renewed),
        outs_y,
        outs_z,
        outs_yz,
        (mid,),
    ) = groups_of(refs, (sizes[3], sizes[3], 10, 3) + sizes[:3] + (1,))
    rows = partial.shape[1]
    complete(pos_ref, counts, partial, ins_x, True, field, 0)
    inside, low_z, high_z = grid_masks(pos_ref, rows, counts)
    before = patched(pos_ref, counts, residual, ins_load)

    def store(z, product):
        on = inside & (z >= low_z) & (z < high_z)
        renewed[z - 1] = jnp.where(on, before(z - 1) - product, 0.0)

    stiffness(field, widened(pos_ref, counts, modulus, ins_x), 1, WIDE - 2, 0, store)
    solve(lambda z: renewed[z], mid, solved, consts)
    write_messages(pos_ref, solved, REACH, counts, outs_y, outs_z, outs_yz)


def last_kernel(counts, sizes, pos_ref, partial, modulus, moved, left, *refs):
    ins_x, ins_modulus, (displacement, residual), (field,) = groups_of(
        refs, (sizes[3], sizes[3], 2, 1)
    )
    rows = partial.shape[1]
    first = planes_of(REACH)[0]
    complete(pos_ref, counts, partial, ins_x, False, field, first)
    core = slice(PAD, rows - PAD)

    def store(z, product):
        at = z - REACH
        one = (moved[z, core, :] + field[z - first, core, :]).T
        two = (left[z - 1, core, :] - product[core]).T
        for c in range(3):
            lane = c * WIDE + REACH
            displacement[c, at] = one[lane : lane + BRICK, :]
            residual[c, at] = two[lane : lane + BRICK, :]

    stiffness(
        field,
        widened(pos_ref, counts, modulus, ins_modulus),
        REACH,
        REACH + BRICK - 1,
        first,
        store,
    )


def call(kernel, inputs, outs, scratch=(), distant=0, limit=24, work=0):
    return pl.pallas_call(
        kernel,
        out_shape=[jax.ShapeDtypeStruct(shape, F32) for shape in outs],
        in_specs=[SMEM] + [HBM] * distant + [VMEM] * (len(inputs) - 1 - distant),
        out_specs=[VMEM] * len(outs),
        scratch_shapes=[
            pltpu.VMEM(shape, F32) if isinstance(shape, tuple) else shape for shape in scratch
        ],
        compiler_params=pltpu.CompilerParams(vmem_limit_bytes=limit * 1024 * 1024),
        cost_estimate=pl.CostEstimate(flops=work, bytes_accessed=work, transcendentals=0),
    )(*inputs)


def local(mesh, load, labels, mask, table):
    columns = load.shape[3]
    rows = columns + 2 * PAD
    counts = tuple(lax.axis_size(axis) for axis in ("gx", "gy", "gz"))
    ways = tuple(phases(count) for count in counts)
    sizes = (ways[1], ways[2], ways[1] * ways[2], ways[0])
    pos = jnp.stack([lax.axis_index(axis) for axis in ("gz", "gy", "gx")]).astype(jnp.int32)
    consts = [jnp.asarray(value) for value in tables(columns // BRICK)]
    spectral = (LENGTH, columns // BRICK * LENGTH, LANES)

    def exchange_yz(values):
        y, z, yz = groups_of(values, sizes[:3])
        z = [swap(value, mesh, {"gz": phase}, None) for phase, value in enumerate(z)]
        y = [swap(value, mesh, {"gy": phase}, None) for phase, value in enumerate(y)]
        yz = [
            swap(value, mesh, {"gy": number // ways[2], "gz": number % ways[2]}, None)
            for number, value in enumerate(yz)
        ]
        return [*y, *z, *yz]

    def exchange_x(values):
        return [swap(value, mesh, {"gx": phase}, None) for phase, value in enumerate(values)]

    def message_shapes(width, height):
        groups = WIDE // width
        return (
            [(LENGTH // groups, height, LANES)] * sizes[0]
            + [(width, height, LANES)] * sizes[1]
            + [(-(-3 * width // (LANES // width)), height, LANES)] * sizes[2]
        )

    bind = lambda kernel, *first: functools.partial(kernel, *first, counts, sizes)
    thick = along(columns)
    thin = (LENGTH, thick, LANES)
    tall = (LENGTH, rows, LANES)
    wide = (WIDE, rows, LANES)
    near = len(planes_of(REACH))

    modulus_core, *out = call(
        bind(prepare_kernel),
        [pos, table, load, labels, mask],
        [(BRICK, BRICK, columns)]
        + [(2 * BRICK + BRICK // 8, 8, columns)] * sizes[0]
        + [(3 * INTERSECTION + REACH, BRICK, columns)] * sizes[1]
        + [(6 + REACH, 8, columns)] * sizes[2],
        [
            pltpu.SMEM(table.shape, F32),
            pltpu.VMEM(labels.shape, jnp.int32),
            pltpu.VMEM(mask.shape, jnp.int32),
            pltpu.VMEM(load.shape, F32),
            pltpu.SemaphoreType.DMA((4,)),
        ],
        distant=4,
        limit=61,
    )
    margins = exchange_yz(out)
    residual, *out = call(
        bind(gather_kernel),
        [pos, load, *margins],
        [tall] + [(LENGTH, PAD, LANES)] * sizes[3],
        [(LENGTH, LANES, columns)],
    )
    from_x = exchange_x(out)
    (modulus,) = call(
        bind(modulus_kernel),
        [pos, modulus_core, *margins],
        [wide],
        [(WIDE, LANES, columns)],
        work=8000000,
    )
    solved, *out = call(
        bind(first_kernel),
        [pos, residual, *from_x, *consts],
        [thin] + message_shapes(FOLD, thick),
        [spectral],
    )
    margins = exchange_yz(out)
    first_edges = exchange_x(
        call(
            bind(edge_kernel, FOLD),
            [pos, solved, *margins, modulus],
            [(THIRD + WIDE // 3, 8, LANES)] * sizes[3],
            [(WIDE, 16, LANES)],
        )
    )
    (partial,) = call(
        bind(fold_kernel, FOLD), [pos, solved, *margins], [wide], work=8000000
    )
    solved, moved, left, *out = call(
        bind(second_kernel),
        [pos, partial, residual, modulus, *from_x, *first_edges, *consts],
        [thin, wide, tall] + message_shapes(REACH, thick),
        [spectral],
        limit=32,
    )
    margins = exchange_yz(out)
    edges = exchange_x(
        call(
            bind(edge_kernel, REACH), [pos, solved, *margins], [(near, 8, LANES)] * sizes[3]
        )
    )
    (partial,) = call(
        bind(fold_kernel, REACH), [pos, solved, *margins], [(near, rows, LANES)], work=8000000
    )
    displacement, residual = call(
        bind(last_kernel),
        [pos, partial, modulus, moved, left, *edges, *first_edges],
        [load.shape, load.shape],
        [(near, rows, LANES)],
        limit=32,
    )
    return displacement, residual


def solution(mesh):
    placed = (P(None, "gz", "gy", "gx"), P("gz", "gy", "gx"), P("gz", "gy", "gx"), P())
    return jax.shard_map(
        functools.partial(local, mesh),
        mesh=mesh,
        in_specs=placed,
        out_specs=(P(None, "gz", "gy", "gx"), P(None, "gz", "gy", "gx")),
        check_vma=False,
    )
```

```python
import functools

import jax
import jax.numpy as jnp
import ml_dtypes
import numpy as np
from jax import lax
from jax.experimental import pallas as pl
from jax.experimental.pallas import tpu as pltpu
from jax.sharding import PartitionSpec as P

BRICK = 32
INTERSECTION = 4
LENGTH = BRICK + 2 * INTERSECTION
REACH = INTERSECTION + 1
WIDE = BRICK + 2 * REACH
LANES = 128
PAD = 8
FOLD = 2 * INTERSECTION + 1

LAMBDA_RATIO = 2.0
SIGMA_SHIFT = 0.1
REF_MODULUS = 1.5
VOID_MODULUS = 0.1

F32 = jnp.float32
BF16 = jnp.bfloat16
VMEM = pl.BlockSpec(memory_space=pltpu.VMEM)
SMEM = pl.BlockSpec(memory_space=pltpu.SMEM)
HBM = pl.BlockSpec(memory_space=pltpu.HBM)


def halves(values):
    values = np.asarray(values, np.float32)
    high = values.astype(ml_dtypes.bfloat16)
    low = (values - high.astype(np.float32)).astype(ml_dtypes.bfloat16)
    return high, low


def right_table(values):
    high, low = halves(values)
    return np.block([[high, low], [high, np.zeros_like(low)]]).astype(ml_dtypes.bfloat16)


def left_table(values):
    high, low = halves(values)
    return np.concatenate([high, high, low], axis=1)


def tables(count_x):
    grid = np.arange(1, LENGTH + 1, dtype=np.float64)
    sine = np.sqrt(2.0 / (LENGTH + 1)) * np.sin(np.pi * np.outer(grid, grid) / (LENGTH + 1))
    eigen = 2.0 - 2.0 * np.cos(np.pi * grid / (LENGTH + 1))
    position = np.arange(LENGTH, dtype=np.float64)
    margin = 2 * INTERSECTION
    ramp = np.minimum(
        np.minimum((position + 0.5) / margin, (LENGTH - 0.5 - position) / margin), 1.0
    )
    rows = count_x * BRICK + 2 * PAD
    ramped = ramp[:, None] * sine
    along_y = np.zeros((LANES, LANES))
    back_y = np.zeros((LANES, LANES))
    for c in range(3):
        lane = c * WIDE + 1
        along_y[lane : lane + LENGTH, c * LENGTH : (c + 1) * LENGTH] = ramped
        back_y[c * LENGTH : (c + 1) * LENGTH, lane : lane + LENGTH] = sine
    along_x = np.zeros((count_x * LENGTH, rows))
    back_x = np.zeros((rows - 2 * INTERSECTION, count_x * LENGTH))
    for b in range(count_x):
        row = b * BRICK + PAD - INTERSECTION
        along_x[b * LENGTH : (b + 1) * LENGTH, row : row + LENGTH] = ramped.T
        back_x[b * BRICK : b * BRICK + LENGTH, b * LENGTH : (b + 1) * LENGTH] = sine
    half = LENGTH // 2
    eye = np.eye(8)
    even = left_table(np.kron(ramped[:half, 0::2].T, eye))
    odd = left_table(np.kron(ramped[:half, 1::2].T, eye))
    back_even = left_table(np.kron(sine[0::2, :half].T, eye))
    back_odd = left_table(np.kron(sine[1::2, :half].T, eye))
    ratio = lambda c, d: LAMBDA_RATIO if c == d else 1.0
    base = np.ones((count_x * LENGTH, LANES))
    steps = np.zeros((LENGTH, 8, LANES))
    order = np.concatenate([np.arange(0, LENGTH, 2), np.arange(1, LENGTH, 2)])
    for c in range(3):
        part = slice(c * LENGTH, (c + 1) * LENGTH)
        base[:, part] = REF_MODULUS * (
            ratio(c, 1) * eigen[None, :]
            + ratio(c, 2) * np.tile(eigen, count_x)[:, None]
            + SIGMA_SHIFT
        )
        steps[:, :, part] = REF_MODULUS * ratio(c, 0) * eigen[order][:, None, None]
    return [
        right_table(along_y),
        left_table(along_x),
        even,
        odd,
        back_even,
        back_odd,
        left_table(back_x),
        right_table(back_y),
        base.astype(np.float32),
        steps.astype(np.float32),
    ]


def phases(count):
    return 1 if count <= 2 else 2


def partners(count, phase):
    found = [i + 1 if (i + phase) % 2 == 0 else i - 1 for i in range(count)]
    return [j if 0 <= j < count else i for i, j in enumerate(found)]


def swap(value, mesh, moves, filler):
    names = mesh.axis_names
    shape = [mesh.shape[name] for name in names]
    found = {name: partners(mesh.shape[name], phase) for name, phase in moves.items()}
    spare = None if filler is None else partners(mesh.shape[filler], 0)
    pairs = []
    for place in np.ndindex(*shape):
        target = list(place)
        for name, other in found.items():
            target[names.index(name)] = other[place[names.index(name)]]
        if any(target[names.index(name)] == place[names.index(name)] for name in found):
            target = list(place)
            if filler is not None:
                target[names.index(filler)] = spare[place[names.index(filler)]]
        pairs.append(tuple(int(np.ravel_multi_index(at, shape)) for at in (place, target)))
    if filler is None and len(found) == 1:
        ((name, other),) = found.items()
        return lax.ppermute(value, name, list(enumerate(other)))
    return lax.ppermute(value, names, pairs)


def spots(shape):
    lane = lax.broadcasted_iota(jnp.int32, shape, len(shape) - 1)
    region = jnp.where(lane >= 3 * WIDE, 3, jnp.where(lane >= 2 * WIDE, 2, jnp.where(lane >= WIDE, 1, 0)))
    spot = jnp.where(region == 3, 4 * LANES, lane - region * WIDE)
    return spot, region


def turn(values, shift):
    return pltpu.roll(values, lax.rem(shift + 2 * LANES, LANES), values.ndim - 1)


def pack(planes, width, start, spot, groups):
    total = jnp.zeros(spot.shape, F32)
    for g, plane in enumerate(planes):
        inside = (spot >= g * width) & (spot < (g + 1) * width)
        total = jnp.where(inside, turn(plane, g * width - start), total)
    return total


def unpack(packed, g, width, start, spot, use):
    inside = (spot >= start) & (spot < start + width) & use
    return jnp.where(inside, turn(packed, start - g * width), 0.0)


def side(pos_ref, dim, phase, count):
    place = pos_ref[dim]
    up = lax.rem(place + phase, 2) == 0
    use = jnp.where(up, place < count - 1, place > 0)
    return up, use


def pick(up, high, low):
    return jnp.where(up, high, low)


def two_terms(values):
    high = values.astype(BF16)
    low = (values - high.astype(F32)).astype(BF16)
    return high, low


def right_product(values, table):
    high, low = two_terms(values)
    product = jnp.dot(jnp.concatenate([high, low], axis=1), table, preferred_element_type=F32)
    return product[:, :LANES] + product[:, LANES:]


def left_product(table, values):
    high, low = two_terms(values)
    return jnp.dot(
        table, jnp.concatenate([high, low, high], axis=0), preferred_element_type=F32
    )


def along(columns):
    return columns + 2 * INTERSECTION


def solve(source, mid, target, consts):
    along_y, along_x, even, odd, back_even, back_odd, back_x, back_y, base, steps = consts
    rows = target.shape[1]
    half = LENGTH // 2

    def forward(t, _):
        both = jnp.concatenate([source(2 * t), source(2 * t + 1)], axis=0)
        turned = right_product(both, along_y[...])
        height = both.shape[0] // 2
        pair = jnp.concatenate([turned[:height], turned[height:]], axis=1)
        done = left_product(along_x[...], pair)
        mid[2 * t] = done[:, :LANES]
        mid[2 * t + 1] = done[:, LANES:]
        return 0

    lax.fori_loop(0, half, forward, 0, unroll=10)

    def across(g, _):
        start = pl.multiple_of(g * 16, 16)

        def plane(z):
            return jnp.concatenate(
                [mid[z, pl.ds(start, 8), :], mid[z, pl.ds(start + 8, 8), :]], axis=1
            )

        planes = [plane(z) for z in range(LENGTH)]
        sums = jnp.concatenate([planes[z] + planes[LENGTH - 1 - z] for z in range(half)], axis=0)
        gaps = jnp.concatenate([planes[z] - planes[LENGTH - 1 - z] for z in range(half)], axis=0)
        ground = jnp.concatenate(
            [base[pl.ds(start, 8), :], base[pl.ds(start + 8, 8), :]], axis=1
        )

        def divisors(first):
            return jnp.concatenate(
                [
                    ground + jnp.concatenate([steps[first + k], steps[first + k]], axis=1)
                    for k in range(half)
                ],
                axis=0,
            )

        near = left_product(back_even[...], left_product(even[...], sums) / divisors(0))
        far = left_product(back_odd[...], left_product(odd[...], gaps) / divisors(half))
        lower = near + far
        upper = near - far
        for z in range(half):
            for h in range(2):
                lanes = slice(h * LANES, (h + 1) * LANES)
                mid[z, pl.ds(start + 8 * h, 8), :] = lower[8 * z : 8 * z + 8, lanes]
                mid[LENGTH - 1 - z, pl.ds(start + 8 * h, 8), :] = upper[8 * z : 8 * z + 8, lanes]
        return 0

    lax.fori_loop(0, mid.shape[1] // 16, across, 0, unroll=5)

    def backward(t, _):
        pair = jnp.concatenate([mid[2 * t], mid[2 * t + 1]], axis=1)
        done = left_product(back_x[...], pair)
        both = jnp.concatenate([done[:, :LANES], done[:, LANES:]], axis=0)
        turned = right_product(both, back_y[...])
        target[2 * t] = turned[:rows]
        target[2 * t + 1] = turned[rows:]
        return 0

    lax.fori_loop(0, half, backward, 0, unroll=10)


def write_messages(pos_ref, solved, width, counts, outs_y, outs_z, outs_yz):
    rows = solved.shape[1]
    spot, _ = spots((rows, LANES))
    lane = lax.broadcasted_iota(jnp.int32, (rows, LANES), 1)
    groups = WIDE // width
    _, count_y, count_z = counts
    for phase, out in enumerate(outs_z):
        up, _ = side(pos_ref, 0, phase, count_z)
        first = pick(up, LENGTH - width, 0)
        for i in range(width):
            out[i] = solved[first + i]
    for phase, out in enumerate(outs_y):
        up, _ = side(pos_ref, 1, phase, count_y)
        start = pick(up, WIDE - 1 - width, 1)
        many = LENGTH // groups

        def one(k, _, out=out, start=start, many=many):
            out[k] = pack(
                [solved[g * many + k] for g in range(groups)], width, start, spot, groups
            )
            return 0

        lax.fori_loop(0, many, one, 0, unroll=5)
    for number, out in enumerate(outs_yz):
        phase_y, phase_z = divmod(number, len(outs_z))
        up_y, _ = side(pos_ref, 1, phase_y, count_y)
        up_z, _ = side(pos_ref, 0, phase_z, count_z)
        start = pick(up_y, WIDE - 1 - width, 1)
        first = pick(up_z, LENGTH - width, 0)
        slots = LANES // width
        for k in range(out.shape[0]):
            total = jnp.zeros((rows, LANES), F32)
            for j in range(slots):
                i, c = divmod(k * slots + j, 3)
                if i < width:
                    inside = (lane >= j * width) & (lane < (j + 1) * width)
                    moved = turn(solved[first + i], j * width - c * WIDE - start)
                    total = jnp.where(inside, moved, total)
            out[k] = total


def planes_of(width):
    return range(FOLD - width, WIDE - FOLD + width)


def add_messages(pos_ref, solved, width, counts, ins_y, ins_z, ins_yz, window, put, get):
    height = solved.shape[1] if window is None else window.size
    rows = slice(None) if window is None else window
    spot, region = spots((height, LANES))
    groups = WIDE // width
    _, count_y, count_z = counts
    sides_y = [side(pos_ref, 1, phase, count_y) for phase in range(len(ins_y))]
    sides_z = [side(pos_ref, 0, phase, count_z) for phase in range(len(ins_z))]
    many = LENGTH // groups
    wanted = planes_of(width)
    for z in range(LENGTH):
        if z + 1 not in wanted:
            continue
        g, k = divmod(z, many)
        total = solved[z, rows, :]
        for (up, use), ref in zip(sides_y, ins_y):
            start = pick(up, WIDE - FOLD, FOLD - width)
            total = total + unpack(ref[k, rows, :], g, width, start, spot, use)
        put(z + 1 - wanted[0], total)
    for plane in (0, WIDE - 1):
        if plane in wanted:
            put(plane - wanted[0], jnp.zeros((height, LANES), F32))
    for phase_z, ((up_z, use_z), ref_z) in enumerate(zip(sides_z, ins_z)):
        first = pick(up_z, WIDE - FOLD - wanted[0], 0)
        for i in range(width):
            total = ref_z[i, rows, :]
            for phase_y, (up_y, use_y) in enumerate(sides_y):
                ref = ins_yz[phase_y * len(ins_z) + phase_z]
                start = pick(up_y, WIDE - FOLD, FOLD - width)
                part = jnp.zeros((height, LANES), F32)
                for c in range(3):
                    k, j = divmod(3 * i + c, LANES // width)
                    moved = turn(ref[k, rows, :], start + c * WIDE - j * width)
                    part = jnp.where(region == c, moved, part)
                inside = (spot >= start) & (spot < start + width) & use_y
                total = total + jnp.where(inside, part, 0.0)
            put(first + i, get(first + i) + jnp.where(use_z, total, 0.0))


def grid_masks(pos_ref, rows, counts):
    count_x, count_y, count_z = counts
    spot, _ = spots((rows, LANES))
    row = lax.broadcasted_iota(jnp.int32, (rows, LANES), 0)
    low_y = pick(pos_ref[1] > 0, 0, REACH)
    high_y = pick(pos_ref[1] < count_y - 1, WIDE, REACH + BRICK)
    low_x = pick(pos_ref[2] > 0, 0, PAD)
    high_x = pick(pos_ref[2] < count_x - 1, rows, rows - PAD)
    inside = (spot >= low_y) & (spot < high_y) & (row >= low_x) & (row < high_x)
    low_z = pick(pos_ref[0] > 0, 0, REACH)
    high_z = pick(pos_ref[0] < count_z - 1, WIDE, REACH + BRICK)
    return inside, low_z, high_z


def from_sides(sides, refs, index):
    low = high = None
    for (up, use), ref in zip(sides, refs):
        value = index(ref)
        one = jnp.where(use & jnp.logical_not(up), value, 0.0)
        two = jnp.where(use & up, value, 0.0)
        low = one if low is None else low + one
        high = two if high is None else high + two
    return low, high


def complete(pos_ref, counts, partial, ins_x, ninth, field, first):
    rows = field.shape[1]
    inside, low_z, high_z = grid_masks(pos_ref, rows, counts)
    sides = [side(pos_ref, 2, phase, counts[0]) for phase in range(len(ins_x))]
    row = lax.broadcasted_iota(jnp.int32, (16, LANES), 0)
    blank = jnp.zeros((8, LANES), F32)

    def one(z, _):
        low, high = from_sides(sides, ins_x, lambda ref: ref[z])
        low = pltpu.roll(jnp.concatenate([low, blank], axis=0), 4, 0)
        high = pltpu.roll(jnp.concatenate([high, blank], axis=0), 4, 0)
        if ninth:
            at = z % 8
            under, over = from_sides(
                sides, ins_x, lambda ref: ref[NINTH + z // 8, at : at + 1, :]
            )
            low = jnp.where(row == 3, under, low)
            high = jnp.where(row == 12, over, high)
        on = inside & (z + first >= low_z) & (z + first < high_z)
        whole = jnp.concatenate(
            [
                partial[z, :16, :] + low,
                partial[z, 16 : rows - 16, :],
                partial[z, rows - 16 :, :] + high,
            ],
            axis=0,
        )
        field[z] = jnp.where(on, whole, 0.0)
        return 0

    if ninth:
        for z in range(field.shape[0]):
            one(z, 0)
    else:
        lax.fori_loop(0, field.shape[0], one, 0, unroll=2)


def widened(pos_ref, counts, modulus, ins_x):
    rows = modulus.shape[1]
    sides = [side(pos_ref, 2, phase, counts[0]) for phase in range(len(ins_x))]
    _, region = spots((PAD, LANES))
    third = WIDE // 3

    def plane(z):
        c = z // third
        low, high = from_sides(sides, ins_x, lambda ref: ref[THIRD + z - c * third])
        edges = []
        for value in (low, high):
            total = turn(value, (2 * WIDE - c * WIDE))
            for target in (0, 1):
                total = jnp.where(region == target, turn(value, (target - c) * WIDE), total)
            edges.append(total)
        return jnp.concatenate([edges[0], modulus[z, PAD : rows - PAD, :], edges[1]], axis=0)

    return plane


def stiffness(field, modulus, first, last, shift, store):
    rows = field.shape[1]
    _, region = spots((rows, LANES))
    scale = [
        jnp.where(region == c, 0.5 * LAMBDA_RATIO, 0.5) for c in range(3)
    ]

    def one(z, carry):
        below, m = carry
        v = field[z - shift]
        next_m = modulus(z + 1)
        above = (m + next_m) * (field[z + 1 - shift] - v)
        gx = (m + pltpu.roll(m, rows - 1, 0)) * (pltpu.roll(v, rows - 1, 0) - v)
        gy = (m + pltpu.roll(m, LANES - 1, 1)) * (pltpu.roll(v, LANES - 1, 1) - v)
        total = SIGMA_SHIFT * m * v + scale[0] * (below - above)
        total = total + scale[1] * (pltpu.roll(gy, 1, 1) - gy)
        total = total + scale[2] * (pltpu.roll(gx, 1, 0) - gx)
        store(z, total)
        return above, next_m

    m = modulus(first)
    below = (modulus(first - 1) + m) * (field[first - shift] - field[first - 1 - shift])
    lax.fori_loop(first, last + 1, one, (below, m), unroll=4)


def groups_of(refs, sizes):
    found = []
    at = 0
    for size in sizes:
        found.append(refs[at : at + size])
        at += size
    return found


def prepare_kernel(counts, sizes, pos_ref, table_in, load_in, labels_in, mask_in, *refs):
    (modulus_out,), outs_y, outs_z, outs_yz, fetched = groups_of(refs, (1,) + sizes[:3] + (5,))
    table_ref, labels, mask, load, arrived = fetched
    _, count_y, count_z = counts
    copies = [
        pltpu.make_async_copy(source, target, arrived.at[number])
        for number, (source, target) in enumerate(
            [(table_in, table_ref), (labels_in, labels), (mask_in, mask), (load_in, load)]
        )
    ]
    for copy in copies:
        copy.start()
    for copy in copies[:3]:
        copy.wait()

    def one(z, _):
        label = labels[z]
        looked = jnp.zeros(label.shape, F32)
        for k in range(table_ref.shape[0]):
            looked = jnp.where(label == k, table_ref[k], looked)
        modulus_out[z] = jnp.where(mask[z] == 1, looked, VOID_MODULUS)
        return 0

    lax.fori_loop(0, BRICK, one, 0, unroll=4)
    copies[3].wait()
    thin = INTERSECTION
    pairs = BRICK // 2

    def ends(plane, up, count):
        return jnp.where(up, plane[BRICK - count :, :], plane[:count, :])

    for phase, out in enumerate(outs_z):
        up, _ = side(pos_ref, 0, phase, count_z)
        first = pick(up, BRICK - thin, 0)
        for c in range(3):
            for i in range(thin):
                out[c * thin + i] = load[c, first + i]
        first = pick(up, BRICK - REACH, 0)
        for i in range(REACH):
            out[3 * thin + i] = modulus_out[first + i]
    for phase, out in enumerate(outs_y):
        up, _ = side(pos_ref, 1, phase, count_y)
        for c in range(4):
            for z in range(BRICK):
                plane = load[c, z] if c < 3 else modulus_out[z]
                row = z % 2 * thin
                out[c * pairs + z // 2, row : row + thin, :] = ends(plane, up, thin)
        for z in range(BRICK):
            plane = modulus_out[z]
            fifth = jnp.where(
                up, plane[BRICK - REACH : BRICK - thin, :], plane[thin:REACH, :]
            )
            out[4 * pairs + z // 8, z % 8 : z % 8 + 1, :] = fifth
    for number, out in enumerate(outs_yz):
        phase_y, phase_z = divmod(number, len(outs_z))
        up_y, _ = side(pos_ref, 1, phase_y, count_y)
        up_z, _ = side(pos_ref, 0, phase_z, count_z)
        first = pick(up_z, BRICK - thin, 0)
        for c in range(3):
            for i in range(thin):
                row = i % 2 * thin
                out[c * 2 + i // 2, row : row + thin, :] = ends(load[c, first + i], up_y, thin)
        first = pick(up_z, BRICK - REACH, 0)
        for i in range(REACH):
            out[6 + i] = ends(modulus_out[first + i], up_y, 8)


def gather_kernel(counts, sizes, pos_ref, load, *refs):
    ins_y, ins_z, ins_yz, (load_out,), outs_x, (wide,) = groups_of(
        refs, sizes[:3] + (1, sizes[3], 1)
    )
    columns = load.shape[3]
    rows = columns + 2 * PAD
    count_x, count_y, count_z = counts
    thin = INTERSECTION
    pairs = BRICK // 2
    sides_y = [side(pos_ref, 1, phase, count_y) for phase in range(len(ins_y))]
    sides_z = [side(pos_ref, 0, phase, count_z) for phase in range(len(ins_z))]
    blank = jnp.zeros((PAD, LANES), F32)

    def place(slot, c, centre, low, high):
        lane = c * WIDE + REACH
        wide[slot, lane : lane + BRICK, :] = centre
        wide[slot, lane - thin : lane, :] = low
        wide[slot, lane + BRICK : lane + BRICK + thin, :] = high

    def finish(z):
        load_out[z, :PAD, :] = blank
        load_out[z, PAD : PAD + columns, :] = wide[z].T
        load_out[z, rows - PAD :, :] = blank

    def clear(z, _):
        wide[z] = jnp.zeros((LANES, columns), F32)
        return 0

    lax.fori_loop(0, LENGTH, clear, 0, unroll=4)

    def pair(t, _):
        for h in range(2):
            z = 2 * t + h
            for c in range(3):
                low, high = from_sides(
                    sides_y, ins_y, lambda ref: ref[c * pairs + t, h * thin : (h + 1) * thin, :]
                )
                place(z + thin, c, load[c, z], low, high)
        for h in range(2):
            finish(2 * t + h + thin)
        return 0

    lax.fori_loop(0, pairs, pair, 0, unroll=2)
    for i in range(thin):
        row = i % 2 * thin
        for c in range(3):
            centre = from_sides(sides_z, ins_z, lambda ref: ref[c * thin + i])
            corner = [[], []]
            for phase_y in range(len(ins_y)):
                refs_z = ins_yz[phase_y * len(ins_z) : (phase_y + 1) * len(ins_z)]
                found = from_sides(
                    sides_z, refs_z, lambda ref: ref[c * 2 + i // 2, row : row + thin, :]
                )
                corner[0].append(found[0])
                corner[1].append(found[1])
            for which, slot in ((0, i), (1, thin + BRICK + i)):
                low, high = from_sides(sides_y, corner[which], lambda value: value)
                place(slot, c, centre[which], low, high)
        finish(i)
        finish(thin + BRICK + i)
    for phase, out in enumerate(outs_x):
        up, _ = side(pos_ref, 2, phase, count_x)
        start = pl.multiple_of(pick(up, rows - 2 * PAD, PAD), PAD)
        for z in range(LENGTH):
            out[z] = load_out[z, pl.ds(start, PAD), :]


def modulus_kernel(counts, sizes, pos_ref, modulus, *refs):
    ins_y, ins_z, ins_yz, (modulus_out,), (wide,) = groups_of(refs, sizes[:3] + (1, 1))
    columns = modulus.shape[2]
    rows = columns + 2 * PAD
    count_x, count_y, count_z = counts
    thin = INTERSECTION
    pairs = BRICK // 2
    sides_y = [side(pos_ref, 1, phase, count_y) for phase in range(len(ins_y))]
    sides_z = [side(pos_ref, 0, phase, count_z) for phase in range(len(ins_z))]
    blank = jnp.zeros((PAD, LANES), F32)

    def finish(z, centre, low, high, low_end, high_end):
        for c in range(3):
            lane = c * WIDE + REACH
            wide[z, lane : lane + BRICK, :] = centre
            wide[z, lane - thin : lane, :] = low
            wide[z, lane + BRICK : lane + BRICK + thin, :] = high
            wide[z, lane - REACH : lane - thin, :] = low_end
            wide[z, lane + BRICK + thin : lane + BRICK + REACH, :] = high_end
        wide[z, 3 * WIDE :, :] = jnp.zeros((LANES - 3 * WIDE, columns), F32)
        modulus_out[z, :PAD, :] = blank
        modulus_out[z, PAD : PAD + columns, :] = wide[z].T
        modulus_out[z, rows - PAD :, :] = blank

    for z in range(BRICK):
        row = z % 2 * thin
        low, high = from_sides(
            sides_y, ins_y, lambda ref: ref[3 * pairs + z // 2, row : row + thin, :]
        )
        low_end, high_end = from_sides(
            sides_y, ins_y, lambda ref: ref[4 * pairs + z // 8, z % 8 : z % 8 + 1, :]
        )
        finish(z + REACH, modulus[z], low, high, low_end, high_end)
    for i in range(REACH):
        centre = from_sides(sides_z, ins_z, lambda ref: ref[3 * thin + i])
        corner = [[], []]
        for phase_y in range(len(ins_y)):
            refs_z = ins_yz[phase_y * len(ins_z) : (phase_y + 1) * len(ins_z)]
            found = from_sides(sides_z, refs_z, lambda ref: ref[6 + i])
            corner[0].append(found[0])
            corner[1].append(found[1])
        for which, slot in ((0, i), (1, REACH + BRICK + i)):
            low, high = from_sides(sides_y, corner[which], lambda value: value)
            finish(
                slot,
                centre[which],
                low[8 - thin :, :],
                high[:thin, :],
                low[8 - REACH : 8 - thin, :],
                high[thin:REACH, :],
            )


def patched(pos_ref, counts, residual, ins_x):
    rows = residual.shape[1]
    sides = [side(pos_ref, 2, phase, counts[0]) for phase in range(len(ins_x))]

    def plane(z):
        low, high = from_sides(sides, ins_x, lambda ref: ref[z])
        return jnp.concatenate([low, residual[z, PAD : rows - PAD, :], high], axis=0)

    return plane


def first_kernel(counts, sizes, pos_ref, residual, *refs):
    ins_x, consts, (solved,), outs_y, outs_z, outs_yz, (mid,) = groups_of(
        refs, (sizes[3], 10, 1) + sizes[:3] + (1,)
    )
    solve(patched(pos_ref, counts, residual, ins_x), mid, solved, consts)
    write_messages(pos_ref, solved, FOLD, counts, outs_y, outs_z, outs_yz)


NINTH = WIDE
THIRD = NINTH + -(-WIDE // 8)


def edge_kernel(width, counts, sizes, pos_ref, solved, *refs):
    extra = 1 if width == FOLD else 0
    ins_y, ins_z, ins_yz, modulus, outs_x, scratch = groups_of(
        refs, sizes[:3] + (extra, sizes[3], extra)
    )
    rows = solved.shape[1]
    height = 16 if extra else 8
    _, region = spots((PAD, LANES))
    third = WIDE // 3
    for phase, out in enumerate(outs_x):
        up, _ = side(pos_ref, 2, phase, counts[0])
        window = pl.ds(pl.multiple_of(pick(up, rows - height, 0), 8), height)

        found = scratch[0] if extra else out

        def put(plane, value, found=found):
            found[plane] = value

        def get(plane, found=found):
            return found[plane]

        add_messages(pos_ref, solved, width, counts, ins_y, ins_z, ins_yz, window, put, get)
        if extra:
            for z in range(WIDE):
                outer = found[z]
                out[z] = jnp.where(up, outer[8:], outer[:8])
                ninth = jnp.where(up, outer[7:8], outer[8:9])
                out[NINTH + z // 8, z % 8 : z % 8 + 1, :] = ninth
        for ref in modulus:
            place = pl.ds(pl.multiple_of(pick(up, ref.shape[1] - 2 * PAD, PAD), PAD), PAD)
            for k in range(third):
                total = ref[k, place, :]
                for c in (1, 2):
                    total = jnp.where(region == c, ref[k + c * third, place, :], total)
                out[THIRD + k] = total


def fold_kernel(width, counts, sizes, pos_ref, solved, *refs):
    ins_y, ins_z, ins_yz, (field,) = groups_of(refs, sizes[:3] + (1,))
    rows = solved.shape[1]
    thin = INTERSECTION
    core = slice(thin, thin + rows)
    blank = jnp.zeros((thin, LANES), F32)

    def put(plane, value):
        field[plane, core, :] = value

    def get(plane):
        return field[plane, core, :]

    for z in range(field.shape[0]):
        field[z, :thin, :] = blank
        field[z, thin + rows :, :] = blank
    add_messages(pos_ref, solved, width, counts, ins_y, ins_z, ins_yz, None, put, get)


def second_kernel(counts, sizes, pos_ref, partial, residual, modulus, *refs):
    (
        ins_load,
        ins_x,
        consts,
        (solved, field, renewed),
        outs_y,
        outs_z,
        outs_yz,
        (mid,),
    ) = groups_of(refs, (sizes[3], sizes[3], 10, 3) + sizes[:3] + (1,))
    rows = partial.shape[1]
    complete(pos_ref, counts, partial, ins_x, True, field, 0)
    inside, low_z, high_z = grid_masks(pos_ref, rows, counts)
    before = patched(pos_ref, counts, residual, ins_load)

    def store(z, product):
        on = inside & (z >= low_z) & (z < high_z)
        renewed[z - 1] = jnp.where(on, before(z - 1) - product, 0.0)

    stiffness(field, widened(pos_ref, counts, modulus, ins_x), 1, WIDE - 2, 0, store)
    solve(lambda z: renewed[z], mid, solved, consts)
    write_messages(pos_ref, solved, REACH, counts, outs_y, outs_z, outs_yz)


def last_kernel(counts, sizes, pos_ref, partial, modulus, moved, left, *refs):
    ins_x, ins_modulus, (displacement, residual), (field,) = groups_of(
        refs, (sizes[3], sizes[3], 2, 1)
    )
    rows = partial.shape[1]
    first = planes_of(REACH)[0]
    complete(pos_ref, counts, partial, ins_x, False, field, first)
    core = slice(PAD, rows - PAD)

    def store(z, product):
        at = z - REACH
        one = (moved[z, core, :] + field[z - first, core, :]).T
        two = (left[z - 1, core, :] - product[core]).T
        for c in range(3):
            lane = c * WIDE + REACH
            displacement[c, at] = one[lane : lane + BRICK, :]
            residual[c, at] = two[lane : lane + BRICK, :]

    stiffness(
        field,
        widened(pos_ref, counts, modulus, ins_modulus),
        REACH,
        REACH + BRICK - 1,
        first,
        store,
    )


def call(kernel, inputs, outs, scratch=(), distant=0, limit=24, work=0):
    return pl.pallas_call(
        kernel,
        out_shape=[jax.ShapeDtypeStruct(shape, F32) for shape in outs],
        in_specs=[SMEM] + [HBM] * distant + [VMEM] * (len(inputs) - 1 - distant),
        out_specs=[VMEM] * len(outs),
        scratch_shapes=[
            pltpu.VMEM(shape, F32) if isinstance(shape, tuple) else shape for shape in scratch
        ],
        compiler_params=pltpu.CompilerParams(vmem_limit_bytes=limit * 1024 * 1024),
        cost_estimate=pl.CostEstimate(flops=work, bytes_accessed=work, transcendentals=0),
    )(*inputs)


def local(mesh, load, labels, mask, table):
    columns = load.shape[3]
    rows = columns + 2 * PAD
    counts = tuple(lax.axis_size(axis) for axis in ("gx", "gy", "gz"))
    ways = tuple(phases(count) for count in counts)
    sizes = (ways[1], ways[2], ways[1] * ways[2], ways[0])
    pos = jnp.stack([lax.axis_index(axis) for axis in ("gz", "gy", "gx")]).astype(jnp.int32)
    consts = [jnp.asarray(value) for value in tables(columns // BRICK)]
    spectral = (LENGTH, columns // BRICK * LENGTH, LANES)

    def exchange_yz(values, filler=None):
        y, z, yz = groups_of(values, sizes[:3])
        z = [swap(value, mesh, {"gz": phase}, filler) for phase, value in enumerate(z)]
        y = [swap(value, mesh, {"gy": phase}, None) for phase, value in enumerate(y)]
        yz = [
            swap(value, mesh, {"gy": number // ways[2], "gz": number % ways[2]}, filler)
            for number, value in enumerate(yz)
        ]
        return [*y, *z, *yz]

    def exchange_x(values, filler=None):
        return [swap(value, mesh, {"gx": phase}, filler) for phase, value in enumerate(values)]

    def message_shapes(width, height):
        groups = WIDE // width
        return (
            [(LENGTH // groups, height, LANES)] * sizes[0]
            + [(width, height, LANES)] * sizes[1]
            + [(-(-3 * width // (LANES // width)), height, LANES)] * sizes[2]
        )

    bind = lambda kernel, *first: functools.partial(kernel, *first, counts, sizes)
    thick = along(columns)
    thin = (LENGTH, thick, LANES)
    tall = (LENGTH, rows, LANES)
    wide = (WIDE, rows, LANES)
    near = len(planes_of(REACH))

    modulus_core, *out = call(
        bind(prepare_kernel),
        [pos, table, load, labels, mask],
        [(BRICK, BRICK, columns)]
        + [(2 * BRICK + BRICK // 8, 8, columns)] * sizes[0]
        + [(3 * INTERSECTION + REACH, BRICK, columns)] * sizes[1]
        + [(6 + REACH, 8, columns)] * sizes[2],
        [
            pltpu.SMEM(table.shape, F32),
            pltpu.VMEM(labels.shape, jnp.int32),
            pltpu.VMEM(mask.shape, jnp.int32),
            pltpu.VMEM(load.shape, F32),
            pltpu.SemaphoreType.DMA((4,)),
        ],
        distant=4,
        limit=61,
    )
    margins = exchange_yz(out, "gx")
    residual, *out = call(
        bind(gather_kernel),
        [pos, load, *margins],
        [tall] + [(LENGTH, PAD, LANES)] * sizes[3],
        [(LENGTH, LANES, columns)],
    )
    from_x = exchange_x(out)
    (modulus,) = call(
        bind(modulus_kernel),
        [pos, modulus_core, *margins],
        [wide],
        [(WIDE, LANES, columns)],
        work=8000000,
    )
    solved, *out = call(
        bind(first_kernel),
        [pos, residual, *from_x, *consts],
        [thin] + message_shapes(FOLD, thick),
        [spectral],
    )
    margins = exchange_yz(out)
    first_edges = exchange_x(
        call(
            bind(edge_kernel, FOLD),
            [pos, solved, *margins, modulus],
            [(THIRD + WIDE // 3, 8, LANES)] * sizes[3],
            [(WIDE, 16, LANES)],
        )
    )
    (partial,) = call(
        bind(fold_kernel, FOLD), [pos, solved, *margins], [wide], work=8000000
    )
    solved, moved, left, *out = call(
        bind(second_kernel),
        [pos, partial, residual, modulus, *from_x, *first_edges, *consts],
        [thin, wide, tall] + message_shapes(REACH, thick),
        [spectral],
        limit=32,
    )
    margins = exchange_yz(out)
    edges = exchange_x(
        call(
            bind(edge_kernel, REACH), [pos, solved, *margins], [(near, 8, LANES)] * sizes[3]
        ),
        "gy",
    )
    (partial,) = call(
        bind(fold_kernel, REACH), [pos, solved, *margins], [(near, rows, LANES)], work=8000000
    )
    displacement, residual = call(
        bind(last_kernel),
        [pos, partial, modulus, moved, left, *edges, *first_edges],
        [load.shape, load.shape],
        [(near, rows, LANES)],
        limit=32,
    )
    return displacement, residual


def solution(mesh):
    placed = (P(None, "gz", "gy", "gx"), P("gz", "gy", "gx"), P("gz", "gy", "gx"), P())
    return jax.shard_map(
        functools.partial(local, mesh),
        mesh=mesh,
        in_specs=placed,
        out_specs=(P(None, "gz", "gy", "gx"), P(None, "gz", "gy", "gx")),
        check_vma=False,
    )
```

```python
import functools

import jax
import jax.numpy as jnp
import ml_dtypes
import numpy as np
from jax import lax
from jax.experimental import pallas as pl
from jax.experimental.pallas import tpu as pltpu
from jax.sharding import PartitionSpec as P

BRICK = 32
INTERSECTION = 4
LENGTH = BRICK + 2 * INTERSECTION
REACH = INTERSECTION + 1
WIDE = BRICK + 2 * REACH
LANES = 128
PAD = 8
FOLD = 2 * INTERSECTION + 1

LAMBDA_RATIO = 2.0
SIGMA_SHIFT = 0.1
REF_MODULUS = 1.5
VOID_MODULUS = 0.1

F32 = jnp.float32
BF16 = jnp.bfloat16
VMEM = pl.BlockSpec(memory_space=pltpu.VMEM)
SMEM = pl.BlockSpec(memory_space=pltpu.SMEM)
HBM = pl.BlockSpec(memory_space=pltpu.HBM)


def halves(values):
    values = np.asarray(values, np.float32)
    high = values.astype(ml_dtypes.bfloat16)
    low = (values - high.astype(np.float32)).astype(ml_dtypes.bfloat16)
    return high, low


def right_table(values):
    high, low = halves(values)
    return np.block([[high, low], [high, np.zeros_like(low)]]).astype(ml_dtypes.bfloat16)


def left_table(values):
    high, low = halves(values)
    return np.concatenate([high, high, low], axis=1)


def tables(count_x):
    grid = np.arange(1, LENGTH + 1, dtype=np.float64)
    sine = np.sqrt(2.0 / (LENGTH + 1)) * np.sin(np.pi * np.outer(grid, grid) / (LENGTH + 1))
    eigen = 2.0 - 2.0 * np.cos(np.pi * grid / (LENGTH + 1))
    position = np.arange(LENGTH, dtype=np.float64)
    margin = 2 * INTERSECTION
    ramp = np.minimum(
        np.minimum((position + 0.5) / margin, (LENGTH - 0.5 - position) / margin), 1.0
    )
    rows = count_x * BRICK + 2 * PAD
    ramped = ramp[:, None] * sine
    along_y = np.zeros((LANES, LANES))
    back_y = np.zeros((LANES, LANES))
    for c in range(3):
        lane = c * WIDE + 1
        along_y[lane : lane + LENGTH, c * LENGTH : (c + 1) * LENGTH] = ramped
        back_y[c * LENGTH : (c + 1) * LENGTH, lane : lane + LENGTH] = sine
    along_x = np.zeros((count_x * LENGTH, rows))
    back_x = np.zeros((rows - 2 * INTERSECTION, count_x * LENGTH))
    for b in range(count_x):
        row = b * BRICK + PAD - INTERSECTION
        along_x[b * LENGTH : (b + 1) * LENGTH, row : row + LENGTH] = ramped.T
        back_x[b * BRICK : b * BRICK + LENGTH, b * LENGTH : (b + 1) * LENGTH] = sine
    half = LENGTH // 2
    eye = np.eye(8)
    even = left_table(np.kron(ramped[:half, 0::2].T, eye))
    odd = left_table(np.kron(ramped[:half, 1::2].T, eye))
    back_even = left_table(np.kron(sine[0::2, :half].T, eye))
    back_odd = left_table(np.kron(sine[1::2, :half].T, eye))
    ratio = lambda c, d: LAMBDA_RATIO if c == d else 1.0
    base = np.ones((count_x * LENGTH, LANES))
    steps = np.zeros((LENGTH, 8, LANES))
    order = np.concatenate([np.arange(0, LENGTH, 2), np.arange(1, LENGTH, 2)])
    for c in range(3):
        part = slice(c * LENGTH, (c + 1) * LENGTH)
        base[:, part] = REF_MODULUS * (
            ratio(c, 1) * eigen[None, :]
            + ratio(c, 2) * np.tile(eigen, count_x)[:, None]
            + SIGMA_SHIFT
        )
        steps[:, :, part] = REF_MODULUS * ratio(c, 0) * eigen[order][:, None, None]
    return [
        right_table(along_y),
        left_table(along_x),
        even,
        odd,
        back_even,
        back_odd,
        left_table(back_x),
        right_table(back_y),
        base.astype(np.float32),
        steps.astype(np.float32),
    ]


def phases(count):
    return 1 if count <= 2 else 2


def partners(count, phase):
    found = [i + 1 if (i + phase) % 2 == 0 else i - 1 for i in range(count)]
    return [j if 0 <= j < count else i for i, j in enumerate(found)]


def swap(value, mesh, moves, filler):
    names = mesh.axis_names
    shape = [mesh.shape[name] for name in names]
    found = {name: partners(mesh.shape[name], phase) for name, phase in moves.items()}
    spare = None if filler is None else partners(mesh.shape[filler], 0)
    pairs = []
    for place in np.ndindex(*shape):
        target = list(place)
        for name, other in found.items():
            target[names.index(name)] = other[place[names.index(name)]]
        if any(target[names.index(name)] == place[names.index(name)] for name in found):
            target = list(place)
            if filler is not None:
                target[names.index(filler)] = spare[place[names.index(filler)]]
        pairs.append(tuple(int(np.ravel_multi_index(at, shape)) for at in (place, target)))
    if filler is None and len(found) == 1:
        ((name, other),) = found.items()
        return lax.ppermute(value, name, list(enumerate(other)))
    return lax.ppermute(value, names, pairs)


def spots(shape):
    lane = lax.broadcasted_iota(jnp.int32, shape, len(shape) - 1)
    region = jnp.where(lane >= 3 * WIDE, 3, jnp.where(lane >= 2 * WIDE, 2, jnp.where(lane >= WIDE, 1, 0)))
    spot = jnp.where(region == 3, 4 * LANES, lane - region * WIDE)
    return spot, region


def turn(values, shift):
    return pltpu.roll(values, lax.rem(shift + 2 * LANES, LANES), values.ndim - 1)


def pack(planes, width, start, spot, groups):
    total = jnp.zeros(spot.shape, F32)
    for g, plane in enumerate(planes):
        inside = (spot >= g * width) & (spot < (g + 1) * width)
        total = jnp.where(inside, turn(plane, g * width - start), total)
    return total


def unpack(packed, g, width, start, spot, use):
    inside = (spot >= start) & (spot < start + width) & use
    return jnp.where(inside, turn(packed, start - g * width), 0.0)


def side(pos_ref, dim, phase, count):
    place = pos_ref[dim]
    up = lax.rem(place + phase, 2) == 0
    use = jnp.where(up, place < count - 1, place > 0)
    return up, use


def pick(up, high, low):
    return jnp.where(up, high, low)


def two_terms(values):
    high = values.astype(BF16)
    low = (values - high.astype(F32)).astype(BF16)
    return high, low


def right_product(values, table):
    high, low = two_terms(values)
    product = jnp.dot(jnp.concatenate([high, low], axis=1), table, preferred_element_type=F32)
    return product[:, :LANES] + product[:, LANES:]


def left_product(table, values):
    high, low = two_terms(values)
    return jnp.dot(
        table, jnp.concatenate([high, low, high], axis=0), preferred_element_type=F32
    )


def along(columns):
    return columns + 2 * INTERSECTION


def solve(source, mid, target, consts):
    spectrum(source, mid, consts)
    recover(mid, target, consts[6:8], lambda t: t)


def spectrum(source, mid, consts):
    along_y, along_x, even, odd, back_even, back_odd, back_x, back_y, base, steps = consts
    half = LENGTH // 2

    def forward(t, _):
        both = jnp.concatenate([source(2 * t), source(2 * t + 1)], axis=0)
        turned = right_product(both, along_y[...])
        height = both.shape[0] // 2
        pair = jnp.concatenate([turned[:height], turned[height:]], axis=1)
        done = left_product(along_x[...], pair)
        mid[2 * t] = done[:, :LANES]
        mid[2 * t + 1] = done[:, LANES:]
        return 0

    lax.fori_loop(0, half, forward, 0, unroll=10)

    def across(g, _):
        start = pl.multiple_of(g * 16, 16)

        def plane(z):
            return jnp.concatenate(
                [mid[z, pl.ds(start, 8), :], mid[z, pl.ds(start + 8, 8), :]], axis=1
            )

        planes = [plane(z) for z in range(LENGTH)]
        sums = jnp.concatenate([planes[z] + planes[LENGTH - 1 - z] for z in range(half)], axis=0)
        gaps = jnp.concatenate([planes[z] - planes[LENGTH - 1 - z] for z in range(half)], axis=0)
        ground = jnp.concatenate(
            [base[pl.ds(start, 8), :], base[pl.ds(start + 8, 8), :]], axis=1
        )

        def divisors(first):
            return jnp.concatenate(
                [
                    ground + jnp.concatenate([steps[first + k], steps[first + k]], axis=1)
                    for k in range(half)
                ],
                axis=0,
            )

        near = left_product(back_even[...], left_product(even[...], sums) / divisors(0))
        far = left_product(back_odd[...], left_product(odd[...], gaps) / divisors(half))
        lower = near + far
        upper = near - far
        for z in range(half):
            for h in range(2):
                lanes = slice(h * LANES, (h + 1) * LANES)
                mid[z, pl.ds(start + 8 * h, 8), :] = lower[8 * z : 8 * z + 8, lanes]
                mid[LENGTH - 1 - z, pl.ds(start + 8 * h, 8), :] = upper[8 * z : 8 * z + 8, lanes]
        return 0

    lax.fori_loop(0, mid.shape[1] // 16, across, 0, unroll=5)


def recover(mid, target, consts, where):
    back_x, back_y = consts
    rows = target.shape[1]

    def backward(t, _):
        at = where(t)
        pair = jnp.concatenate([mid[2 * at], mid[2 * at + 1]], axis=1)
        done = left_product(back_x[...], pair)
        both = jnp.concatenate([done[:, :LANES], done[:, LANES:]], axis=0)
        turned = right_product(both, back_y[...])
        target[2 * t] = turned[:rows]
        target[2 * t + 1] = turned[rows:]
        return 0

    lax.fori_loop(0, target.shape[0] // 2, backward, 0, unroll=10)


def write_messages(pos_ref, solved, width, counts, outs_y, outs_z, outs_yz):
    count, rows, _ = solved.shape
    spot, _ = spots((rows, LANES))
    lane = lax.broadcasted_iota(jnp.int32, (rows, LANES), 1)
    groups = WIDE // width
    _, count_y, count_z = counts
    for phase, out in enumerate(outs_z):
        up, _ = side(pos_ref, 0, phase, count_z)
        first = pick(up, count - width, 0)
        for i in range(width):
            out[i] = solved[first + i]
    for phase, out in enumerate(outs_y):
        up, _ = side(pos_ref, 1, phase, count_y)
        start = pick(up, WIDE - 1 - width, 1)
        many = count // groups

        def one(k, _, out=out, start=start, many=many):
            out[k] = pack(
                [solved[g * many + k] for g in range(groups)], width, start, spot, groups
            )
            return 0

        lax.fori_loop(0, many, one, 0, unroll=5)
    for number, out in enumerate(outs_yz):
        phase_y, phase_z = divmod(number, len(outs_z))
        up_y, _ = side(pos_ref, 1, phase_y, count_y)
        up_z, _ = side(pos_ref, 0, phase_z, count_z)
        start = pick(up_y, WIDE - 1 - width, 1)
        first = pick(up_z, count - width, 0)
        slots = LANES // width
        for k in range(out.shape[0]):
            total = jnp.zeros((rows, LANES), F32)
            for j in range(slots):
                i, c = divmod(k * slots + j, 3)
                if i < width:
                    inside = (lane >= j * width) & (lane < (j + 1) * width)
                    moved = turn(solved[first + i], j * width - c * WIDE - start)
                    total = jnp.where(inside, moved, total)
            out[k] = total


QUARTER = LENGTH // 4


def place_of(z, parts):
    if parts == 1:
        return 0, z
    if QUARTER <= z < LENGTH - QUARTER:
        return 1, z - QUARTER
    return 0, z if z < QUARTER else z - 2 * QUARTER


def planes_of(width):
    return range(FOLD - width, WIDE - FOLD + width)


def add_messages(pos_ref, solved, width, counts, ins_y, ins_z, ins_yz, window, put, get):
    height = solved[0].shape[1] if window is None else window.size
    rows = slice(None) if window is None else window
    spot, region = spots((height, LANES))
    groups = WIDE // width
    _, count_y, count_z = counts
    parts = len(solved)
    sides_y = [side(pos_ref, 1, phase, count_y) for phase in range(len(ins_y))]
    sides_z = [side(pos_ref, 0, phase, count_z) for phase in range(len(ins_z))]
    many = LENGTH // groups
    wanted = planes_of(width)
    for z in range(LENGTH):
        if z + 1 not in wanted:
            continue
        part, at = place_of(z, parts)
        g, k = divmod(z, many)
        total = solved[part][at, rows, :]
        for (up, use), ref in zip(sides_y, ins_y):
            start = pick(up, WIDE - FOLD, FOLD - width)
            total = total + unpack(ref[k, rows, :], g, width, start, spot, use)
        put(z + 1 - wanted[0], total)
    for plane in (0, WIDE - 1):
        if plane in wanted:
            put(plane - wanted[0], jnp.zeros((height, LANES), F32))
    for phase_z, ((up_z, use_z), ref_z) in enumerate(zip(sides_z, ins_z)):
        first = pick(up_z, WIDE - FOLD - wanted[0], 0)
        for i in range(width):
            total = ref_z[i, rows, :]
            for phase_y, (up_y, use_y) in enumerate(sides_y):
                ref = ins_yz[phase_y * len(ins_z) + phase_z]
                start = pick(up_y, WIDE - FOLD, FOLD - width)
                part = jnp.zeros((height, LANES), F32)
                for c in range(3):
                    k, j = divmod(3 * i + c, LANES // width)
                    moved = turn(ref[k, rows, :], start + c * WIDE - j * width)
                    part = jnp.where(region == c, moved, part)
                inside = (spot >= start) & (spot < start + width) & use_y
                total = total + jnp.where(inside, part, 0.0)
            put(first + i, get(first + i) + jnp.where(use_z, total, 0.0))


def grid_masks(pos_ref, rows, counts):
    count_x, count_y, count_z = counts
    spot, _ = spots((rows, LANES))
    row = lax.broadcasted_iota(jnp.int32, (rows, LANES), 0)
    low_y = pick(pos_ref[1] > 0, 0, REACH)
    high_y = pick(pos_ref[1] < count_y - 1, WIDE, REACH + BRICK)
    low_x = pick(pos_ref[2] > 0, 0, PAD)
    high_x = pick(pos_ref[2] < count_x - 1, rows, rows - PAD)
    inside = (spot >= low_y) & (spot < high_y) & (row >= low_x) & (row < high_x)
    low_z = pick(pos_ref[0] > 0, 0, REACH)
    high_z = pick(pos_ref[0] < count_z - 1, WIDE, REACH + BRICK)
    return inside, low_z, high_z


def from_sides(sides, refs, index):
    low = high = None
    for (up, use), ref in zip(sides, refs):
        value = index(ref)
        one = jnp.where(use & jnp.logical_not(up), value, 0.0)
        two = jnp.where(use & up, value, 0.0)
        low = one if low is None else low + one
        high = two if high is None else high + two
    return low, high


def complete(pos_ref, counts, partial, ins_x, ninth, field, first):
    rows = field.shape[1]
    inside, low_z, high_z = grid_masks(pos_ref, rows, counts)
    sides = [side(pos_ref, 2, phase, counts[0]) for phase in range(len(ins_x))]
    row = lax.broadcasted_iota(jnp.int32, (16, LANES), 0)
    blank = jnp.zeros((8, LANES), F32)

    def one(z, _):
        low, high = from_sides(sides, ins_x, lambda ref: ref[z])
        low = pltpu.roll(jnp.concatenate([low, blank], axis=0), 4, 0)
        high = pltpu.roll(jnp.concatenate([high, blank], axis=0), 4, 0)
        if ninth:
            at = z % 8
            under, over = from_sides(
                sides, ins_x, lambda ref: ref[NINTH + z // 8, at : at + 1, :]
            )
            low = jnp.where(row == 3, under, low)
            high = jnp.where(row == 12, over, high)
        on = inside & (z + first >= low_z) & (z + first < high_z)
        whole = jnp.concatenate(
            [
                partial[z, :16, :] + low,
                partial[z, 16 : rows - 16, :],
                partial[z, rows - 16 :, :] + high,
            ],
            axis=0,
        )
        field[z] = jnp.where(on, whole, 0.0)
        return 0

    if ninth:
        for z in range(field.shape[0]):
            one(z, 0)
    else:
        lax.fori_loop(0, field.shape[0], one, 0, unroll=2)


def widened(pos_ref, counts, modulus, ins_x):
    rows = modulus.shape[1]
    sides = [side(pos_ref, 2, phase, counts[0]) for phase in range(len(ins_x))]
    _, region = spots((PAD, LANES))
    third = WIDE // 3

    def plane(z):
        c = z // third
        low, high = from_sides(sides, ins_x, lambda ref: ref[THIRD + z - c * third])
        edges = []
        for value in (low, high):
            total = turn(value, (2 * WIDE - c * WIDE))
            for target in (0, 1):
                total = jnp.where(region == target, turn(value, (target - c) * WIDE), total)
            edges.append(total)
        return jnp.concatenate([edges[0], modulus[z, PAD : rows - PAD, :], edges[1]], axis=0)

    return plane


def stiffness(field, modulus, first, last, shift, store):
    rows = field.shape[1]
    _, region = spots((rows, LANES))
    scale = [
        jnp.where(region == c, 0.5 * LAMBDA_RATIO, 0.5) for c in range(3)
    ]

    def one(z, carry):
        below, m = carry
        v = field[z - shift]
        next_m = modulus(z + 1)
        above = (m + next_m) * (field[z + 1 - shift] - v)
        gx = (m + pltpu.roll(m, rows - 1, 0)) * (pltpu.roll(v, rows - 1, 0) - v)
        gy = (m + pltpu.roll(m, LANES - 1, 1)) * (pltpu.roll(v, LANES - 1, 1) - v)
        total = SIGMA_SHIFT * m * v + scale[0] * (below - above)
        total = total + scale[1] * (pltpu.roll(gy, 1, 1) - gy)
        total = total + scale[2] * (pltpu.roll(gx, 1, 0) - gx)
        store(z, total)
        return above, next_m

    m = modulus(first)
    below = (modulus(first - 1) + m) * (field[first - shift] - field[first - 1 - shift])
    lax.fori_loop(first, last + 1, one, (below, m), unroll=4)


def groups_of(refs, sizes):
    found = []
    at = 0
    for size in sizes:
        found.append(refs[at : at + size])
        at += size
    return found


def prepare_kernel(counts, sizes, pos_ref, table_in, load_in, labels_in, mask_in, *refs):
    (modulus_out,), outs_y, outs_z, outs_yz, fetched = groups_of(refs, (1,) + sizes[:3] + (5,))
    table_ref, labels, mask, load, arrived = fetched
    _, count_y, count_z = counts
    copies = [
        pltpu.make_async_copy(source, target, arrived.at[number])
        for number, (source, target) in enumerate(
            [(table_in, table_ref), (labels_in, labels), (mask_in, mask), (load_in, load)]
        )
    ]
    for copy in copies:
        copy.start()
    for copy in copies[:3]:
        copy.wait()

    def one(z, _):
        label = labels[z]
        looked = jnp.zeros(label.shape, F32)
        for k in range(table_ref.shape[0]):
            looked = jnp.where(label == k, table_ref[k], looked)
        modulus_out[z] = jnp.where(mask[z] == 1, looked, VOID_MODULUS)
        return 0

    lax.fori_loop(0, BRICK, one, 0, unroll=4)
    copies[3].wait()
    thin = INTERSECTION
    pairs = BRICK // 2

    def ends(plane, up, count):
        return jnp.where(up, plane[BRICK - count :, :], plane[:count, :])

    for phase, out in enumerate(outs_z):
        up, _ = side(pos_ref, 0, phase, count_z)
        first = pick(up, BRICK - thin, 0)
        for c in range(3):
            for i in range(thin):
                out[c * thin + i] = load[c, first + i]
        first = pick(up, BRICK - REACH, 0)
        for i in range(REACH):
            out[3 * thin + i] = modulus_out[first + i]
    for phase, out in enumerate(outs_y):
        up, _ = side(pos_ref, 1, phase, count_y)
        for c in range(4):
            for z in range(BRICK):
                plane = load[c, z] if c < 3 else modulus_out[z]
                row = z % 2 * thin
                out[c * pairs + z // 2, row : row + thin, :] = ends(plane, up, thin)
        for z in range(BRICK):
            plane = modulus_out[z]
            fifth = jnp.where(
                up, plane[BRICK - REACH : BRICK - thin, :], plane[thin:REACH, :]
            )
            out[4 * pairs + z // 8, z % 8 : z % 8 + 1, :] = fifth
    for number, out in enumerate(outs_yz):
        phase_y, phase_z = divmod(number, len(outs_z))
        up_y, _ = side(pos_ref, 1, phase_y, count_y)
        up_z, _ = side(pos_ref, 0, phase_z, count_z)
        first = pick(up_z, BRICK - thin, 0)
        for c in range(3):
            for i in range(thin):
                row = i % 2 * thin
                out[c * 2 + i // 2, row : row + thin, :] = ends(load[c, first + i], up_y, thin)
        first = pick(up_z, BRICK - REACH, 0)
        for i in range(REACH):
            out[6 + i] = ends(modulus_out[first + i], up_y, 8)


def gather_kernel(counts, sizes, pos_ref, load, *refs):
    ins_y, ins_z, ins_yz, (load_out,), outs_x, (wide,) = groups_of(
        refs, sizes[:3] + (1, sizes[3], 1)
    )
    columns = load.shape[3]
    rows = columns + 2 * PAD
    count_x, count_y, count_z = counts
    thin = INTERSECTION
    pairs = BRICK // 2
    sides_y = [side(pos_ref, 1, phase, count_y) for phase in range(len(ins_y))]
    sides_z = [side(pos_ref, 0, phase, count_z) for phase in range(len(ins_z))]
    blank = jnp.zeros((PAD, LANES), F32)

    def place(slot, c, centre, low, high):
        lane = c * WIDE + REACH
        wide[slot, lane : lane + BRICK, :] = centre
        wide[slot, lane - thin : lane, :] = low
        wide[slot, lane + BRICK : lane + BRICK + thin, :] = high

    def finish(z):
        load_out[z, :PAD, :] = blank
        load_out[z, PAD : PAD + columns, :] = wide[z].T
        load_out[z, rows - PAD :, :] = blank

    def clear(z, _):
        wide[z] = jnp.zeros((LANES, columns), F32)
        return 0

    lax.fori_loop(0, LENGTH, clear, 0, unroll=4)

    def pair(t, _):
        for h in range(2):
            z = 2 * t + h
            for c in range(3):
                low, high = from_sides(
                    sides_y, ins_y, lambda ref: ref[c * pairs + t, h * thin : (h + 1) * thin, :]
                )
                place(z + thin, c, load[c, z], low, high)
        for h in range(2):
            finish(2 * t + h + thin)
        return 0

    lax.fori_loop(0, pairs, pair, 0, unroll=2)
    for i in range(thin):
        row = i % 2 * thin
        for c in range(3):
            centre = from_sides(sides_z, ins_z, lambda ref: ref[c * thin + i])
            corner = [[], []]
            for phase_y in range(len(ins_y)):
                refs_z = ins_yz[phase_y * len(ins_z) : (phase_y + 1) * len(ins_z)]
                found = from_sides(
                    sides_z, refs_z, lambda ref: ref[c * 2 + i // 2, row : row + thin, :]
                )
                corner[0].append(found[0])
                corner[1].append(found[1])
            for which, slot in ((0, i), (1, thin + BRICK + i)):
                low, high = from_sides(sides_y, corner[which], lambda value: value)
                place(slot, c, centre[which], low, high)
        finish(i)
        finish(thin + BRICK + i)
    for phase, out in enumerate(outs_x):
        up, _ = side(pos_ref, 2, phase, count_x)
        start = pl.multiple_of(pick(up, rows - 2 * PAD, PAD), PAD)
        for z in range(LENGTH):
            out[z] = load_out[z, pl.ds(start, PAD), :]


def modulus_kernel(counts, sizes, pos_ref, modulus, *refs):
    ins_y, ins_z, ins_yz, (modulus_out,), (wide,) = groups_of(refs, sizes[:3] + (1, 1))
    columns = modulus.shape[2]
    rows = columns + 2 * PAD
    count_x, count_y, count_z = counts
    thin = INTERSECTION
    pairs = BRICK // 2
    sides_y = [side(pos_ref, 1, phase, count_y) for phase in range(len(ins_y))]
    sides_z = [side(pos_ref, 0, phase, count_z) for phase in range(len(ins_z))]
    blank = jnp.zeros((PAD, LANES), F32)

    def finish(z, centre, low, high, low_end, high_end):
        for c in range(3):
            lane = c * WIDE + REACH
            wide[z, lane : lane + BRICK, :] = centre
            wide[z, lane - thin : lane, :] = low
            wide[z, lane + BRICK : lane + BRICK + thin, :] = high
            wide[z, lane - REACH : lane - thin, :] = low_end
            wide[z, lane + BRICK + thin : lane + BRICK + REACH, :] = high_end
        wide[z, 3 * WIDE :, :] = jnp.zeros((LANES - 3 * WIDE, columns), F32)
        modulus_out[z, :PAD, :] = blank
        modulus_out[z, PAD : PAD + columns, :] = wide[z].T
        modulus_out[z, rows - PAD :, :] = blank

    for z in range(BRICK):
        row = z % 2 * thin
        low, high = from_sides(
            sides_y, ins_y, lambda ref: ref[3 * pairs + z // 2, row : row + thin, :]
        )
        low_end, high_end = from_sides(
            sides_y, ins_y, lambda ref: ref[4 * pairs + z // 8, z % 8 : z % 8 + 1, :]
        )
        finish(z + REACH, modulus[z], low, high, low_end, high_end)
    for i in range(REACH):
        centre = from_sides(sides_z, ins_z, lambda ref: ref[3 * thin + i])
        corner = [[], []]
        for phase_y in range(len(ins_y)):
            refs_z = ins_yz[phase_y * len(ins_z) : (phase_y + 1) * len(ins_z)]
            found = from_sides(sides_z, refs_z, lambda ref: ref[6 + i])
            corner[0].append(found[0])
            corner[1].append(found[1])
        for which, slot in ((0, i), (1, REACH + BRICK + i)):
            low, high = from_sides(sides_y, corner[which], lambda value: value)
            finish(
                slot,
                centre[which],
                low[8 - thin :, :],
                high[:thin, :],
                low[8 - REACH : 8 - thin, :],
                high[thin:REACH, :],
            )


def patched(pos_ref, counts, residual, ins_x):
    rows = residual.shape[1]
    sides = [side(pos_ref, 2, phase, counts[0]) for phase in range(len(ins_x))]

    def plane(z):
        low, high = from_sides(sides, ins_x, lambda ref: ref[z])
        return jnp.concatenate([low, residual[z, PAD : rows - PAD, :], high], axis=0)

    return plane


def first_kernel(counts, sizes, pos_ref, residual, *refs):
    ins_x, consts, (outer, mid), outs_z, outs_yz = groups_of(
        refs, (sizes[3], 10, 2) + sizes[1:3]
    )
    spectrum(patched(pos_ref, counts, residual, ins_x), mid, consts)
    quarter = QUARTER // 2
    recover(mid, outer, consts[6:8], lambda t: jnp.where(t < quarter, t, t + 2 * quarter))
    write_messages(pos_ref, outer, FOLD, counts, [], outs_z, outs_yz)


def inner_kernel(counts, sizes, pos_ref, outer, mid, back_x, back_y, inner, *outs_y):
    recover(mid, inner, (back_x, back_y), lambda t: t + QUARTER // 2)
    spot, _ = spots(outer.shape[1:])
    groups = WIDE // FOLD
    many = LENGTH // groups
    for phase, out in enumerate(outs_y):
        up, _ = side(pos_ref, 1, phase, counts[1])
        start = pick(up, WIDE - 1 - FOLD, 1)
        for k in range(many):
            places = [place_of(g * many + k, 2) for g in range(groups)]
            planes = [(outer, inner)[part][at] for part, at in places]
            out[k] = pack(planes, FOLD, start, spot, groups)


NINTH = WIDE
THIRD = NINTH + -(-WIDE // 8)


def edge_kernel(width, counts, sizes, pos_ref, *refs):
    extra = 1 if width == FOLD else 0
    parts = 1 + extra
    solved, ins_y, ins_z, ins_yz, modulus, outs_x, scratch = groups_of(
        refs, (parts,) + sizes[:3] + (extra, sizes[3], extra)
    )
    rows = solved[0].shape[1]
    height = 16 if extra else 8
    _, region = spots((PAD, LANES))
    third = WIDE // 3
    for phase, out in enumerate(outs_x):
        up, _ = side(pos_ref, 2, phase, counts[0])
        window = pl.ds(pl.multiple_of(pick(up, rows - height, 0), 8), height)

        found = scratch[0] if extra else out

        def put(plane, value, found=found):
            found[plane] = value

        def get(plane, found=found):
            return found[plane]

        add_messages(pos_ref, solved, width, counts, ins_y, ins_z, ins_yz, window, put, get)
        if extra:
            for z in range(WIDE):
                outer = found[z]
                out[z] = jnp.where(up, outer[8:], outer[:8])
                ninth = jnp.where(up, outer[7:8], outer[8:9])
                out[NINTH + z // 8, z % 8 : z % 8 + 1, :] = ninth
        for ref in modulus:
            place = pl.ds(pl.multiple_of(pick(up, ref.shape[1] - 2 * PAD, PAD), PAD), PAD)
            for k in range(third):
                total = ref[k, place, :]
                for c in (1, 2):
                    total = jnp.where(region == c, ref[k + c * third, place, :], total)
                out[THIRD + k] = total


def fold_kernel(width, counts, sizes, pos_ref, *refs):
    parts = 2 if width == FOLD else 1
    solved, ins_y, ins_z, ins_yz, (field,) = groups_of(
        refs, (parts,) + sizes[:3] + (1,)
    )
    rows = solved[0].shape[1]
    thin = INTERSECTION
    core = slice(thin, thin + rows)
    blank = jnp.zeros((thin, LANES), F32)

    def put(plane, value):
        field[plane, core, :] = value

    def get(plane):
        return field[plane, core, :]

    for z in range(field.shape[0]):
        field[z, :thin, :] = blank
        field[z, thin + rows :, :] = blank
    add_messages(pos_ref, solved, width, counts, ins_y, ins_z, ins_yz, None, put, get)


def second_kernel(counts, sizes, pos_ref, partial, residual, modulus, *refs):
    (
        ins_load,
        ins_x,
        consts,
        (solved, field, renewed),
        outs_y,
        outs_z,
        outs_yz,
        (mid,),
    ) = groups_of(refs, (sizes[3], sizes[3], 10, 3) + sizes[:3] + (1,))
    rows = partial.shape[1]
    complete(pos_ref, counts, partial, ins_x, True, field, 0)
    inside, low_z, high_z = grid_masks(pos_ref, rows, counts)
    before = patched(pos_ref, counts, residual, ins_load)

    def store(z, product):
        on = inside & (z >= low_z) & (z < high_z)
        renewed[z - 1] = jnp.where(on, before(z - 1) - product, 0.0)

    stiffness(field, widened(pos_ref, counts, modulus, ins_x), 1, WIDE - 2, 0, store)
    solve(lambda z: renewed[z], mid, solved, consts)
    write_messages(pos_ref, solved, REACH, counts, outs_y, outs_z, outs_yz)


def last_kernel(counts, sizes, pos_ref, partial, modulus, moved, left, *refs):
    ins_x, ins_modulus, (displacement, residual), (field,) = groups_of(
        refs, (sizes[3], sizes[3], 2, 1)
    )
    rows = partial.shape[1]
    first = planes_of(REACH)[0]
    complete(pos_ref, counts, partial, ins_x, False, field, first)
    core = slice(PAD, rows - PAD)

    def store(z, product):
        at = z - REACH
        one = (moved[z, core, :] + field[z - first, core, :]).T
        two = (left[z - 1, core, :] - product[core]).T
        for c in range(3):
            lane = c * WIDE + REACH
            displacement[c, at] = one[lane : lane + BRICK, :]
            residual[c, at] = two[lane : lane + BRICK, :]

    stiffness(
        field,
        widened(pos_ref, counts, modulus, ins_modulus),
        REACH,
        REACH + BRICK - 1,
        first,
        store,
    )


def call(kernel, inputs, outs, scratch=(), distant=0, limit=24, work=0):
    return pl.pallas_call(
        kernel,
        out_shape=[jax.ShapeDtypeStruct(shape, F32) for shape in outs],
        in_specs=[SMEM] + [HBM] * distant + [VMEM] * (len(inputs) - 1 - distant),
        out_specs=[VMEM] * len(outs),
        scratch_shapes=[
            pltpu.VMEM(shape, F32) if isinstance(shape, tuple) else shape for shape in scratch
        ],
        compiler_params=pltpu.CompilerParams(vmem_limit_bytes=limit * 1024 * 1024),
        cost_estimate=pl.CostEstimate(flops=work, bytes_accessed=work, transcendentals=0),
    )(*inputs)


def local(mesh, load, labels, mask, table):
    columns = load.shape[3]
    rows = columns + 2 * PAD
    counts = tuple(lax.axis_size(axis) for axis in ("gx", "gy", "gz"))
    ways = tuple(phases(count) for count in counts)
    sizes = (ways[1], ways[2], ways[1] * ways[2], ways[0])
    pos = jnp.stack([lax.axis_index(axis) for axis in ("gz", "gy", "gx")]).astype(jnp.int32)
    consts = [jnp.asarray(value) for value in tables(columns // BRICK)]
    spectral = (LENGTH, columns // BRICK * LENGTH, LANES)

    def exchange_yz(values, filler=None):
        y, z, yz = groups_of(values, (len(values) - sizes[1] - sizes[2],) + sizes[1:3])
        z = [swap(value, mesh, {"gz": phase}, filler) for phase, value in enumerate(z)]
        y = [swap(value, mesh, {"gy": n % ways[1]}, None) for n, value in enumerate(y)]
        yz = [
            swap(value, mesh, {"gy": number // ways[2], "gz": number % ways[2]}, filler)
            for number, value in enumerate(yz)
        ]
        return [*y, *z, *yz]

    def exchange_x(values, filler=None):
        return [swap(value, mesh, {"gx": phase}, filler) for phase, value in enumerate(values)]

    def message_shapes(width, height, count=LENGTH):
        groups = WIDE // width
        return (
            [(count // groups, height, LANES)] * sizes[0]
            + [(width, height, LANES)] * sizes[1]
            + [(-(-3 * width // (LANES // width)), height, LANES)] * sizes[2]
        )

    bind = lambda kernel, *first: functools.partial(kernel, *first, counts, sizes)
    thick = along(columns)
    thin = (LENGTH, thick, LANES)
    tall = (LENGTH, rows, LANES)
    wide = (WIDE, rows, LANES)
    near = len(planes_of(REACH))

    modulus_core, *out = call(
        bind(prepare_kernel),
        [pos, table, load, labels, mask],
        [(BRICK, BRICK, columns)]
        + [(2 * BRICK + BRICK // 8, 8, columns)] * sizes[0]
        + [(3 * INTERSECTION + REACH, BRICK, columns)] * sizes[1]
        + [(6 + REACH, 8, columns)] * sizes[2],
        [
            pltpu.SMEM(table.shape, F32),
            pltpu.VMEM(labels.shape, jnp.int32),
            pltpu.VMEM(mask.shape, jnp.int32),
            pltpu.VMEM(load.shape, F32),
            pltpu.SemaphoreType.DMA((4,)),
        ],
        distant=4,
        limit=61,
    )
    margins = exchange_yz(out, "gx")
    residual, *out = call(
        bind(gather_kernel),
        [pos, load, *margins],
        [tall] + [(LENGTH, PAD, LANES)] * sizes[3],
        [(LENGTH, LANES, columns)],
    )
    from_x = exchange_x(out)
    (modulus,) = call(
        bind(modulus_kernel),
        [pos, modulus_core, *margins],
        [wide],
        [(WIDE, LANES, columns)],
        work=8000000,
    )
    part = (LENGTH // 2, thick, LANES)
    first_shapes = message_shapes(FOLD, thick)
    outer, mid, *out = call(
        bind(first_kernel), [pos, residual, *from_x, *consts], [part, spectral] + first_shapes[sizes[0] :]
    )
    inner, *late = call(
        bind(inner_kernel),
        [pos, outer, mid, *consts[6:8]],
        [part] + first_shapes[: sizes[0]],
        work=8000000,
    )
    solved = [outer, inner]
    margins = exchange_yz([*late, *out])
    first_edges = exchange_x(
        call(
            bind(edge_kernel, FOLD),
            [pos, *solved, *margins, modulus],
            [(THIRD + WIDE // 3, 8, LANES)] * sizes[3],
            [(WIDE, 16, LANES)],
        )
    )
    (partial,) = call(
        bind(fold_kernel, FOLD), [pos, *solved, *margins], [wide], work=8000000
    )
    solved, moved, left, *out = call(
        bind(second_kernel),
        [pos, partial, residual, modulus, *from_x, *first_edges, *consts],
        [thin, wide, tall] + message_shapes(REACH, thick),
        [spectral],
        limit=32,
    )
    margins = exchange_yz(out)
    edges = exchange_x(
        call(
            bind(edge_kernel, REACH), [pos, solved, *margins], [(near, 8, LANES)] * sizes[3]
        ),
        "gy",
    )
    (partial,) = call(
        bind(fold_kernel, REACH), [pos, solved, *margins], [(near, rows, LANES)], work=8000000
    )
    displacement, residual = call(
        bind(last_kernel),
        [pos, partial, modulus, moved, left, *edges, *first_edges],
        [load.shape, load.shape],
        [(near, rows, LANES)],
        limit=32,
    )
    return displacement, residual


def solution(mesh):
    placed = (P(None, "gz", "gy", "gx"), P("gz", "gy", "gx"), P("gz", "gy", "gx"), P())
    return jax.shard_map(
        functools.partial(local, mesh),
        mesh=mesh,
        in_specs=placed,
        out_specs=(P(None, "gz", "gy", "gx"), P(None, "gz", "gy", "gx")),
        check_vma=False,
    )
```

```python
import functools

import jax
import jax.numpy as jnp
import ml_dtypes
import numpy as np
from jax import lax
from jax.experimental import pallas as pl
from jax.experimental.pallas import tpu as pltpu
from jax.sharding import PartitionSpec as P

BRICK = 32
INTERSECTION = 4
LENGTH = BRICK + 2 * INTERSECTION
REACH = INTERSECTION + 1
WIDE = BRICK + 2 * REACH
LANES = 128
PAD = 8
FOLD = 2 * INTERSECTION + 1

LAMBDA_RATIO = 2.0
SIGMA_SHIFT = 0.1
REF_MODULUS = 1.5
VOID_MODULUS = 0.1

F32 = jnp.float32
BF16 = jnp.bfloat16
VMEM = pl.BlockSpec(memory_space=pltpu.VMEM)
SMEM = pl.BlockSpec(memory_space=pltpu.SMEM)
HBM = pl.BlockSpec(memory_space=pltpu.HBM)


def halves(values):
    values = np.asarray(values, np.float32)
    high = values.astype(ml_dtypes.bfloat16)
    low = (values - high.astype(np.float32)).astype(ml_dtypes.bfloat16)
    return high, low


def right_table(values):
    high, low = halves(values)
    return np.block([[high, low], [high, np.zeros_like(low)]]).astype(ml_dtypes.bfloat16)


def left_table(values):
    high, low = halves(values)
    return np.concatenate([high, high, low], axis=1)


def tables(count_x):
    grid = np.arange(1, LENGTH + 1, dtype=np.float64)
    sine = np.sqrt(2.0 / (LENGTH + 1)) * np.sin(np.pi * np.outer(grid, grid) / (LENGTH + 1))
    eigen = 2.0 - 2.0 * np.cos(np.pi * grid / (LENGTH + 1))
    position = np.arange(LENGTH, dtype=np.float64)
    margin = 2 * INTERSECTION
    ramp = np.minimum(
        np.minimum((position + 0.5) / margin, (LENGTH - 0.5 - position) / margin), 1.0
    )
    rows = count_x * BRICK + 2 * PAD
    ramped = ramp[:, None] * sine
    along_y = np.zeros((LANES, LANES))
    back_y = np.zeros((LANES, LANES))
    for c in range(3):
        lane = c * WIDE + 1
        along_y[lane : lane + LENGTH, c * LENGTH : (c + 1) * LENGTH] = ramped
        back_y[c * LENGTH : (c + 1) * LENGTH, lane : lane + LENGTH] = sine
    along_x = np.zeros((count_x * LENGTH, rows))
    back_x = np.zeros((rows - 2 * INTERSECTION, count_x * LENGTH))
    for b in range(count_x):
        row = b * BRICK + PAD - INTERSECTION
        along_x[b * LENGTH : (b + 1) * LENGTH, row : row + LENGTH] = ramped.T
        back_x[b * BRICK : b * BRICK + LENGTH, b * LENGTH : (b + 1) * LENGTH] = sine
    half = LENGTH // 2
    eye = np.eye(8)
    even = left_table(np.kron(ramped[:half, 0::2].T, eye))
    odd = left_table(np.kron(ramped[:half, 1::2].T, eye))
    back_even = left_table(np.kron(sine[0::2, :half].T, eye))
    back_odd = left_table(np.kron(sine[1::2, :half].T, eye))
    ratio = lambda c, d: LAMBDA_RATIO if c == d else 1.0
    base = np.ones((count_x * LENGTH, LANES))
    steps = np.zeros((LENGTH, 8, LANES))
    order = np.concatenate([np.arange(0, LENGTH, 2), np.arange(1, LENGTH, 2)])
    for c in range(3):
        part = slice(c * LENGTH, (c + 1) * LENGTH)
        base[:, part] = REF_MODULUS * (
            ratio(c, 1) * eigen[None, :]
            + ratio(c, 2) * np.tile(eigen, count_x)[:, None]
            + SIGMA_SHIFT
        )
        steps[:, :, part] = REF_MODULUS * ratio(c, 0) * eigen[order][:, None, None]
    return [
        right_table(along_y),
        left_table(along_x),
        even,
        odd,
        back_even,
        back_odd,
        left_table(back_x),
        right_table(back_y),
        base.astype(np.float32),
        steps.astype(np.float32),
    ]


def phases(count):
    return 1 if count <= 2 else 2


def partners(count, phase):
    found = [i + 1 if (i + phase) % 2 == 0 else i - 1 for i in range(count)]
    return [j if 0 <= j < count else i for i, j in enumerate(found)]


def swap(value, mesh, moves, filler):
    names = mesh.axis_names
    shape = [mesh.shape[name] for name in names]
    found = {name: partners(mesh.shape[name], phase) for name, phase in moves.items()}
    spare = None if filler is None else partners(mesh.shape[filler], 0)
    pairs = []
    for place in np.ndindex(*shape):
        target = list(place)
        for name, other in found.items():
            target[names.index(name)] = other[place[names.index(name)]]
        if any(target[names.index(name)] == place[names.index(name)] for name in found):
            target = list(place)
            if filler is not None:
                target[names.index(filler)] = spare[place[names.index(filler)]]
        pairs.append(tuple(int(np.ravel_multi_index(at, shape)) for at in (place, target)))
    if filler is None and len(found) == 1:
        ((name, other),) = found.items()
        return lax.ppermute(value, name, list(enumerate(other)))
    return lax.ppermute(value, names, pairs)


def spots(shape):
    lane = lax.broadcasted_iota(jnp.int32, shape, len(shape) - 1)
    region = jnp.where(lane >= 3 * WIDE, 3, jnp.where(lane >= 2 * WIDE, 2, jnp.where(lane >= WIDE, 1, 0)))
    spot = jnp.where(region == 3, 4 * LANES, lane - region * WIDE)
    return spot, region


def turn(values, shift):
    return pltpu.roll(values, lax.rem(shift + 2 * LANES, LANES), values.ndim - 1)


def pack(planes, width, start, spot, groups):
    total = jnp.zeros(spot.shape, F32)
    for g, plane in enumerate(planes):
        inside = (spot >= g * width) & (spot < (g + 1) * width)
        total = jnp.where(inside, turn(plane, g * width - start), total)
    return total


def unpack(packed, g, width, start, spot, use):
    inside = (spot >= start) & (spot < start + width) & use
    return jnp.where(inside, turn(packed, start - g * width), 0.0)


def side(pos_ref, dim, phase, count):
    place = pos_ref[dim]
    up = lax.rem(place + phase, 2) == 0
    use = jnp.where(up, place < count - 1, place > 0)
    return up, use


def pick(up, high, low):
    return jnp.where(up, high, low)


def two_terms(values):
    high = values.astype(BF16)
    low = (values - high.astype(F32)).astype(BF16)
    return high, low


def right_product(values, table):
    high, low = two_terms(values)
    product = jnp.dot(jnp.concatenate([high, low], axis=1), table, preferred_element_type=F32)
    return product[:, :LANES] + product[:, LANES:]


def left_product(table, values):
    high, low = two_terms(values)
    return jnp.dot(
        table, jnp.concatenate([high, low, high], axis=0), preferred_element_type=F32
    )


def along(columns):
    return columns + 2 * INTERSECTION


def solve(source, mid, target, consts):
    spectrum(source, mid, consts)
    recover(mid, target, consts[6:8], lambda t: t)


def spectrum(source, mid, consts):
    along_y, along_x, even, odd, back_even, back_odd, back_x, back_y, base, steps = consts
    half = LENGTH // 2

    def forward(t, _):
        both = jnp.concatenate([source(2 * t), source(2 * t + 1)], axis=0)
        turned = right_product(both, along_y[...])
        height = both.shape[0] // 2
        pair = jnp.concatenate([turned[:height], turned[height:]], axis=1)
        done = left_product(along_x[...], pair)
        mid[2 * t] = done[:, :LANES]
        mid[2 * t + 1] = done[:, LANES:]
        return 0

    lax.fori_loop(0, half, forward, 0, unroll=10)

    def across(g, _):
        start = pl.multiple_of(g * 16, 16)

        def plane(z):
            return jnp.concatenate(
                [mid[z, pl.ds(start, 8), :], mid[z, pl.ds(start + 8, 8), :]], axis=1
            )

        planes = [plane(z) for z in range(LENGTH)]
        sums = jnp.concatenate([planes[z] + planes[LENGTH - 1 - z] for z in range(half)], axis=0)
        gaps = jnp.concatenate([planes[z] - planes[LENGTH - 1 - z] for z in range(half)], axis=0)
        ground = jnp.concatenate(
            [base[pl.ds(start, 8), :], base[pl.ds(start + 8, 8), :]], axis=1
        )

        def divisors(first):
            return jnp.concatenate(
                [
                    ground + jnp.concatenate([steps[first + k], steps[first + k]], axis=1)
                    for k in range(half)
                ],
                axis=0,
            )

        near = left_product(back_even[...], left_product(even[...], sums) / divisors(0))
        far = left_product(back_odd[...], left_product(odd[...], gaps) / divisors(half))
        lower = near + far
        upper = near - far
        for z in range(half):
            for h in range(2):
                lanes = slice(h * LANES, (h + 1) * LANES)
                mid[z, pl.ds(start + 8 * h, 8), :] = lower[8 * z : 8 * z + 8, lanes]
                mid[LENGTH - 1 - z, pl.ds(start + 8 * h, 8), :] = upper[8 * z : 8 * z + 8, lanes]
        return 0

    lax.fori_loop(0, mid.shape[1] // 16, across, 0, unroll=5)


def recover(mid, target, consts, where):
    back_x, back_y = consts
    rows = target.shape[1]

    def backward(t, _):
        at = where(t)
        pair = jnp.concatenate([mid[2 * at], mid[2 * at + 1]], axis=1)
        done = left_product(back_x[...], pair)
        both = jnp.concatenate([done[:, :LANES], done[:, LANES:]], axis=0)
        turned = right_product(both, back_y[...])
        target[2 * t] = turned[:rows]
        target[2 * t + 1] = turned[rows:]
        return 0

    lax.fori_loop(0, target.shape[0] // 2, backward, 0, unroll=10)


def write_messages(pos_ref, solved, width, counts, outs_y, outs_z, outs_yz):
    count, rows, _ = solved.shape
    spot, _ = spots((rows, LANES))
    lane = lax.broadcasted_iota(jnp.int32, (rows, LANES), 1)
    groups = WIDE // width
    _, count_y, count_z = counts
    for phase, out in enumerate(outs_z):
        up, _ = side(pos_ref, 0, phase, count_z)
        first = pick(up, count - width, 0)
        for i in range(width):
            out[i] = solved[first + i]
    for phase, out in enumerate(outs_y):
        up, _ = side(pos_ref, 1, phase, count_y)
        start = pick(up, WIDE - 1 - width, 1)
        many = count // groups

        def one(k, _, out=out, start=start, many=many):
            out[k] = pack(
                [solved[g * many + k] for g in range(groups)], width, start, spot, groups
            )
            return 0

        lax.fori_loop(0, many, one, 0, unroll=5)
    for number, out in enumerate(outs_yz):
        phase_y, phase_z = divmod(number, len(outs_z))
        up_y, _ = side(pos_ref, 1, phase_y, count_y)
        up_z, _ = side(pos_ref, 0, phase_z, count_z)
        start = pick(up_y, WIDE - 1 - width, 1)
        first = pick(up_z, count - width, 0)
        slots = LANES // width
        for k in range(out.shape[0]):
            total = jnp.zeros((rows, LANES), F32)
            for j in range(slots):
                i, c = divmod(k * slots + j, 3)
                if i < width:
                    inside = (lane >= j * width) & (lane < (j + 1) * width)
                    moved = turn(solved[first + i], j * width - c * WIDE - start)
                    total = jnp.where(inside, moved, total)
            out[k] = total


QUARTER = LENGTH // 4


def place_of(z, parts):
    if parts == 1:
        return 0, z
    if QUARTER <= z < LENGTH - QUARTER:
        return 1, z - QUARTER
    return 0, z if z < QUARTER else z - 2 * QUARTER


def planes_of(width):
    return range(FOLD - width, WIDE - FOLD + width)


def add_messages(pos_ref, solved, width, counts, ins_y, ins_z, ins_yz, window, put, get):
    height = solved[0].shape[1] if window is None else window.size
    rows = slice(None) if window is None else window
    spot, region = spots((height, LANES))
    groups = WIDE // width
    _, count_y, count_z = counts
    parts = len(solved)
    sides_y = [side(pos_ref, 1, phase, count_y) for phase in range(len(ins_y))]
    sides_z = [side(pos_ref, 0, phase, count_z) for phase in range(len(ins_z))]
    many = LENGTH // groups
    wanted = planes_of(width)
    for z in range(LENGTH):
        if z + 1 not in wanted:
            continue
        part, at = place_of(z, parts)
        g, k = divmod(z, many)
        total = solved[part][at, rows, :]
        for (up, use), ref in zip(sides_y, ins_y):
            start = pick(up, WIDE - FOLD, FOLD - width)
            total = total + unpack(ref[k, rows, :], g, width, start, spot, use)
        put(z + 1 - wanted[0], total)
    for plane in (0, WIDE - 1):
        if plane in wanted:
            put(plane - wanted[0], jnp.zeros((height, LANES), F32))
    for phase_z, ((up_z, use_z), ref_z) in enumerate(zip(sides_z, ins_z)):
        first = pick(up_z, WIDE - FOLD - wanted[0], 0)
        for i in range(width):
            total = ref_z[i, rows, :]
            for phase_y, (up_y, use_y) in enumerate(sides_y):
                ref = ins_yz[phase_y * len(ins_z) + phase_z]
                start = pick(up_y, WIDE - FOLD, FOLD - width)
                part = jnp.zeros((height, LANES), F32)
                for c in range(3):
                    k, j = divmod(3 * i + c, LANES // width)
                    moved = turn(ref[k, rows, :], start + c * WIDE - j * width)
                    part = jnp.where(region == c, moved, part)
                inside = (spot >= start) & (spot < start + width) & use_y
                total = total + jnp.where(inside, part, 0.0)
            put(first + i, get(first + i) + jnp.where(use_z, total, 0.0))


def grid_masks(pos_ref, rows, counts):
    count_x, count_y, count_z = counts
    spot, _ = spots((rows, LANES))
    row = lax.broadcasted_iota(jnp.int32, (rows, LANES), 0)
    low_y = pick(pos_ref[1] > 0, 0, REACH)
    high_y = pick(pos_ref[1] < count_y - 1, WIDE, REACH + BRICK)
    low_x = pick(pos_ref[2] > 0, 0, PAD)
    high_x = pick(pos_ref[2] < count_x - 1, rows, rows - PAD)
    inside = (spot >= low_y) & (spot < high_y) & (row >= low_x) & (row < high_x)
    low_z = pick(pos_ref[0] > 0, 0, REACH)
    high_z = pick(pos_ref[0] < count_z - 1, WIDE, REACH + BRICK)
    return inside, low_z, high_z


def from_sides(sides, refs, index):
    low = high = None
    for (up, use), ref in zip(sides, refs):
        value = index(ref)
        one = jnp.where(use & jnp.logical_not(up), value, 0.0)
        two = jnp.where(use & up, value, 0.0)
        low = one if low is None else low + one
        high = two if high is None else high + two
    return low, high


def complete(pos_ref, counts, partial, ins_x, ninth, field, first):
    rows = field.shape[1]
    inside, low_z, high_z = grid_masks(pos_ref, rows, counts)
    sides = [side(pos_ref, 2, phase, counts[0]) for phase in range(len(ins_x))]
    row = lax.broadcasted_iota(jnp.int32, (16, LANES), 0)
    blank = jnp.zeros((8, LANES), F32)

    def one(z, _):
        low, high = from_sides(sides, ins_x, lambda ref: ref[z])
        low = pltpu.roll(jnp.concatenate([low, blank], axis=0), 4, 0)
        high = pltpu.roll(jnp.concatenate([high, blank], axis=0), 4, 0)
        if ninth:
            at = z % 8
            under, over = from_sides(
                sides, ins_x, lambda ref: ref[NINTH + z // 8, at : at + 1, :]
            )
            low = jnp.where(row == 3, under, low)
            high = jnp.where(row == 12, over, high)
        on = inside & (z + first >= low_z) & (z + first < high_z)
        whole = jnp.concatenate(
            [
                partial[z, :16, :] + low,
                partial[z, 16 : rows - 16, :],
                partial[z, rows - 16 :, :] + high,
            ],
            axis=0,
        )
        field[z] = jnp.where(on, whole, 0.0)
        return 0

    if ninth:
        for z in range(field.shape[0]):
            one(z, 0)
    else:
        lax.fori_loop(0, field.shape[0], one, 0, unroll=2)


def widened(pos_ref, counts, modulus, beside, ins_x):
    rows = modulus.shape[1]
    sides = [side(pos_ref, 2, phase, counts[0]) for phase in range(len(ins_x))]
    _, region = spots((PAD, LANES))
    third = WIDE // 3

    def plane(z):
        c = z // third
        low, high = from_sides(sides, ins_x, lambda ref: ref[THIRD + z - c * third])
        edges = []
        for value in (low, high):
            total = turn(value, (2 * WIDE - c * WIDE))
            for target in (0, 1):
                total = jnp.where(region == target, turn(value, (target - c) * WIDE), total)
            edges.append(total)
        core = slice(PAD, rows - PAD)
        if beside is None:
            return jnp.concatenate([edges[0], modulus[z, core, :], edges[1]], axis=0), None
        low, high = (pltpu.roll(edge, LANES - 1, 1) for edge in edges)
        return (
            jnp.concatenate([edges[0], modulus[z, core, :], edges[1]], axis=0),
            jnp.concatenate([low, beside[z, core, :], high], axis=0),
        )

    return plane


def stiffness(field, modulus, first, last, shift, store, unroll):
    rows = field.shape[1]
    _, region = spots((rows, LANES))
    scale = [
        jnp.where(region == c, 0.5 * LAMBDA_RATIO, 0.5) for c in range(3)
    ]

    def one(z, carry):
        below, m, beside = carry
        v = field[z - shift]
        next_m, next_beside = modulus(z + 1)
        above = (m + next_m) * (field[z + 1 - shift] - v)
        gx = (m + pltpu.roll(m, rows - 1, 0)) * (pltpu.roll(v, rows - 1, 0) - v)
        beside = pltpu.roll(m, LANES - 1, 1) if beside is None else beside
        gy = (m + beside) * (pltpu.roll(v, LANES - 1, 1) - v)
        total = SIGMA_SHIFT * m * v + scale[0] * (below - above)
        total = total + scale[1] * (pltpu.roll(gy, 1, 1) - gy)
        total = total + scale[2] * (pltpu.roll(gx, 1, 0) - gx)
        store(z, total)
        return above, next_m, next_beside

    m, beside = modulus(first)
    below = (modulus(first - 1)[0] + m) * (field[first - shift] - field[first - 1 - shift])
    lax.fori_loop(first, last + 1, one, (below, m, beside), unroll=unroll)


def groups_of(refs, sizes):
    found = []
    at = 0
    for size in sizes:
        found.append(refs[at : at + size])
        at += size
    return found


def prepare_kernel(counts, sizes, pos_ref, table_in, load_in, labels_in, mask_in, *refs):
    (modulus_out,), outs_y, outs_z, outs_yz, fetched = groups_of(refs, (1,) + sizes[:3] + (5,))
    table_ref, labels, mask, load, arrived = fetched
    _, count_y, count_z = counts
    copies = [
        pltpu.make_async_copy(source, target, arrived.at[number])
        for number, (source, target) in enumerate(
            [(table_in, table_ref), (labels_in, labels), (mask_in, mask), (load_in, load)]
        )
    ]
    for copy in copies:
        copy.start()
    for copy in copies[:3]:
        copy.wait()

    def one(z, _):
        label = labels[z]
        looked = jnp.zeros(label.shape, F32)
        for k in range(table_ref.shape[0]):
            looked = jnp.where(label == k, table_ref[k], looked)
        modulus_out[z] = jnp.where(mask[z] == 1, looked, VOID_MODULUS)
        return 0

    lax.fori_loop(0, BRICK, one, 0, unroll=4)
    copies[3].wait()
    thin = INTERSECTION
    pairs = BRICK // 2

    def ends(plane, up, count):
        return jnp.where(up, plane[BRICK - count :, :], plane[:count, :])

    for phase, out in enumerate(outs_z):
        up, _ = side(pos_ref, 0, phase, count_z)
        first = pick(up, BRICK - thin, 0)
        for c in range(3):
            for i in range(thin):
                out[c * thin + i] = load[c, first + i]
        first = pick(up, BRICK - REACH, 0)
        for i in range(REACH):
            out[3 * thin + i] = modulus_out[first + i]
    for phase, out in enumerate(outs_y):
        up, _ = side(pos_ref, 1, phase, count_y)
        for c in range(4):
            for z in range(BRICK):
                plane = load[c, z] if c < 3 else modulus_out[z]
                row = z % 2 * thin
                out[c * pairs + z // 2, row : row + thin, :] = ends(plane, up, thin)
        for z in range(BRICK):
            plane = modulus_out[z]
            fifth = jnp.where(
                up, plane[BRICK - REACH : BRICK - thin, :], plane[thin:REACH, :]
            )
            out[4 * pairs + z // 8, z % 8 : z % 8 + 1, :] = fifth
    for number, out in enumerate(outs_yz):
        phase_y, phase_z = divmod(number, len(outs_z))
        up_y, _ = side(pos_ref, 1, phase_y, count_y)
        up_z, _ = side(pos_ref, 0, phase_z, count_z)
        first = pick(up_z, BRICK - thin, 0)
        for c in range(3):
            for i in range(thin):
                row = i % 2 * thin
                out[c * 2 + i // 2, row : row + thin, :] = ends(load[c, first + i], up_y, thin)
        first = pick(up_z, BRICK - REACH, 0)
        for i in range(REACH):
            out[6 + i] = ends(modulus_out[first + i], up_y, 8)


def gather_kernel(counts, sizes, pos_ref, load, *refs):
    ins_y, ins_z, ins_yz, (load_out,), outs_x, (wide,) = groups_of(
        refs, sizes[:3] + (1, sizes[3], 1)
    )
    columns = load.shape[3]
    rows = columns + 2 * PAD
    count_x, count_y, count_z = counts
    thin = INTERSECTION
    pairs = BRICK // 2
    sides_y = [side(pos_ref, 1, phase, count_y) for phase in range(len(ins_y))]
    sides_z = [side(pos_ref, 0, phase, count_z) for phase in range(len(ins_z))]
    blank = jnp.zeros((PAD, LANES), F32)

    def place(slot, c, centre, low, high):
        lane = c * WIDE + REACH
        wide[slot, lane : lane + BRICK, :] = centre
        wide[slot, lane - thin : lane, :] = low
        wide[slot, lane + BRICK : lane + BRICK + thin, :] = high

    def finish(z):
        load_out[z, :PAD, :] = blank
        load_out[z, PAD : PAD + columns, :] = wide[z].T
        load_out[z, rows - PAD :, :] = blank

    def clear(z, _):
        wide[z] = jnp.zeros((LANES, columns), F32)
        return 0

    lax.fori_loop(0, LENGTH, clear, 0, unroll=4)

    def pair(t, _):
        for h in range(2):
            z = 2 * t + h
            for c in range(3):
                low, high = from_sides(
                    sides_y, ins_y, lambda ref: ref[c * pairs + t, h * thin : (h + 1) * thin, :]
                )
                place(z + thin, c, load[c, z], low, high)
        for h in range(2):
            finish(2 * t + h + thin)
        return 0

    lax.fori_loop(0, pairs, pair, 0, unroll=2)
    for i in range(thin):
        row = i % 2 * thin
        for c in range(3):
            centre = from_sides(sides_z, ins_z, lambda ref: ref[c * thin + i])
            corner = [[], []]
            for phase_y in range(len(ins_y)):
                refs_z = ins_yz[phase_y * len(ins_z) : (phase_y + 1) * len(ins_z)]
                found = from_sides(
                    sides_z, refs_z, lambda ref: ref[c * 2 + i // 2, row : row + thin, :]
                )
                corner[0].append(found[0])
                corner[1].append(found[1])
            for which, slot in ((0, i), (1, thin + BRICK + i)):
                low, high = from_sides(sides_y, corner[which], lambda value: value)
                place(slot, c, centre[which], low, high)
        finish(i)
        finish(thin + BRICK + i)
    for phase, out in enumerate(outs_x):
        up, _ = side(pos_ref, 2, phase, count_x)
        start = pl.multiple_of(pick(up, rows - 2 * PAD, PAD), PAD)
        for z in range(LENGTH):
            out[z] = load_out[z, pl.ds(start, PAD), :]


def modulus_kernel(counts, sizes, pos_ref, modulus, *refs):
    ins_y, ins_z, ins_yz, (modulus_out, beside_out), (wide,) = groups_of(
        refs, sizes[:3] + (2, 1)
    )
    columns = modulus.shape[2]
    rows = columns + 2 * PAD
    count_x, count_y, count_z = counts
    thin = INTERSECTION
    pairs = BRICK // 2
    sides_y = [side(pos_ref, 1, phase, count_y) for phase in range(len(ins_y))]
    sides_z = [side(pos_ref, 0, phase, count_z) for phase in range(len(ins_z))]
    blank = jnp.zeros((PAD, LANES), F32)

    def finish(z, centre, low, high, low_end, high_end):
        for c in range(3):
            lane = c * WIDE + REACH
            wide[z, lane : lane + BRICK, :] = centre
            wide[z, lane - thin : lane, :] = low
            wide[z, lane + BRICK : lane + BRICK + thin, :] = high
            wide[z, lane - REACH : lane - thin, :] = low_end
            wide[z, lane + BRICK + thin : lane + BRICK + REACH, :] = high_end
        wide[z, 3 * WIDE :, :] = jnp.zeros((LANES - 3 * WIDE, columns), F32)
        modulus_out[z, :PAD, :] = blank
        turned = wide[z].T
        modulus_out[z, PAD : PAD + columns, :] = turned
        beside_out[z, :PAD, :] = blank
        beside_out[z, PAD : PAD + columns, :] = pltpu.roll(turned, LANES - 1, 1)
        beside_out[z, rows - PAD :, :] = blank
        modulus_out[z, rows - PAD :, :] = blank

    for z in range(BRICK):
        row = z % 2 * thin
        low, high = from_sides(
            sides_y, ins_y, lambda ref: ref[3 * pairs + z // 2, row : row + thin, :]
        )
        low_end, high_end = from_sides(
            sides_y, ins_y, lambda ref: ref[4 * pairs + z // 8, z % 8 : z % 8 + 1, :]
        )
        finish(z + REACH, modulus[z], low, high, low_end, high_end)
    for i in range(REACH):
        centre = from_sides(sides_z, ins_z, lambda ref: ref[3 * thin + i])
        corner = [[], []]
        for phase_y in range(len(ins_y)):
            refs_z = ins_yz[phase_y * len(ins_z) : (phase_y + 1) * len(ins_z)]
            found = from_sides(sides_z, refs_z, lambda ref: ref[6 + i])
            corner[0].append(found[0])
            corner[1].append(found[1])
        for which, slot in ((0, i), (1, REACH + BRICK + i)):
            low, high = from_sides(sides_y, corner[which], lambda value: value)
            finish(
                slot,
                centre[which],
                low[8 - thin :, :],
                high[:thin, :],
                low[8 - REACH : 8 - thin, :],
                high[thin:REACH, :],
            )


def patched(pos_ref, counts, residual, ins_x):
    rows = residual.shape[1]
    sides = [side(pos_ref, 2, phase, counts[0]) for phase in range(len(ins_x))]

    def plane(z):
        low, high = from_sides(sides, ins_x, lambda ref: ref[z])
        return jnp.concatenate([low, residual[z, PAD : rows - PAD, :], high], axis=0)

    return plane


def first_kernel(counts, sizes, pos_ref, residual, *refs):
    ins_x, consts, (outer, mid), outs_z, outs_yz = groups_of(
        refs, (sizes[3], 10, 2) + sizes[1:3]
    )
    spectrum(patched(pos_ref, counts, residual, ins_x), mid, consts)
    quarter = QUARTER // 2
    recover(mid, outer, consts[6:8], lambda t: jnp.where(t < quarter, t, t + 2 * quarter))
    write_messages(pos_ref, outer, FOLD, counts, [], outs_z, outs_yz)


def inner_kernel(counts, sizes, pos_ref, outer, mid, back_x, back_y, inner, *outs_y):
    recover(mid, inner, (back_x, back_y), lambda t: t + QUARTER // 2)
    spot, _ = spots(outer.shape[1:])
    groups = WIDE // FOLD
    many = LENGTH // groups
    for phase, out in enumerate(outs_y):
        up, _ = side(pos_ref, 1, phase, counts[1])
        start = pick(up, WIDE - 1 - FOLD, 1)
        for k in range(many):
            places = [place_of(g * many + k, 2) for g in range(groups)]
            planes = [(outer, inner)[part][at] for part, at in places]
            out[k] = pack(planes, FOLD, start, spot, groups)


NINTH = WIDE
THIRD = NINTH + -(-WIDE // 8)


def edge_kernel(width, counts, sizes, pos_ref, *refs):
    extra = 1 if width == FOLD else 0
    parts = 1 + extra
    solved, ins_y, ins_z, ins_yz, modulus, outs_x, scratch = groups_of(
        refs, (parts,) + sizes[:3] + (extra, sizes[3], extra)
    )
    rows = solved[0].shape[1]
    height = 16 if extra else 8
    _, region = spots((PAD, LANES))
    third = WIDE // 3
    for phase, out in enumerate(outs_x):
        up, _ = side(pos_ref, 2, phase, counts[0])
        window = pl.ds(pl.multiple_of(pick(up, rows - height, 0), 8), height)

        found = scratch[0] if extra else out

        def put(plane, value, found=found):
            found[plane] = value

        def get(plane, found=found):
            return found[plane]

        add_messages(pos_ref, solved, width, counts, ins_y, ins_z, ins_yz, window, put, get)
        if extra:
            for z in range(WIDE):
                outer = found[z]
                out[z] = jnp.where(up, outer[8:], outer[:8])
                ninth = jnp.where(up, outer[7:8], outer[8:9])
                out[NINTH + z // 8, z % 8 : z % 8 + 1, :] = ninth
        for ref in modulus:
            place = pl.ds(pl.multiple_of(pick(up, ref.shape[1] - 2 * PAD, PAD), PAD), PAD)
            for k in range(third):
                total = ref[k, place, :]
                for c in (1, 2):
                    total = jnp.where(region == c, ref[k + c * third, place, :], total)
                out[THIRD + k] = total


def fold_kernel(width, counts, sizes, pos_ref, *refs):
    parts = 2 if width == FOLD else 1
    solved, ins_y, ins_z, ins_yz, (field,) = groups_of(
        refs, (parts,) + sizes[:3] + (1,)
    )
    rows = solved[0].shape[1]
    thin = INTERSECTION
    core = slice(thin, thin + rows)
    blank = jnp.zeros((thin, LANES), F32)

    def put(plane, value):
        field[plane, core, :] = value

    def get(plane):
        return field[plane, core, :]

    for z in range(field.shape[0]):
        field[z, :thin, :] = blank
        field[z, thin + rows :, :] = blank
    add_messages(pos_ref, solved, width, counts, ins_y, ins_z, ins_yz, None, put, get)


def second_kernel(counts, sizes, pos_ref, partial, residual, modulus, *refs):
    (
        ins_load,
        ins_x,
        consts,
        (solved, field, renewed),
        outs_y,
        outs_z,
        outs_yz,
        (mid,),
    ) = groups_of(refs, (sizes[3], sizes[3], 10, 3) + sizes[:3] + (1,))
    rows = partial.shape[1]
    complete(pos_ref, counts, partial, ins_x, True, field, 0)
    inside, low_z, high_z = grid_masks(pos_ref, rows, counts)
    before = patched(pos_ref, counts, residual, ins_load)

    def store(z, product):
        on = inside & (z >= low_z) & (z < high_z)
        renewed[z - 1] = jnp.where(on, before(z - 1) - product, 0.0)

    stiffness(field, widened(pos_ref, counts, modulus, None, ins_x), 1, WIDE - 2, 0, store, 4)
    solve(lambda z: renewed[z], mid, solved, consts)
    write_messages(pos_ref, solved, REACH, counts, outs_y, outs_z, outs_yz)


def last_kernel(counts, sizes, pos_ref, partial, modulus, beside, moved, left, *refs):
    ins_x, ins_modulus, (displacement, residual), (field,) = groups_of(
        refs, (sizes[3], sizes[3], 2, 1)
    )
    rows = partial.shape[1]
    first = planes_of(REACH)[0]
    complete(pos_ref, counts, partial, ins_x, False, field, first)
    core = slice(PAD, rows - PAD)

    def store(z, product):
        at = z - REACH
        one = (moved[z, core, :] + field[z - first, core, :]).T
        two = (left[z - 1, core, :] - product[core]).T
        for c in range(3):
            lane = c * WIDE + REACH
            displacement[c, at] = one[lane : lane + BRICK, :]
            residual[c, at] = two[lane : lane + BRICK, :]

    stiffness(
        field,
        widened(pos_ref, counts, modulus, beside, ins_modulus),
        REACH,
        REACH + BRICK - 1,
        first,
        store,
        8,
    )


def call(kernel, inputs, outs, scratch=(), distant=0, limit=24, work=0):
    return pl.pallas_call(
        kernel,
        out_shape=[jax.ShapeDtypeStruct(shape, F32) for shape in outs],
        in_specs=[SMEM] + [HBM] * distant + [VMEM] * (len(inputs) - 1 - distant),
        out_specs=[VMEM] * len(outs),
        scratch_shapes=[
            pltpu.VMEM(shape, F32) if isinstance(shape, tuple) else shape for shape in scratch
        ],
        compiler_params=pltpu.CompilerParams(vmem_limit_bytes=limit * 1024 * 1024),
        cost_estimate=pl.CostEstimate(flops=work, bytes_accessed=work, transcendentals=0),
    )(*inputs)


def local(mesh, load, labels, mask, table):
    columns = load.shape[3]
    rows = columns + 2 * PAD
    counts = tuple(lax.axis_size(axis) for axis in ("gx", "gy", "gz"))
    ways = tuple(phases(count) for count in counts)
    sizes = (ways[1], ways[2], ways[1] * ways[2], ways[0])
    pos = jnp.stack([lax.axis_index(axis) for axis in ("gz", "gy", "gx")]).astype(jnp.int32)
    consts = [jnp.asarray(value) for value in tables(columns // BRICK)]
    spectral = (LENGTH, columns // BRICK * LENGTH, LANES)

    def exchange_yz(values, filler=None):
        y, z, yz = groups_of(values, (len(values) - sizes[1] - sizes[2],) + sizes[1:3])
        z = [swap(value, mesh, {"gz": phase}, filler) for phase, value in enumerate(z)]
        y = [swap(value, mesh, {"gy": n % ways[1]}, None) for n, value in enumerate(y)]
        yz = [
            swap(value, mesh, {"gy": number // ways[2], "gz": number % ways[2]}, filler)
            for number, value in enumerate(yz)
        ]
        return [*y, *z, *yz]

    def exchange_x(values, filler=None):
        return [swap(value, mesh, {"gx": phase}, filler) for phase, value in enumerate(values)]

    def message_shapes(width, height, count=LENGTH):
        groups = WIDE // width
        return (
            [(count // groups, height, LANES)] * sizes[0]
            + [(width, height, LANES)] * sizes[1]
            + [(-(-3 * width // (LANES // width)), height, LANES)] * sizes[2]
        )

    bind = lambda kernel, *first: functools.partial(kernel, *first, counts, sizes)
    thick = along(columns)
    thin = (LENGTH, thick, LANES)
    tall = (LENGTH, rows, LANES)
    wide = (WIDE, rows, LANES)
    near = len(planes_of(REACH))

    modulus_core, *out = call(
        bind(prepare_kernel),
        [pos, table, load, labels, mask],
        [(BRICK, BRICK, columns)]
        + [(2 * BRICK + BRICK // 8, 8, columns)] * sizes[0]
        + [(3 * INTERSECTION + REACH, BRICK, columns)] * sizes[1]
        + [(6 + REACH, 8, columns)] * sizes[2],
        [
            pltpu.SMEM(table.shape, F32),
            pltpu.VMEM(labels.shape, jnp.int32),
            pltpu.VMEM(mask.shape, jnp.int32),
            pltpu.VMEM(load.shape, F32),
            pltpu.SemaphoreType.DMA((4,)),
        ],
        distant=4,
        limit=61,
    )
    margins = exchange_yz(out, "gx")
    residual, *out = call(
        bind(gather_kernel),
        [pos, load, *margins],
        [tall] + [(LENGTH, PAD, LANES)] * sizes[3],
        [(LENGTH, LANES, columns)],
    )
    from_x = exchange_x(out)
    modulus, beside = call(
        bind(modulus_kernel),
        [pos, modulus_core, *margins],
        [wide, wide],
        [(WIDE, LANES, columns)],
        work=8000000,
    )
    part = (LENGTH // 2, thick, LANES)
    first_shapes = message_shapes(FOLD, thick)
    outer, mid, *out = call(
        bind(first_kernel), [pos, residual, *from_x, *consts], [part, spectral] + first_shapes[sizes[0] :]
    )
    inner, *late = call(
        bind(inner_kernel),
        [pos, outer, mid, *consts[6:8]],
        [part] + first_shapes[: sizes[0]],
        work=8000000,
    )
    solved = [outer, inner]
    margins = exchange_yz([*late, *out])
    first_edges = exchange_x(
        call(
            bind(edge_kernel, FOLD),
            [pos, *solved, *margins, modulus],
            [(THIRD + WIDE // 3, 8, LANES)] * sizes[3],
            [(WIDE, 16, LANES)],
        )
    )
    (partial,) = call(
        bind(fold_kernel, FOLD), [pos, *solved, *margins], [wide], work=8000000
    )
    solved, moved, left, *out = call(
        bind(second_kernel),
        [pos, partial, residual, modulus, *from_x, *first_edges, *consts],
        [thin, wide, tall] + message_shapes(REACH, thick),
        [spectral],
        limit=32,
    )
    margins = exchange_yz(out)
    edges = exchange_x(
        call(
            bind(edge_kernel, REACH), [pos, solved, *margins], [(near, 8, LANES)] * sizes[3]
        ),
        "gy",
    )
    (partial,) = call(
        bind(fold_kernel, REACH), [pos, solved, *margins], [(near, rows, LANES)], work=8000000
    )
    displacement, residual = call(
        bind(last_kernel),
        [pos, partial, modulus, beside, moved, left, *edges, *first_edges],
        [load.shape, load.shape],
        [(near, rows, LANES)],
        limit=32,
    )
    return displacement, residual


def solution(mesh):
    placed = (P(None, "gz", "gy", "gx"), P("gz", "gy", "gx"), P("gz", "gy", "gx"), P())
    return jax.shard_map(
        functools.partial(local, mesh),
        mesh=mesh,
        in_specs=placed,
        out_specs=(P(None, "gz", "gy", "gx"), P(None, "gz", "gy", "gx")),
        check_vma=False,
    )
```

```python
import functools

import jax
import jax.numpy as jnp
import ml_dtypes
import numpy as np
from jax import lax
from jax.experimental import pallas as pl
from jax.experimental.pallas import tpu as pltpu
from jax.sharding import PartitionSpec as P

BRICK = 32
INTERSECTION = 4
LENGTH = BRICK + 2 * INTERSECTION
REACH = INTERSECTION + 1
WIDE = BRICK + 2 * REACH
LANES = 128
PAD = 8
FOLD = 2 * INTERSECTION + 1

LAMBDA_RATIO = 2.0
SIGMA_SHIFT = 0.1
REF_MODULUS = 1.5
VOID_MODULUS = 0.1

F32 = jnp.float32
BF16 = jnp.bfloat16
VMEM = pl.BlockSpec(memory_space=pltpu.VMEM)
SMEM = pl.BlockSpec(memory_space=pltpu.SMEM)
HBM = pl.BlockSpec(memory_space=pltpu.HBM)


def halves(values):
    values = np.asarray(values, np.float32)
    high = values.astype(ml_dtypes.bfloat16)
    low = (values - high.astype(np.float32)).astype(ml_dtypes.bfloat16)
    return high, low


def right_table(values):
    high, low = halves(values)
    return np.block([[high, low], [high, np.zeros_like(low)]]).astype(ml_dtypes.bfloat16)


def left_table(values):
    high, low = halves(values)
    return np.concatenate([high, high, low], axis=1)


def tables(count_x):
    grid = np.arange(1, LENGTH + 1, dtype=np.float64)
    sine = np.sqrt(2.0 / (LENGTH + 1)) * np.sin(np.pi * np.outer(grid, grid) / (LENGTH + 1))
    eigen = 2.0 - 2.0 * np.cos(np.pi * grid / (LENGTH + 1))
    position = np.arange(LENGTH, dtype=np.float64)
    margin = 2 * INTERSECTION
    ramp = np.minimum(
        np.minimum((position + 0.5) / margin, (LENGTH - 0.5 - position) / margin), 1.0
    )
    rows = count_x * BRICK + 2 * PAD
    ramped = ramp[:, None] * sine
    along_y = np.zeros((LANES, LANES))
    back_y = np.zeros((LANES, LANES))
    for c in range(3):
        lane = c * WIDE + 1
        along_y[lane : lane + LENGTH, c * LENGTH : (c + 1) * LENGTH] = ramped
        back_y[c * LENGTH : (c + 1) * LENGTH, lane : lane + LENGTH] = sine
    along_x = np.zeros((count_x * LENGTH, rows))
    back_x = np.zeros((rows - 2 * INTERSECTION, count_x * LENGTH))
    for b in range(count_x):
        row = b * BRICK + PAD - INTERSECTION
        along_x[b * LENGTH : (b + 1) * LENGTH, row : row + LENGTH] = ramped.T
        back_x[b * BRICK : b * BRICK + LENGTH, b * LENGTH : (b + 1) * LENGTH] = sine
    half = LENGTH // 2
    eye = np.eye(8)
    even = left_table(np.kron(ramped[:half, 0::2].T, eye))
    odd = left_table(np.kron(ramped[:half, 1::2].T, eye))
    back_even = left_table(np.kron(sine[0::2, :half].T, eye))
    back_odd = left_table(np.kron(sine[1::2, :half].T, eye))
    ratio = lambda c, d: LAMBDA_RATIO if c == d else 1.0
    base = np.ones((count_x * LENGTH, LANES))
    steps = np.zeros((LENGTH, 8, LANES))
    order = np.concatenate([np.arange(0, LENGTH, 2), np.arange(1, LENGTH, 2)])
    for c in range(3):
        part = slice(c * LENGTH, (c + 1) * LENGTH)
        base[:, part] = REF_MODULUS * (
            ratio(c, 1) * eigen[None, :]
            + ratio(c, 2) * np.tile(eigen, count_x)[:, None]
            + SIGMA_SHIFT
        )
        steps[:, :, part] = REF_MODULUS * ratio(c, 0) * eigen[order][:, None, None]
    return [
        right_table(along_y),
        left_table(along_x),
        even,
        odd,
        back_even,
        back_odd,
        left_table(back_x),
        right_table(back_y),
        base.astype(np.float32),
        steps.astype(np.float32),
    ]


def phases(count):
    return 1 if count <= 2 else 2


def partners(count, phase):
    found = [i + 1 if (i + phase) % 2 == 0 else i - 1 for i in range(count)]
    return [j if 0 <= j < count else i for i, j in enumerate(found)]


def swap(value, mesh, moves, filler):
    names = mesh.axis_names
    shape = [mesh.shape[name] for name in names]
    found = {name: partners(mesh.shape[name], phase) for name, phase in moves.items()}
    spare = None if filler is None else partners(mesh.shape[filler], 0)
    pairs = []
    for place in np.ndindex(*shape):
        target = list(place)
        for name, other in found.items():
            target[names.index(name)] = other[place[names.index(name)]]
        if any(target[names.index(name)] == place[names.index(name)] for name in found):
            target = list(place)
            if filler is not None:
                target[names.index(filler)] = spare[place[names.index(filler)]]
        pairs.append(tuple(int(np.ravel_multi_index(at, shape)) for at in (place, target)))
    if filler is None and len(found) == 1:
        ((name, other),) = found.items()
        return lax.ppermute(value, name, list(enumerate(other)))
    return lax.ppermute(value, names, pairs)


def spots(shape):
    lane = lax.broadcasted_iota(jnp.int32, shape, len(shape) - 1)
    region = jnp.where(lane >= 3 * WIDE, 3, jnp.where(lane >= 2 * WIDE, 2, jnp.where(lane >= WIDE, 1, 0)))
    spot = jnp.where(region == 3, 4 * LANES, lane - region * WIDE)
    return spot, region


def turn(values, shift):
    return pltpu.roll(values, lax.rem(shift + 2 * LANES, LANES), values.ndim - 1)


def pack(planes, width, start, spot, groups):
    total = jnp.zeros(spot.shape, F32)
    for g, plane in enumerate(planes):
        inside = (spot >= g * width) & (spot < (g + 1) * width)
        total = jnp.where(inside, turn(plane, g * width - start), total)
    return total


def unpack(packed, g, width, start, spot, use):
    inside = (spot >= start) & (spot < start + width) & use
    return jnp.where(inside, turn(packed, start - g * width), 0.0)


def side(pos_ref, dim, phase, count):
    place = pos_ref[dim]
    up = lax.rem(place + phase, 2) == 0
    use = jnp.where(up, place < count - 1, place > 0)
    return up, use


def pick(up, high, low):
    return jnp.where(up, high, low)


def two_terms(values):
    high = values.astype(BF16)
    low = (values - high.astype(F32)).astype(BF16)
    return high, low


def right_product(values, table):
    high, low = two_terms(values)
    product = jnp.dot(jnp.concatenate([high, low], axis=1), table, preferred_element_type=F32)
    return product[:, :LANES] + product[:, LANES:]


def left_product(table, values):
    high, low = two_terms(values)
    return jnp.dot(
        table, jnp.concatenate([high, low, high], axis=0), preferred_element_type=F32
    )


def along(columns):
    return columns + 2 * INTERSECTION


def solve(source, mid, target, consts):
    spectrum(source, mid, consts)
    recover(mid, target, consts[6:8], lambda t: t)


def spectrum(source, mid, consts):
    along_y, along_x, even, odd, back_even, back_odd, back_x, back_y, base, steps = consts
    half = LENGTH // 2

    def forward(t, _):
        both = jnp.concatenate([source(2 * t), source(2 * t + 1)], axis=0)
        turned = right_product(both, along_y[...])
        height = both.shape[0] // 2
        pair = jnp.concatenate([turned[:height], turned[height:]], axis=1)
        done = left_product(along_x[...], pair)
        mid[2 * t] = done[:, :LANES]
        mid[2 * t + 1] = done[:, LANES:]
        return 0

    lax.fori_loop(0, half, forward, 0, unroll=10)

    def across(g, _):
        start = pl.multiple_of(g * 16, 16)

        def plane(z):
            return jnp.concatenate(
                [mid[z, pl.ds(start, 8), :], mid[z, pl.ds(start + 8, 8), :]], axis=1
            )

        planes = [plane(z) for z in range(LENGTH)]
        sums = jnp.concatenate([planes[z] + planes[LENGTH - 1 - z] for z in range(half)], axis=0)
        gaps = jnp.concatenate([planes[z] - planes[LENGTH - 1 - z] for z in range(half)], axis=0)
        ground = jnp.concatenate(
            [base[pl.ds(start, 8), :], base[pl.ds(start + 8, 8), :]], axis=1
        )

        def divisors(first):
            return jnp.concatenate(
                [
                    ground + jnp.concatenate([steps[first + k], steps[first + k]], axis=1)
                    for k in range(half)
                ],
                axis=0,
            )

        near = left_product(back_even[...], left_product(even[...], sums) / divisors(0))
        far = left_product(back_odd[...], left_product(odd[...], gaps) / divisors(half))
        lower = near + far
        upper = near - far
        for z in range(half):
            for h in range(2):
                lanes = slice(h * LANES, (h + 1) * LANES)
                mid[z, pl.ds(start + 8 * h, 8), :] = lower[8 * z : 8 * z + 8, lanes]
                mid[LENGTH - 1 - z, pl.ds(start + 8 * h, 8), :] = upper[8 * z : 8 * z + 8, lanes]
        return 0

    lax.fori_loop(0, mid.shape[1] // 16, across, 0, unroll=5)


def recover(mid, target, consts, where):
    back_x, back_y = consts
    rows = target.shape[1]

    def backward(t, _):
        at = where(t)
        pair = jnp.concatenate([mid[2 * at], mid[2 * at + 1]], axis=1)
        done = left_product(back_x[...], pair)
        both = jnp.concatenate([done[:, :LANES], done[:, LANES:]], axis=0)
        turned = right_product(both, back_y[...])
        target[2 * t] = turned[:rows]
        target[2 * t + 1] = turned[rows:]
        return 0

    lax.fori_loop(0, target.shape[0] // 2, backward, 0, unroll=10)


def write_messages(pos_ref, solved, width, counts, outs_y, outs_z, outs_yz):
    count, rows, _ = solved.shape
    spot, _ = spots((rows, LANES))
    lane = lax.broadcasted_iota(jnp.int32, (rows, LANES), 1)
    groups = WIDE // width
    _, count_y, count_z = counts
    for phase, out in enumerate(outs_z):
        up, _ = side(pos_ref, 0, phase, count_z)
        first = pick(up, count - width, 0)
        for i in range(width):
            out[i] = solved[first + i]
    for phase, out in enumerate(outs_y):
        up, _ = side(pos_ref, 1, phase, count_y)
        start = pick(up, WIDE - 1 - width, 1)
        many = count // groups

        def one(k, _, out=out, start=start, many=many):
            out[k] = pack(
                [solved[g * many + k] for g in range(groups)], width, start, spot, groups
            )
            return 0

        lax.fori_loop(0, many, one, 0, unroll=5)
    for number, out in enumerate(outs_yz):
        phase_y, phase_z = divmod(number, len(outs_z))
        up_y, _ = side(pos_ref, 1, phase_y, count_y)
        up_z, _ = side(pos_ref, 0, phase_z, count_z)
        start = pick(up_y, WIDE - 1 - width, 1)
        first = pick(up_z, count - width, 0)
        slots = LANES // width
        for k in range(out.shape[0]):
            total = jnp.zeros((rows, LANES), F32)
            for j in range(slots):
                i, c = divmod(k * slots + j, 3)
                if i < width:
                    inside = (lane >= j * width) & (lane < (j + 1) * width)
                    moved = turn(solved[first + i], j * width - c * WIDE - start)
                    total = jnp.where(inside, moved, total)
            out[k] = total


QUARTER = LENGTH // 4


def place_of(z, parts):
    if parts == 1:
        return 0, z
    if QUARTER <= z < LENGTH - QUARTER:
        return 1, z - QUARTER
    return 0, z if z < QUARTER else z - 2 * QUARTER


def planes_of(width):
    return range(FOLD - width, WIDE - FOLD + width)


def add_messages(pos_ref, solved, width, counts, ins_y, ins_z, ins_yz, window, put, get):
    height = solved[0].shape[1] if window is None else window.size
    rows = slice(None) if window is None else window
    spot, region = spots((height, LANES))
    groups = WIDE // width
    _, count_y, count_z = counts
    parts = len(solved)
    sides_y = [side(pos_ref, 1, phase, count_y) for phase in range(len(ins_y))]
    sides_z = [side(pos_ref, 0, phase, count_z) for phase in range(len(ins_z))]
    many = LENGTH // groups
    wanted = planes_of(width)
    for z in range(LENGTH):
        if z + 1 not in wanted:
            continue
        part, at = place_of(z, parts)
        g, k = divmod(z, many)
        total = solved[part][at, rows, :]
        for (up, use), ref in zip(sides_y, ins_y):
            start = pick(up, WIDE - FOLD, FOLD - width)
            total = total + unpack(ref[k, rows, :], g, width, start, spot, use)
        put(z + 1 - wanted[0], total)
    for plane in (0, WIDE - 1):
        if plane in wanted:
            put(plane - wanted[0], jnp.zeros((height, LANES), F32))
    for phase_z, ((up_z, use_z), ref_z) in enumerate(zip(sides_z, ins_z)):
        first = pick(up_z, WIDE - FOLD - wanted[0], 0)
        for i in range(width):
            total = ref_z[i, rows, :]
            for phase_y, (up_y, use_y) in enumerate(sides_y):
                ref = ins_yz[phase_y * len(ins_z) + phase_z]
                start = pick(up_y, WIDE - FOLD, FOLD - width)
                part = jnp.zeros((height, LANES), F32)
                for c in range(3):
                    k, j = divmod(3 * i + c, LANES // width)
                    moved = turn(ref[k, rows, :], start + c * WIDE - j * width)
                    part = jnp.where(region == c, moved, part)
                inside = (spot >= start) & (spot < start + width) & use_y
                total = total + jnp.where(inside, part, 0.0)
            put(first + i, get(first + i) + jnp.where(use_z, total, 0.0))


def grid_masks(pos_ref, rows, counts):
    count_x, count_y, count_z = counts
    spot, _ = spots((rows, LANES))
    row = lax.broadcasted_iota(jnp.int32, (rows, LANES), 0)
    low_y = pick(pos_ref[1] > 0, 0, REACH)
    high_y = pick(pos_ref[1] < count_y - 1, WIDE, REACH + BRICK)
    low_x = pick(pos_ref[2] > 0, 0, PAD)
    high_x = pick(pos_ref[2] < count_x - 1, rows, rows - PAD)
    inside = (spot >= low_y) & (spot < high_y) & (row >= low_x) & (row < high_x)
    low_z = pick(pos_ref[0] > 0, 0, REACH)
    high_z = pick(pos_ref[0] < count_z - 1, WIDE, REACH + BRICK)
    return inside, low_z, high_z


def from_sides(sides, refs, index):
    low = high = None
    for (up, use), ref in zip(sides, refs):
        value = index(ref)
        one = jnp.where(use & jnp.logical_not(up), value, 0.0)
        two = jnp.where(use & up, value, 0.0)
        low = one if low is None else low + one
        high = two if high is None else high + two
    return low, high


def complete(pos_ref, counts, partial, ins_x, ninth, field, first):
    rows = field.shape[1]
    inside, low_z, high_z = grid_masks(pos_ref, rows, counts)
    sides = [side(pos_ref, 2, phase, counts[0]) for phase in range(len(ins_x))]
    row = lax.broadcasted_iota(jnp.int32, (16, LANES), 0)
    blank = jnp.zeros((8, LANES), F32)

    def one(z, _):
        low, high = from_sides(sides, ins_x, lambda ref: ref[z])
        low = pltpu.roll(jnp.concatenate([low, blank], axis=0), 4, 0)
        high = pltpu.roll(jnp.concatenate([high, blank], axis=0), 4, 0)
        if ninth:
            at = z % 8
            under, over = from_sides(
                sides, ins_x, lambda ref: ref[NINTH + z // 8, at : at + 1, :]
            )
            low = jnp.where(row == 3, under, low)
            high = jnp.where(row == 12, over, high)
        on = inside & (z + first >= low_z) & (z + first < high_z)
        whole = jnp.concatenate(
            [
                partial[z, :16, :] + low,
                partial[z, 16 : rows - 16, :],
                partial[z, rows - 16 :, :] + high,
            ],
            axis=0,
        )
        field[z] = jnp.where(on, whole, 0.0)
        return 0

    if ninth:
        for z in range(field.shape[0]):
            one(z, 0)
    else:
        for z in range(field.shape[0]):
            one(z, 0)


def widened(pos_ref, counts, modulus, beside, ins_x):
    rows = modulus.shape[1]
    sides = [side(pos_ref, 2, phase, counts[0]) for phase in range(len(ins_x))]
    _, region = spots((PAD, LANES))
    third = WIDE // 3

    def plane(z):
        c = z // third
        low, high = from_sides(sides, ins_x, lambda ref: ref[THIRD + z - c * third])
        edges = []
        for value in (low, high):
            total = turn(value, (2 * WIDE - c * WIDE))
            for target in (0, 1):
                total = jnp.where(region == target, turn(value, (target - c) * WIDE), total)
            edges.append(total)
        core = slice(PAD, rows - PAD)
        if beside is None:
            return jnp.concatenate([edges[0], modulus[z, core, :], edges[1]], axis=0), None
        low, high = (pltpu.roll(edge, LANES - 1, 1) for edge in edges)
        return (
            jnp.concatenate([edges[0], modulus[z, core, :], edges[1]], axis=0),
            jnp.concatenate([low, beside[z, core, :], high], axis=0),
        )

    return plane


def stiffness(field, modulus, first, last, shift, store, unroll):
    rows = field.shape[1]
    _, region = spots((rows, LANES))
    scale = [
        jnp.where(region == c, 0.5 * LAMBDA_RATIO, 0.5) for c in range(3)
    ]

    def one(z, carry):
        below, m, beside = carry
        v = field[z - shift]
        next_m, next_beside = modulus(z + 1)
        above = (m + next_m) * (field[z + 1 - shift] - v)
        gx = (m + pltpu.roll(m, rows - 1, 0)) * (pltpu.roll(v, rows - 1, 0) - v)
        beside = pltpu.roll(m, LANES - 1, 1) if beside is None else beside
        gy = (m + beside) * (pltpu.roll(v, LANES - 1, 1) - v)
        total = SIGMA_SHIFT * m * v + scale[0] * (below - above)
        total = total + scale[1] * (pltpu.roll(gy, 1, 1) - gy)
        total = total + scale[2] * (pltpu.roll(gx, 1, 0) - gx)
        store(z, total)
        return above, next_m, next_beside

    m, beside = modulus(first)
    below = (modulus(first - 1)[0] + m) * (field[first - shift] - field[first - 1 - shift])
    lax.fori_loop(first, last + 1, one, (below, m, beside), unroll=unroll)


def groups_of(refs, sizes):
    found = []
    at = 0
    for size in sizes:
        found.append(refs[at : at + size])
        at += size
    return found


def prepare_kernel(counts, sizes, pos_ref, table_in, load_in, labels_in, mask_in, *refs):
    (modulus_out,), outs_y, outs_z, outs_yz, fetched = groups_of(refs, (1,) + sizes[:3] + (5,))
    table_ref, labels, mask, load, arrived = fetched
    _, count_y, count_z = counts
    copies = [
        pltpu.make_async_copy(source, target, arrived.at[number])
        for number, (source, target) in enumerate(
            [(table_in, table_ref), (labels_in, labels), (mask_in, mask), (load_in, load)]
        )
    ]
    for copy in copies:
        copy.start()
    for copy in copies[:3]:
        copy.wait()

    def one(z, _):
        label = labels[z]
        looked = jnp.zeros(label.shape, F32)
        for k in range(table_ref.shape[0]):
            looked = jnp.where(label == k, table_ref[k], looked)
        modulus_out[z] = jnp.where(mask[z] == 1, looked, VOID_MODULUS)
        return 0

    lax.fori_loop(0, BRICK, one, 0, unroll=4)
    copies[3].wait()
    thin = INTERSECTION
    pairs = BRICK // 2

    def ends(plane, up, count):
        return jnp.where(up, plane[BRICK - count :, :], plane[:count, :])

    for phase, out in enumerate(outs_z):
        up, _ = side(pos_ref, 0, phase, count_z)
        first = pick(up, BRICK - thin, 0)
        for c in range(3):
            for i in range(thin):
                out[c * thin + i] = load[c, first + i]
        first = pick(up, BRICK - REACH, 0)
        for i in range(REACH):
            out[3 * thin + i] = modulus_out[first + i]
    for phase, out in enumerate(outs_y):
        up, _ = side(pos_ref, 1, phase, count_y)
        for c in range(4):
            for z in range(BRICK):
                plane = load[c, z] if c < 3 else modulus_out[z]
                row = z % 2 * thin
                out[c * pairs + z // 2, row : row + thin, :] = ends(plane, up, thin)
        for z in range(BRICK):
            plane = modulus_out[z]
            fifth = jnp.where(
                up, plane[BRICK - REACH : BRICK - thin, :], plane[thin:REACH, :]
            )
            out[4 * pairs + z // 8, z % 8 : z % 8 + 1, :] = fifth
    for number, out in enumerate(outs_yz):
        phase_y, phase_z = divmod(number, len(outs_z))
        up_y, _ = side(pos_ref, 1, phase_y, count_y)
        up_z, _ = side(pos_ref, 0, phase_z, count_z)
        first = pick(up_z, BRICK - thin, 0)
        for c in range(3):
            for i in range(thin):
                row = i % 2 * thin
                out[c * 2 + i // 2, row : row + thin, :] = ends(load[c, first + i], up_y, thin)
        first = pick(up_z, BRICK - REACH, 0)
        for i in range(REACH):
            out[6 + i] = ends(modulus_out[first + i], up_y, 8)


def gather_kernel(counts, sizes, pos_ref, load, *refs):
    ins_y, ins_z, ins_yz, (load_out,), outs_x, (wide,) = groups_of(
        refs, sizes[:3] + (1, sizes[3], 1)
    )
    columns = load.shape[3]
    rows = columns + 2 * PAD
    count_x, count_y, count_z = counts
    thin = INTERSECTION
    pairs = BRICK // 2
    sides_y = [side(pos_ref, 1, phase, count_y) for phase in range(len(ins_y))]
    sides_z = [side(pos_ref, 0, phase, count_z) for phase in range(len(ins_z))]
    blank = jnp.zeros((PAD, LANES), F32)

    def place(slot, c, centre, low, high):
        lane = c * WIDE + REACH
        wide[slot, lane : lane + BRICK, :] = centre
        wide[slot, lane - thin : lane, :] = low
        wide[slot, lane + BRICK : lane + BRICK + thin, :] = high

    def finish(z):
        load_out[z, :PAD, :] = blank
        load_out[z, PAD : PAD + columns, :] = wide[z].T
        load_out[z, rows - PAD :, :] = blank

    def clear(z, _):
        wide[z] = jnp.zeros((LANES, columns), F32)
        return 0

    lax.fori_loop(0, LENGTH, clear, 0, unroll=4)

    def pair(t, _):
        for h in range(2):
            z = 2 * t + h
            for c in range(3):
                low, high = from_sides(
                    sides_y, ins_y, lambda ref: ref[c * pairs + t, h * thin : (h + 1) * thin, :]
                )
                place(z + thin, c, load[c, z], low, high)
        for h in range(2):
            finish(2 * t + h + thin)
        return 0

    lax.fori_loop(0, pairs, pair, 0, unroll=4)
    for i in range(thin):
        row = i % 2 * thin
        for c in range(3):
            centre = from_sides(sides_z, ins_z, lambda ref: ref[c * thin + i])
            corner = [[], []]
            for phase_y in range(len(ins_y)):
                refs_z = ins_yz[phase_y * len(ins_z) : (phase_y + 1) * len(ins_z)]
                found = from_sides(
                    sides_z, refs_z, lambda ref: ref[c * 2 + i // 2, row : row + thin, :]
                )
                corner[0].append(found[0])
                corner[1].append(found[1])
            for which, slot in ((0, i), (1, thin + BRICK + i)):
                low, high = from_sides(sides_y, corner[which], lambda value: value)
                place(slot, c, centre[which], low, high)
        finish(i)
        finish(thin + BRICK + i)
    for phase, out in enumerate(outs_x):
        up, _ = side(pos_ref, 2, phase, count_x)
        start = pl.multiple_of(pick(up, rows - 2 * PAD, PAD), PAD)
        for z in range(LENGTH):
            out[z] = load_out[z, pl.ds(start, PAD), :]


def modulus_kernel(counts, sizes, pos_ref, modulus, *refs):
    ins_y, ins_z, ins_yz, (modulus_out, beside_out), (wide,) = groups_of(
        refs, sizes[:3] + (2, 1)
    )
    columns = modulus.shape[2]
    rows = columns + 2 * PAD
    count_x, count_y, count_z = counts
    thin = INTERSECTION
    pairs = BRICK // 2
    sides_y = [side(pos_ref, 1, phase, count_y) for phase in range(len(ins_y))]
    sides_z = [side(pos_ref, 0, phase, count_z) for phase in range(len(ins_z))]
    blank = jnp.zeros((PAD, LANES), F32)

    def finish(z, centre, low, high, low_end, high_end):
        for c in range(3):
            lane = c * WIDE + REACH
            wide[z, lane : lane + BRICK, :] = centre
            wide[z, lane - thin : lane, :] = low
            wide[z, lane + BRICK : lane + BRICK + thin, :] = high
            wide[z, lane - REACH : lane - thin, :] = low_end
            wide[z, lane + BRICK + thin : lane + BRICK + REACH, :] = high_end
        wide[z, 3 * WIDE :, :] = jnp.zeros((LANES - 3 * WIDE, columns), F32)
        modulus_out[z, :PAD, :] = blank
        turned = wide[z].T
        modulus_out[z, PAD : PAD + columns, :] = turned
        beside_out[z, :PAD, :] = blank
        beside_out[z, PAD : PAD + columns, :] = pltpu.roll(turned, LANES - 1, 1)
        beside_out[z, rows - PAD :, :] = blank
        modulus_out[z, rows - PAD :, :] = blank

    for z in range(BRICK):
        row = z % 2 * thin
        low, high = from_sides(
            sides_y, ins_y, lambda ref: ref[3 * pairs + z // 2, row : row + thin, :]
        )
        low_end, high_end = from_sides(
            sides_y, ins_y, lambda ref: ref[4 * pairs + z // 8, z % 8 : z % 8 + 1, :]
        )
        finish(z + REACH, modulus[z], low, high, low_end, high_end)
    for i in range(REACH):
        centre = from_sides(sides_z, ins_z, lambda ref: ref[3 * thin + i])
        corner = [[], []]
        for phase_y in range(len(ins_y)):
            refs_z = ins_yz[phase_y * len(ins_z) : (phase_y + 1) * len(ins_z)]
            found = from_sides(sides_z, refs_z, lambda ref: ref[6 + i])
            corner[0].append(found[0])
            corner[1].append(found[1])
        for which, slot in ((0, i), (1, REACH + BRICK + i)):
            low, high = from_sides(sides_y, corner[which], lambda value: value)
            finish(
                slot,
                centre[which],
                low[8 - thin :, :],
                high[:thin, :],
                low[8 - REACH : 8 - thin, :],
                high[thin:REACH, :],
            )


def patched(pos_ref, counts, residual, ins_x):
    rows = residual.shape[1]
    sides = [side(pos_ref, 2, phase, counts[0]) for phase in range(len(ins_x))]

    def plane(z):
        low, high = from_sides(sides, ins_x, lambda ref: ref[z])
        return jnp.concatenate([low, residual[z, PAD : rows - PAD, :], high], axis=0)

    return plane


def first_kernel(counts, sizes, pos_ref, residual, *refs):
    ins_x, consts, (outer, mid), outs_z, outs_yz = groups_of(
        refs, (sizes[3], 10, 2) + sizes[1:3]
    )
    spectrum(patched(pos_ref, counts, residual, ins_x), mid, consts)
    quarter = QUARTER // 2
    recover(mid, outer, consts[6:8], lambda t: jnp.where(t < quarter, t, t + 2 * quarter))
    write_messages(pos_ref, outer, FOLD, counts, [], outs_z, outs_yz)


def inner_kernel(counts, sizes, pos_ref, outer, mid, back_x, back_y, inner, *outs_y):
    recover(mid, inner, (back_x, back_y), lambda t: t + QUARTER // 2)
    spot, _ = spots(outer.shape[1:])
    groups = WIDE // FOLD
    many = LENGTH // groups
    for phase, out in enumerate(outs_y):
        up, _ = side(pos_ref, 1, phase, counts[1])
        start = pick(up, WIDE - 1 - FOLD, 1)
        for k in range(many):
            places = [place_of(g * many + k, 2) for g in range(groups)]
            planes = [(outer, inner)[part][at] for part, at in places]
            out[k] = pack(planes, FOLD, start, spot, groups)


NINTH = WIDE
THIRD = NINTH + -(-WIDE // 8)


def edge_kernel(width, counts, sizes, pos_ref, *refs):
    extra = 1 if width == FOLD else 0
    parts = 1 + extra
    solved, ins_y, ins_z, ins_yz, modulus, outs_x, scratch = groups_of(
        refs, (parts,) + sizes[:3] + (extra, sizes[3], extra)
    )
    rows = solved[0].shape[1]
    height = 16 if extra else 8
    _, region = spots((PAD, LANES))
    third = WIDE // 3
    for phase, out in enumerate(outs_x):
        up, _ = side(pos_ref, 2, phase, counts[0])
        window = pl.ds(pl.multiple_of(pick(up, rows - height, 0), 8), height)

        found = scratch[0] if extra else out

        def put(plane, value, found=found):
            found[plane] = value

        def get(plane, found=found):
            return found[plane]

        add_messages(pos_ref, solved, width, counts, ins_y, ins_z, ins_yz, window, put, get)
        if extra:
            for z in range(WIDE):
                outer = found[z]
                out[z] = jnp.where(up, outer[8:], outer[:8])
                ninth = jnp.where(up, outer[7:8], outer[8:9])
                out[NINTH + z // 8, z % 8 : z % 8 + 1, :] = ninth
        for ref in modulus:
            place = pl.ds(pl.multiple_of(pick(up, ref.shape[1] - 2 * PAD, PAD), PAD), PAD)
            for k in range(third):
                total = ref[k, place, :]
                for c in (1, 2):
                    total = jnp.where(region == c, ref[k + c * third, place, :], total)
                out[THIRD + k] = total


def fold_kernel(width, counts, sizes, pos_ref, *refs):
    parts = 2 if width == FOLD else 1
    solved, ins_y, ins_z, ins_yz, (field,) = groups_of(
        refs, (parts,) + sizes[:3] + (1,)
    )
    rows = solved[0].shape[1]
    thin = INTERSECTION
    core = slice(thin, thin + rows)
    blank = jnp.zeros((thin, LANES), F32)

    def put(plane, value):
        field[plane, core, :] = value

    def get(plane):
        return field[plane, core, :]

    for z in range(field.shape[0]):
        field[z, :thin, :] = blank
        field[z, thin + rows :, :] = blank
    add_messages(pos_ref, solved, width, counts, ins_y, ins_z, ins_yz, None, put, get)


def second_kernel(counts, sizes, pos_ref, partial, residual, modulus, *refs):
    (
        ins_load,
        ins_x,
        consts,
        (solved, field, renewed),
        outs_y,
        outs_z,
        outs_yz,
        (mid,),
    ) = groups_of(refs, (sizes[3], sizes[3], 10, 3) + sizes[:3] + (1,))
    rows = partial.shape[1]
    complete(pos_ref, counts, partial, ins_x, True, field, 0)
    inside, low_z, high_z = grid_masks(pos_ref, rows, counts)
    before = patched(pos_ref, counts, residual, ins_load)

    def store(z, product):
        on = inside & (z >= low_z) & (z < high_z)
        renewed[z - 1] = jnp.where(on, before(z - 1) - product, 0.0)

    stiffness(field, widened(pos_ref, counts, modulus, None, ins_x), 1, WIDE - 2, 0, store, 4)
    solve(lambda z: renewed[z], mid, solved, consts)
    write_messages(pos_ref, solved, REACH, counts, outs_y, outs_z, outs_yz)


def last_kernel(counts, sizes, pos_ref, partial, modulus, beside, moved, left, *refs):
    ins_x, ins_modulus, (displacement, residual), (field,) = groups_of(
        refs, (sizes[3], sizes[3], 2, 1)
    )
    rows = partial.shape[1]
    first = planes_of(REACH)[0]
    complete(pos_ref, counts, partial, ins_x, False, field, first)
    core = slice(PAD, rows - PAD)

    def store(z, product):
        at = z - REACH
        one = (moved[z, core, :] + field[z - first, core, :]).T
        two = (left[z - 1, core, :] - product[core]).T
        for c in range(3):
            lane = c * WIDE + REACH
            displacement[c, at] = one[lane : lane + BRICK, :]
            residual[c, at] = two[lane : lane + BRICK, :]

    stiffness(
        field,
        widened(pos_ref, counts, modulus, beside, ins_modulus),
        REACH,
        REACH + BRICK - 1,
        first,
        store,
        8,
    )


def call(kernel, inputs, outs, scratch=(), distant=0, limit=24, work=0):
    return pl.pallas_call(
        kernel,
        out_shape=[jax.ShapeDtypeStruct(shape, F32) for shape in outs],
        in_specs=[SMEM] + [HBM] * distant + [VMEM] * (len(inputs) - 1 - distant),
        out_specs=[VMEM] * len(outs),
        scratch_shapes=[
            pltpu.VMEM(shape, F32) if isinstance(shape, tuple) else shape for shape in scratch
        ],
        compiler_params=pltpu.CompilerParams(vmem_limit_bytes=limit * 1024 * 1024),
        cost_estimate=pl.CostEstimate(flops=work, bytes_accessed=work, transcendentals=0),
    )(*inputs)


def local(mesh, load, labels, mask, table):
    columns = load.shape[3]
    rows = columns + 2 * PAD
    counts = tuple(lax.axis_size(axis) for axis in ("gx", "gy", "gz"))
    ways = tuple(phases(count) for count in counts)
    sizes = (ways[1], ways[2], ways[1] * ways[2], ways[0])
    pos = jnp.stack([lax.axis_index(axis) for axis in ("gz", "gy", "gx")]).astype(jnp.int32)
    consts = [jnp.asarray(value) for value in tables(columns // BRICK)]
    spectral = (LENGTH, columns // BRICK * LENGTH, LANES)

    def exchange_yz(values, filler=None):
        y, z, yz = groups_of(values, (len(values) - sizes[1] - sizes[2],) + sizes[1:3])
        z = [swap(value, mesh, {"gz": phase}, filler) for phase, value in enumerate(z)]
        y = [swap(value, mesh, {"gy": n % ways[1]}, None) for n, value in enumerate(y)]
        yz = [
            swap(value, mesh, {"gy": number // ways[2], "gz": number % ways[2]}, filler)
            for number, value in enumerate(yz)
        ]
        return [*y, *z, *yz]

    def exchange_x(values, filler=None):
        return [swap(value, mesh, {"gx": phase}, filler) for phase, value in enumerate(values)]

    def message_shapes(width, height, count=LENGTH):
        groups = WIDE // width
        return (
            [(count // groups, height, LANES)] * sizes[0]
            + [(width, height, LANES)] * sizes[1]
            + [(-(-3 * width // (LANES // width)), height, LANES)] * sizes[2]
        )

    bind = lambda kernel, *first: functools.partial(kernel, *first, counts, sizes)
    thick = along(columns)
    thin = (LENGTH, thick, LANES)
    tall = (LENGTH, rows, LANES)
    wide = (WIDE, rows, LANES)
    near = len(planes_of(REACH))

    modulus_core, *out = call(
        bind(prepare_kernel),
        [pos, table, load, labels, mask],
        [(BRICK, BRICK, columns)]
        + [(2 * BRICK + BRICK // 8, 8, columns)] * sizes[0]
        + [(3 * INTERSECTION + REACH, BRICK, columns)] * sizes[1]
        + [(6 + REACH, 8, columns)] * sizes[2],
        [
            pltpu.SMEM(table.shape, F32),
            pltpu.VMEM(labels.shape, jnp.int32),
            pltpu.VMEM(mask.shape, jnp.int32),
            pltpu.VMEM(load.shape, F32),
            pltpu.SemaphoreType.DMA((4,)),
        ],
        distant=4,
        limit=61,
    )
    margins = exchange_yz(out, "gx")
    residual, *out = call(
        bind(gather_kernel),
        [pos, load, *margins],
        [tall] + [(LENGTH, PAD, LANES)] * sizes[3],
        [(LENGTH, LANES, columns)],
    )
    from_x = exchange_x(out)
    modulus, beside = call(
        bind(modulus_kernel),
        [pos, modulus_core, *margins],
        [wide, wide],
        [(WIDE, LANES, columns)],
        work=8000000,
    )
    part = (LENGTH // 2, thick, LANES)
    first_shapes = message_shapes(FOLD, thick)
    outer, mid, *out = call(
        bind(first_kernel), [pos, residual, *from_x, *consts], [part, spectral] + first_shapes[sizes[0] :]
    )
    inner, *late = call(
        bind(inner_kernel),
        [pos, outer, mid, *consts[6:8]],
        [part] + first_shapes[: sizes[0]],
        work=8000000,
    )
    solved = [outer, inner]
    margins = exchange_yz([*late, *out])
    first_edges = exchange_x(
        call(
            bind(edge_kernel, FOLD),
            [pos, *solved, *margins, modulus],
            [(THIRD + WIDE // 3, 8, LANES)] * sizes[3],
            [(WIDE, 16, LANES)],
        )
    )
    (partial,) = call(
        bind(fold_kernel, FOLD), [pos, *solved, *margins], [wide], work=8000000
    )
    solved, moved, left, *out = call(
        bind(second_kernel),
        [pos, partial, residual, modulus, *from_x, *first_edges, *consts],
        [thin, wide, tall] + message_shapes(REACH, thick),
        [spectral],
        limit=32,
    )
    margins = exchange_yz(out, "gx")
    edges = exchange_x(
        call(
            bind(edge_kernel, REACH), [pos, solved, *margins], [(near, 8, LANES)] * sizes[3]
        ),
        "gy",
    )
    (partial,) = call(
        bind(fold_kernel, REACH), [pos, solved, *margins], [(near, rows, LANES)], work=8000000
    )
    displacement, residual = call(
        bind(last_kernel),
        [pos, partial, modulus, beside, moved, left, *edges, *first_edges],
        [load.shape, load.shape],
        [(near, rows, LANES)],
        limit=32,
    )
    return displacement, residual


def solution(mesh):
    placed = (P(None, "gz", "gy", "gx"), P("gz", "gy", "gx"), P("gz", "gy", "gx"), P())
    return jax.shard_map(
        functools.partial(local, mesh),
        mesh=mesh,
        in_specs=placed,
        out_specs=(P(None, "gz", "gy", "gx"), P(None, "gz", "gy", "gx")),
        check_vma=False,
    )
```

```python
import functools

import jax
import jax.numpy as jnp
import ml_dtypes
import numpy as np
from jax import lax
from jax.experimental import pallas as pl
from jax.experimental.pallas import tpu as pltpu
from jax.sharding import PartitionSpec as P

BRICK = 32
INTERSECTION = 4
LENGTH = BRICK + 2 * INTERSECTION
REACH = INTERSECTION + 1
WIDE = BRICK + 2 * REACH
LANES = 128
PAD = 8
FOLD = 2 * INTERSECTION + 1

LAMBDA_RATIO = 2.0
SIGMA_SHIFT = 0.1
REF_MODULUS = 1.5
VOID_MODULUS = 0.1

F32 = jnp.float32
BF16 = jnp.bfloat16
VMEM = pl.BlockSpec(memory_space=pltpu.VMEM)
SMEM = pl.BlockSpec(memory_space=pltpu.SMEM)
HBM = pl.BlockSpec(memory_space=pltpu.HBM)


def halves(values):
    values = np.asarray(values, np.float32)
    high = values.astype(ml_dtypes.bfloat16)
    low = (values - high.astype(np.float32)).astype(ml_dtypes.bfloat16)
    return high, low


def right_table(values):
    high, low = halves(values)
    return np.block([[high, low], [high, np.zeros_like(low)]]).astype(ml_dtypes.bfloat16)


def left_table(values):
    high, low = halves(values)
    return np.concatenate([high, high, low], axis=1)


def tables(count_x):
    grid = np.arange(1, LENGTH + 1, dtype=np.float64)
    sine = np.sqrt(2.0 / (LENGTH + 1)) * np.sin(np.pi * np.outer(grid, grid) / (LENGTH + 1))
    eigen = 2.0 - 2.0 * np.cos(np.pi * grid / (LENGTH + 1))
    position = np.arange(LENGTH, dtype=np.float64)
    margin = 2 * INTERSECTION
    ramp = np.minimum(
        np.minimum((position + 0.5) / margin, (LENGTH - 0.5 - position) / margin), 1.0
    )
    rows = count_x * BRICK + 2 * PAD
    ramped = ramp[:, None] * sine
    along_y = np.zeros((LANES, LANES))
    back_y = np.zeros((LANES, LANES))
    for c in range(3):
        lane = c * WIDE + 1
        along_y[lane : lane + LENGTH, c * LENGTH : (c + 1) * LENGTH] = ramped
        back_y[c * LENGTH : (c + 1) * LENGTH, lane : lane + LENGTH] = sine
    along_x = np.zeros((count_x * LENGTH, rows))
    back_x = np.zeros((rows - 2 * INTERSECTION, count_x * LENGTH))
    for b in range(count_x):
        row = b * BRICK + PAD - INTERSECTION
        along_x[b * LENGTH : (b + 1) * LENGTH, row : row + LENGTH] = ramped.T
        back_x[b * BRICK : b * BRICK + LENGTH, b * LENGTH : (b + 1) * LENGTH] = sine
    half = LENGTH // 2
    eye = np.eye(8)
    even = left_table(np.kron(ramped[:half, 0::2].T, eye))
    odd = left_table(np.kron(ramped[:half, 1::2].T, eye))
    back_even = left_table(np.kron(sine[0::2, :half].T, eye))
    back_odd = left_table(np.kron(sine[1::2, :half].T, eye))
    ratio = lambda c, d: LAMBDA_RATIO if c == d else 1.0
    base = np.ones((count_x * LENGTH, LANES))
    steps = np.zeros((LENGTH, 8, LANES))
    order = np.concatenate([np.arange(0, LENGTH, 2), np.arange(1, LENGTH, 2)])
    for c in range(3):
        part = slice(c * LENGTH, (c + 1) * LENGTH)
        base[:, part] = REF_MODULUS * (
            ratio(c, 1) * eigen[None, :]
            + ratio(c, 2) * np.tile(eigen, count_x)[:, None]
            + SIGMA_SHIFT
        )
        steps[:, :, part] = REF_MODULUS * ratio(c, 0) * eigen[order][:, None, None]
    return [
        right_table(along_y),
        left_table(along_x),
        even,
        odd,
        back_even,
        back_odd,
        left_table(back_x),
        right_table(back_y),
        base.astype(np.float32),
        steps.astype(np.float32),
    ]


def phases(count):
    return 1 if count <= 2 else 2


def partners(count, phase):
    found = [i + 1 if (i + phase) % 2 == 0 else i - 1 for i in range(count)]
    return [j if 0 <= j < count else i for i, j in enumerate(found)]


def swap(value, mesh, moves, filler):
    names = mesh.axis_names
    shape = [mesh.shape[name] for name in names]
    found = {name: partners(mesh.shape[name], phase) for name, phase in moves.items()}
    spare = None if filler is None else partners(mesh.shape[filler], 0)
    pairs = []
    for place in np.ndindex(*shape):
        target = list(place)
        for name, other in found.items():
            target[names.index(name)] = other[place[names.index(name)]]
        if any(target[names.index(name)] == place[names.index(name)] for name in found):
            target = list(place)
            if filler is not None:
                target[names.index(filler)] = spare[place[names.index(filler)]]
        pairs.append(tuple(int(np.ravel_multi_index(at, shape)) for at in (place, target)))
    if filler is None and len(found) == 1:
        ((name, other),) = found.items()
        return lax.ppermute(value, name, list(enumerate(other)))
    return lax.ppermute(value, names, pairs)


def spots(shape):
    lane = lax.broadcasted_iota(jnp.int32, shape, len(shape) - 1)
    region = jnp.where(lane >= 3 * WIDE, 3, jnp.where(lane >= 2 * WIDE, 2, jnp.where(lane >= WIDE, 1, 0)))
    spot = jnp.where(region == 3, 4 * LANES, lane - region * WIDE)
    return spot, region


def turn(values, shift):
    return pltpu.roll(values, lax.rem(shift + 2 * LANES, LANES), values.ndim - 1)


def pack(planes, width, start, spot, groups):
    total = jnp.zeros(spot.shape, F32)
    for g, plane in enumerate(planes):
        inside = (spot >= g * width) & (spot < (g + 1) * width)
        total = jnp.where(inside, turn(plane, g * width - start), total)
    return total


def unpack(packed, g, width, start, spot, use):
    inside = (spot >= start) & (spot < start + width) & use
    return jnp.where(inside, turn(packed, start - g * width), 0.0)


def side(pos_ref, dim, phase, count):
    place = pos_ref[dim]
    up = lax.rem(place + phase, 2) == 0
    use = jnp.where(up, place < count - 1, place > 0)
    return up, use


def pick(up, high, low):
    return jnp.where(up, high, low)


def two_terms(values):
    high = values.astype(BF16)
    low = (values - high.astype(F32)).astype(BF16)
    return high, low


def right_product(values, table):
    high, low = two_terms(values)
    product = jnp.dot(jnp.concatenate([high, low], axis=1), table, preferred_element_type=F32)
    return product[:, :LANES] + product[:, LANES:]


def left_product(table, values):
    high, low = two_terms(values)
    return jnp.dot(
        table, jnp.concatenate([high, low, high], axis=0), preferred_element_type=F32
    )


def along(columns):
    return columns + 2 * INTERSECTION


def solve(source, mid, target, consts):
    spectrum(source, mid, consts)
    recover(mid, target, consts[6:8], lambda t: t)


def spectrum(source, mid, consts):
    along_y, along_x, even, odd, back_even, back_odd, back_x, back_y, base, steps = consts
    half = LENGTH // 2

    def forward(t, _):
        both = jnp.concatenate([source(2 * t), source(2 * t + 1)], axis=0)
        turned = right_product(both, along_y[...])
        height = both.shape[0] // 2
        pair = jnp.concatenate([turned[:height], turned[height:]], axis=1)
        done = left_product(along_x[...], pair)
        mid[2 * t] = done[:, :LANES]
        mid[2 * t + 1] = done[:, LANES:]
        return 0

    lax.fori_loop(0, half, forward, 0, unroll=10)

    def across(g, _):
        start = pl.multiple_of(g * 16, 16)

        def plane(z):
            return jnp.concatenate(
                [mid[z, pl.ds(start, 8), :], mid[z, pl.ds(start + 8, 8), :]], axis=1
            )

        planes = [plane(z) for z in range(LENGTH)]
        sums = jnp.concatenate([planes[z] + planes[LENGTH - 1 - z] for z in range(half)], axis=0)
        gaps = jnp.concatenate([planes[z] - planes[LENGTH - 1 - z] for z in range(half)], axis=0)
        ground = jnp.concatenate(
            [base[pl.ds(start, 8), :], base[pl.ds(start + 8, 8), :]], axis=1
        )

        def divisors(first):
            return jnp.concatenate(
                [
                    ground + jnp.concatenate([steps[first + k], steps[first + k]], axis=1)
                    for k in range(half)
                ],
                axis=0,
            )

        near = left_product(back_even[...], left_product(even[...], sums) / divisors(0))
        far = left_product(back_odd[...], left_product(odd[...], gaps) / divisors(half))
        lower = near + far
        upper = near - far
        for z in range(half):
            for h in range(2):
                lanes = slice(h * LANES, (h + 1) * LANES)
                mid[z, pl.ds(start + 8 * h, 8), :] = lower[8 * z : 8 * z + 8, lanes]
                mid[LENGTH - 1 - z, pl.ds(start + 8 * h, 8), :] = upper[8 * z : 8 * z + 8, lanes]
        return 0

    lax.fori_loop(0, mid.shape[1] // 16, across, 0, unroll=5)


def recover(mid, target, consts, where):
    back_x, back_y = consts
    rows = target.shape[1]

    def backward(t, _):
        at = where(t)
        pair = jnp.concatenate([mid[2 * at], mid[2 * at + 1]], axis=1)
        done = left_product(back_x[...], pair)
        both = jnp.concatenate([done[:, :LANES], done[:, LANES:]], axis=0)
        turned = right_product(both, back_y[...])
        target[2 * t] = turned[:rows]
        target[2 * t + 1] = turned[rows:]
        return 0

    lax.fori_loop(0, target.shape[0] // 2, backward, 0, unroll=10)


def write_messages(pos_ref, solved, width, counts, outs_y, outs_z, outs_yz):
    count, rows, _ = solved.shape
    spot, _ = spots((rows, LANES))
    lane = lax.broadcasted_iota(jnp.int32, (rows, LANES), 1)
    groups = WIDE // width
    _, count_y, count_z = counts
    for phase, out in enumerate(outs_z):
        up, _ = side(pos_ref, 0, phase, count_z)
        first = pick(up, count - width, 0)
        for i in range(width):
            out[i] = solved[first + i]
    for phase, out in enumerate(outs_y):
        up, _ = side(pos_ref, 1, phase, count_y)
        start = pick(up, WIDE - 1 - width, 1)
        many = count // groups

        def one(k, _, out=out, start=start, many=many):
            out[k] = pack(
                [solved[g * many + k] for g in range(groups)], width, start, spot, groups
            )
            return 0

        lax.fori_loop(0, many, one, 0, unroll=5)
    for number, out in enumerate(outs_yz):
        phase_y, phase_z = divmod(number, len(outs_z))
        up_y, _ = side(pos_ref, 1, phase_y, count_y)
        up_z, _ = side(pos_ref, 0, phase_z, count_z)
        start = pick(up_y, WIDE - 1 - width, 1)
        first = pick(up_z, count - width, 0)
        slots = LANES // width
        for k in range(out.shape[0]):
            total = jnp.zeros((rows, LANES), F32)
            for j in range(slots):
                i, c = divmod(k * slots + j, 3)
                if i < width:
                    inside = (lane >= j * width) & (lane < (j + 1) * width)
                    moved = turn(solved[first + i], j * width - c * WIDE - start)
                    total = jnp.where(inside, moved, total)
            out[k] = total


QUARTER = LENGTH // 4


def place_of(z, parts):
    if parts == 1:
        return 0, z
    if QUARTER <= z < LENGTH - QUARTER:
        return 1, z - QUARTER
    return 0, z if z < QUARTER else z - 2 * QUARTER


def planes_of(width):
    return range(FOLD - width, WIDE - FOLD + width)


def add_messages(pos_ref, solved, width, counts, ins_y, ins_z, ins_yz, window, put, get):
    height = solved[0].shape[1] if window is None else window.size
    rows = slice(None) if window is None else window
    spot, region = spots((height, LANES))
    groups = WIDE // width
    _, count_y, count_z = counts
    parts = len(solved)
    sides_y = [side(pos_ref, 1, phase, count_y) for phase in range(len(ins_y))]
    sides_z = [side(pos_ref, 0, phase, count_z) for phase in range(len(ins_z))]
    many = LENGTH // groups
    wanted = planes_of(width)
    for z in range(LENGTH):
        if z + 1 not in wanted:
            continue
        part, at = place_of(z, parts)
        g, k = divmod(z, many)
        total = solved[part][at, rows, :]
        for (up, use), ref in zip(sides_y, ins_y):
            start = pick(up, WIDE - FOLD, FOLD - width)
            total = total + unpack(ref[k, rows, :], g, width, start, spot, use)
        put(z + 1 - wanted[0], total)
    for plane in (0, WIDE - 1):
        if plane in wanted:
            put(plane - wanted[0], jnp.zeros((height, LANES), F32))
    for phase_z, ((up_z, use_z), ref_z) in enumerate(zip(sides_z, ins_z)):
        first = pick(up_z, WIDE - FOLD - wanted[0], 0)
        for i in range(width):
            total = ref_z[i, rows, :]
            for phase_y, (up_y, use_y) in enumerate(sides_y):
                ref = ins_yz[phase_y * len(ins_z) + phase_z]
                start = pick(up_y, WIDE - FOLD, FOLD - width)
                part = jnp.zeros((height, LANES), F32)
                for c in range(3):
                    k, j = divmod(3 * i + c, LANES // width)
                    moved = turn(ref[k, rows, :], start + c * WIDE - j * width)
                    part = jnp.where(region == c, moved, part)
                inside = (spot >= start) & (spot < start + width) & use_y
                total = total + jnp.where(inside, part, 0.0)
            put(first + i, get(first + i) + jnp.where(use_z, total, 0.0))


def grid_masks(pos_ref, rows, counts):
    count_x, count_y, count_z = counts
    spot, _ = spots((rows, LANES))
    row = lax.broadcasted_iota(jnp.int32, (rows, LANES), 0)
    low_y = pick(pos_ref[1] > 0, 0, REACH)
    high_y = pick(pos_ref[1] < count_y - 1, WIDE, REACH + BRICK)
    low_x = pick(pos_ref[2] > 0, 0, PAD)
    high_x = pick(pos_ref[2] < count_x - 1, rows, rows - PAD)
    inside = (spot >= low_y) & (spot < high_y) & (row >= low_x) & (row < high_x)
    low_z = pick(pos_ref[0] > 0, 0, REACH)
    high_z = pick(pos_ref[0] < count_z - 1, WIDE, REACH + BRICK)
    return inside, low_z, high_z


def from_sides(sides, refs, index):
    low = high = None
    for (up, use), ref in zip(sides, refs):
        value = index(ref)
        one = jnp.where(use & jnp.logical_not(up), value, 0.0)
        two = jnp.where(use & up, value, 0.0)
        low = one if low is None else low + one
        high = two if high is None else high + two
    return low, high


def complete(pos_ref, counts, partial, ins_x, ninth, field, first):
    rows = field.shape[1]
    inside, low_z, high_z = grid_masks(pos_ref, rows, counts)
    sides = [side(pos_ref, 2, phase, counts[0]) for phase in range(len(ins_x))]
    row = lax.broadcasted_iota(jnp.int32, (16, LANES), 0)
    blank = jnp.zeros((8, LANES), F32)

    def one(z, _):
        low, high = from_sides(sides, ins_x, lambda ref: ref[z])
        low = pltpu.roll(jnp.concatenate([low, blank], axis=0), 4, 0)
        high = pltpu.roll(jnp.concatenate([high, blank], axis=0), 4, 0)
        if ninth:
            at = z % 8
            under, over = from_sides(
                sides, ins_x, lambda ref: ref[NINTH + z // 8, at : at + 1, :]
            )
            low = jnp.where(row == 3, under, low)
            high = jnp.where(row == 12, over, high)
        on = inside & (z + first >= low_z) & (z + first < high_z)
        whole = jnp.concatenate(
            [
                partial[z, :16, :] + low,
                partial[z, 16 : rows - 16, :],
                partial[z, rows - 16 :, :] + high,
            ],
            axis=0,
        )
        field[z] = jnp.where(on, whole, 0.0)
        return 0

    if ninth:
        for z in range(field.shape[0]):
            one(z, 0)
    else:
        for z in range(field.shape[0]):
            one(z, 0)


def widened(pos_ref, counts, modulus, beside, ins_x):
    rows = modulus.shape[1]
    sides = [side(pos_ref, 2, phase, counts[0]) for phase in range(len(ins_x))]
    _, region = spots((PAD, LANES))
    third = WIDE // 3

    def plane(z):
        c = z // third
        low, high = from_sides(sides, ins_x, lambda ref: ref[THIRD + z - c * third])
        edges = []
        for value in (low, high):
            total = turn(value, (2 * WIDE - c * WIDE))
            for target in (0, 1):
                total = jnp.where(region == target, turn(value, (target - c) * WIDE), total)
            edges.append(total)
        core = slice(PAD, rows - PAD)
        if beside is None:
            return jnp.concatenate([edges[0], modulus[z, core, :], edges[1]], axis=0), None
        low, high = (pltpu.roll(edge, LANES - 1, 1) for edge in edges)
        return (
            jnp.concatenate([edges[0], modulus[z, core, :], edges[1]], axis=0),
            jnp.concatenate([low, beside[z, core, :], high], axis=0),
        )

    return plane


def stiffness(field, modulus, first, last, shift, store, unroll):
    rows = field.shape[1]
    _, region = spots((rows, LANES))
    scale = [
        jnp.where(region == c, 0.5 * LAMBDA_RATIO, 0.5) for c in range(3)
    ]

    def one(z, carry):
        below, m, beside = carry
        v = field[z - shift]
        next_m, next_beside = modulus(z + 1)
        above = (m + next_m) * (field[z + 1 - shift] - v)
        gx = (m + pltpu.roll(m, rows - 1, 0)) * (pltpu.roll(v, rows - 1, 0) - v)
        beside = pltpu.roll(m, LANES - 1, 1) if beside is None else beside
        gy = (m + beside) * (pltpu.roll(v, LANES - 1, 1) - v)
        total = SIGMA_SHIFT * m * v + scale[0] * (below - above)
        total = total + scale[1] * (pltpu.roll(gy, 1, 1) - gy)
        total = total + scale[2] * (pltpu.roll(gx, 1, 0) - gx)
        store(z, total)
        return above, next_m, next_beside

    m, beside = modulus(first)
    below = (modulus(first - 1)[0] + m) * (field[first - shift] - field[first - 1 - shift])
    lax.fori_loop(first, last + 1, one, (below, m, beside), unroll=unroll)


def groups_of(refs, sizes):
    found = []
    at = 0
    for size in sizes:
        found.append(refs[at : at + size])
        at += size
    return found


def prepare_kernel(counts, sizes, pos_ref, table_in, load_in, labels_in, mask_in, *refs):
    (modulus_out,), outs_y, outs_z, outs_yz, fetched = groups_of(refs, (1,) + sizes[:3] + (5,))
    table_ref, labels, mask, load, arrived = fetched
    _, count_y, count_z = counts
    copies = [
        pltpu.make_async_copy(source, target, arrived.at[number])
        for number, (source, target) in enumerate(
            [(table_in, table_ref), (labels_in, labels), (mask_in, mask), (load_in, load)]
        )
    ]
    for copy in copies:
        copy.start()
    for copy in copies[:3]:
        copy.wait()

    def one(z, _):
        label = labels[z]
        looked = jnp.zeros(label.shape, F32)
        for k in range(table_ref.shape[0]):
            looked = jnp.where(label == k, table_ref[k], looked)
        modulus_out[z] = jnp.where(mask[z] == 1, looked, VOID_MODULUS)
        return 0

    lax.fori_loop(0, BRICK, one, 0, unroll=4)
    copies[3].wait()
    thin = INTERSECTION
    pairs = BRICK // 2

    def ends(plane, up, count):
        return jnp.where(up, plane[BRICK - count :, :], plane[:count, :])

    for phase, out in enumerate(outs_z):
        up, _ = side(pos_ref, 0, phase, count_z)
        first = pick(up, BRICK - thin, 0)
        for c in range(3):
            for i in range(thin):
                out[c * thin + i] = load[c, first + i]
        first = pick(up, BRICK - REACH, 0)
        for i in range(REACH):
            out[3 * thin + i] = modulus_out[first + i]
    for phase, out in enumerate(outs_y):
        up, _ = side(pos_ref, 1, phase, count_y)
        for c in range(4):
            for z in range(BRICK):
                plane = load[c, z] if c < 3 else modulus_out[z]
                row = z % 2 * thin
                out[c * pairs + z // 2, row : row + thin, :] = ends(plane, up, thin)
        for z in range(BRICK):
            plane = modulus_out[z]
            fifth = jnp.where(
                up, plane[BRICK - REACH : BRICK - thin, :], plane[thin:REACH, :]
            )
            out[4 * pairs + z // 8, z % 8 : z % 8 + 1, :] = fifth
    for number, out in enumerate(outs_yz):
        phase_y, phase_z = divmod(number, len(outs_z))
        up_y, _ = side(pos_ref, 1, phase_y, count_y)
        up_z, _ = side(pos_ref, 0, phase_z, count_z)
        first = pick(up_z, BRICK - thin, 0)
        for c in range(3):
            for i in range(thin):
                row = i % 2 * thin
                out[c * 2 + i // 2, row : row + thin, :] = ends(load[c, first + i], up_y, thin)
        first = pick(up_z, BRICK - REACH, 0)
        for i in range(REACH):
            out[6 + i] = ends(modulus_out[first + i], up_y, 8)


def gather_kernel(counts, sizes, pos_ref, load, *refs):
    ins_y, ins_z, ins_yz, (load_out,), outs_x, (wide,) = groups_of(
        refs, sizes[:3] + (1, sizes[3], 1)
    )
    columns = load.shape[3]
    rows = columns + 2 * PAD
    count_x, count_y, count_z = counts
    thin = INTERSECTION
    pairs = BRICK // 2
    sides_y = [side(pos_ref, 1, phase, count_y) for phase in range(len(ins_y))]
    sides_z = [side(pos_ref, 0, phase, count_z) for phase in range(len(ins_z))]
    blank = jnp.zeros((PAD, LANES), F32)

    def place(slot, c, centre, low, high):
        lane = c * WIDE + REACH
        wide[slot, lane : lane + BRICK, :] = centre
        wide[slot, lane - thin : lane, :] = low
        wide[slot, lane + BRICK : lane + BRICK + thin, :] = high

    def finish(z):
        load_out[z, :PAD, :] = blank
        load_out[z, PAD : PAD + columns, :] = wide[z].T
        load_out[z, rows - PAD :, :] = blank

    def clear(z, _):
        wide[z] = jnp.zeros((LANES, columns), F32)
        return 0

    lax.fori_loop(0, LENGTH, clear, 0, unroll=4)

    def pair(t, _):
        for h in range(2):
            z = 2 * t + h
            for c in range(3):
                low, high = from_sides(
                    sides_y, ins_y, lambda ref: ref[c * pairs + t, h * thin : (h + 1) * thin, :]
                )
                place(z + thin, c, load[c, z], low, high)
        for h in range(2):
            finish(2 * t + h + thin)
        return 0

    lax.fori_loop(0, pairs, pair, 0, unroll=4)
    for i in range(thin):
        row = i % 2 * thin
        for c in range(3):
            centre = from_sides(sides_z, ins_z, lambda ref: ref[c * thin + i])
            corner = [[], []]
            for phase_y in range(len(ins_y)):
                refs_z = ins_yz[phase_y * len(ins_z) : (phase_y + 1) * len(ins_z)]
                found = from_sides(
                    sides_z, refs_z, lambda ref: ref[c * 2 + i // 2, row : row + thin, :]
                )
                corner[0].append(found[0])
                corner[1].append(found[1])
            for which, slot in ((0, i), (1, thin + BRICK + i)):
                low, high = from_sides(sides_y, corner[which], lambda value: value)
                place(slot, c, centre[which], low, high)
        finish(i)
        finish(thin + BRICK + i)
    for phase, out in enumerate(outs_x):
        up, _ = side(pos_ref, 2, phase, count_x)
        start = pl.multiple_of(pick(up, rows - 2 * PAD, PAD), PAD)
        for z in range(LENGTH):
            out[z] = load_out[z, pl.ds(start, PAD), :]


def modulus_kernel(counts, sizes, pos_ref, modulus, *refs):
    ins_y, ins_z, ins_yz, (modulus_out, beside_out), (wide,) = groups_of(
        refs, sizes[:3] + (2, 1)
    )
    columns = modulus.shape[2]
    rows = columns + 2 * PAD
    count_x, count_y, count_z = counts
    thin = INTERSECTION
    pairs = BRICK // 2
    sides_y = [side(pos_ref, 1, phase, count_y) for phase in range(len(ins_y))]
    sides_z = [side(pos_ref, 0, phase, count_z) for phase in range(len(ins_z))]
    blank = jnp.zeros((PAD, LANES), F32)

    def finish(z, centre, low, high, low_end, high_end):
        for c in range(3):
            lane = c * WIDE + REACH
            wide[z, lane : lane + BRICK, :] = centre
            wide[z, lane - thin : lane, :] = low
            wide[z, lane + BRICK : lane + BRICK + thin, :] = high
            wide[z, lane - REACH : lane - thin, :] = low_end
            wide[z, lane + BRICK + thin : lane + BRICK + REACH, :] = high_end
        wide[z, 3 * WIDE :, :] = jnp.zeros((LANES - 3 * WIDE, columns), F32)
        modulus_out[z, :PAD, :] = blank
        turned = wide[z].T
        modulus_out[z, PAD : PAD + columns, :] = turned
        beside_out[z, :PAD, :] = blank
        beside_out[z, PAD : PAD + columns, :] = pltpu.roll(turned, LANES - 1, 1)
        beside_out[z, rows - PAD :, :] = blank
        modulus_out[z, rows - PAD :, :] = blank

    for z in range(BRICK):
        row = z % 2 * thin
        low, high = from_sides(
            sides_y, ins_y, lambda ref: ref[3 * pairs + z // 2, row : row + thin, :]
        )
        low_end, high_end = from_sides(
            sides_y, ins_y, lambda ref: ref[4 * pairs + z // 8, z % 8 : z % 8 + 1, :]
        )
        finish(z + REACH, modulus[z], low, high, low_end, high_end)
    for i in range(REACH):
        centre = from_sides(sides_z, ins_z, lambda ref: ref[3 * thin + i])
        corner = [[], []]
        for phase_y in range(len(ins_y)):
            refs_z = ins_yz[phase_y * len(ins_z) : (phase_y + 1) * len(ins_z)]
            found = from_sides(sides_z, refs_z, lambda ref: ref[6 + i])
            corner[0].append(found[0])
            corner[1].append(found[1])
        for which, slot in ((0, i), (1, REACH + BRICK + i)):
            low, high = from_sides(sides_y, corner[which], lambda value: value)
            finish(
                slot,
                centre[which],
                low[8 - thin :, :],
                high[:thin, :],
                low[8 - REACH : 8 - thin, :],
                high[thin:REACH, :],
            )


def patched(pos_ref, counts, residual, ins_x):
    rows = residual.shape[1]
    sides = [side(pos_ref, 2, phase, counts[0]) for phase in range(len(ins_x))]

    def plane(z):
        low, high = from_sides(sides, ins_x, lambda ref: ref[z])
        return jnp.concatenate([low, residual[z, PAD : rows - PAD, :], high], axis=0)

    return plane


def first_kernel(counts, sizes, pos_ref, residual, *refs):
    ins_x, consts, (outer, mid), outs_z, outs_yz = groups_of(
        refs, (sizes[3], 10, 2) + sizes[1:3]
    )
    spectrum(patched(pos_ref, counts, residual, ins_x), mid, consts)
    quarter = QUARTER // 2
    recover(mid, outer, consts[6:8], lambda t: jnp.where(t < quarter, t, t + 2 * quarter))
    write_messages(pos_ref, outer, FOLD, counts, [], outs_z, outs_yz)


def inner_kernel(counts, sizes, pos_ref, outer, mid, back_x, back_y, inner, *outs_y):
    recover(mid, inner, (back_x, back_y), lambda t: t + QUARTER // 2)
    spot, _ = spots(outer.shape[1:])
    groups = WIDE // FOLD
    many = LENGTH // groups
    for phase, out in enumerate(outs_y):
        up, _ = side(pos_ref, 1, phase, counts[1])
        start = pick(up, WIDE - 1 - FOLD, 1)
        for k in range(many):
            places = [place_of(g * many + k, 2) for g in range(groups)]
            planes = [(outer, inner)[part][at] for part, at in places]
            out[k] = pack(planes, FOLD, start, spot, groups)


NINTH = WIDE
THIRD = NINTH + -(-WIDE // 8)


def edge_kernel(width, counts, sizes, pos_ref, *refs):
    extra = 1 if width == FOLD else 0
    parts = 1 + extra
    solved, ins_y, ins_z, ins_yz, modulus, outs_x, scratch = groups_of(
        refs, (parts,) + sizes[:3] + (extra, sizes[3], extra)
    )
    rows = solved[0].shape[1]
    height = 16 if extra else 8
    _, region = spots((PAD, LANES))
    third = WIDE // 3
    for phase, out in enumerate(outs_x):
        up, _ = side(pos_ref, 2, phase, counts[0])
        window = pl.ds(pl.multiple_of(pick(up, rows - height, 0), 8), height)

        found = scratch[0] if extra else out

        def put(plane, value, found=found):
            found[plane] = value

        def get(plane, found=found):
            return found[plane]

        add_messages(pos_ref, solved, width, counts, ins_y, ins_z, ins_yz, window, put, get)
        if extra:
            for z in range(WIDE):
                outer = found[z]
                out[z] = jnp.where(up, outer[8:], outer[:8])
                ninth = jnp.where(up, outer[7:8], outer[8:9])
                out[NINTH + z // 8, z % 8 : z % 8 + 1, :] = ninth
        for ref in modulus:
            place = pl.ds(pl.multiple_of(pick(up, ref.shape[1] - 2 * PAD, PAD), PAD), PAD)
            for k in range(third):
                total = ref[k, place, :]
                for c in (1, 2):
                    total = jnp.where(region == c, ref[k + c * third, place, :], total)
                out[THIRD + k] = total


def fold_kernel(width, counts, sizes, pos_ref, *refs):
    parts = 2 if width == FOLD else 1
    solved, ins_y, ins_z, ins_yz, (field,) = groups_of(
        refs, (parts,) + sizes[:3] + (1,)
    )
    rows = solved[0].shape[1]
    thin = INTERSECTION
    core = slice(thin, thin + rows)
    blank = jnp.zeros((thin, LANES), F32)

    def put(plane, value):
        field[plane, core, :] = value

    def get(plane):
        return field[plane, core, :]

    for z in range(field.shape[0]):
        field[z, :thin, :] = blank
        field[z, thin + rows :, :] = blank
    add_messages(pos_ref, solved, width, counts, ins_y, ins_z, ins_yz, None, put, get)


def second_kernel(counts, sizes, pos_ref, partial, residual, modulus, *refs):
    (
        ins_load,
        ins_x,
        consts,
        (solved, field, renewed),
        outs_y,
        outs_z,
        outs_yz,
        (mid,),
    ) = groups_of(refs, (sizes[3], sizes[3], 10, 3) + sizes[:3] + (1,))
    rows = partial.shape[1]
    complete(pos_ref, counts, partial, ins_x, True, field, 0)
    inside, low_z, high_z = grid_masks(pos_ref, rows, counts)
    before = patched(pos_ref, counts, residual, ins_load)

    def store(z, product):
        on = inside & (z >= low_z) & (z < high_z)
        renewed[z - 1] = jnp.where(on, before(z - 1) - product, 0.0)

    stiffness(field, widened(pos_ref, counts, modulus, None, ins_x), 1, WIDE - 2, 0, store, 4)
    solve(lambda z: renewed[z], mid, solved, consts)
    write_messages(pos_ref, solved, REACH, counts, outs_y, outs_z, outs_yz)


def last_kernel(counts, sizes, pos_ref, partial, modulus, beside, moved, left, *refs):
    ins_x, ins_modulus, (displacement, residual), (field,) = groups_of(
        refs, (sizes[3], sizes[3], 2, 1)
    )
    rows = partial.shape[1]
    first = planes_of(REACH)[0]
    complete(pos_ref, counts, partial, ins_x, False, field, first)
    core = slice(PAD, rows - PAD)

    def store(z, product):
        at = z - REACH
        one = (moved[z, core, :] + field[z - first, core, :]).T
        two = (left[z - 1, core, :] - product[core]).T
        for c in range(3):
            lane = c * WIDE + REACH
            displacement[c, at] = one[lane : lane + BRICK, :]
            residual[c, at] = two[lane : lane + BRICK, :]

    stiffness(
        field,
        widened(pos_ref, counts, modulus, beside, ins_modulus),
        REACH,
        REACH + BRICK - 1,
        first,
        store,
        8,
    )


def call(kernel, inputs, outs, scratch=(), distant=0, limit=24, work=0):
    return pl.pallas_call(
        kernel,
        out_shape=[jax.ShapeDtypeStruct(shape, F32) for shape in outs],
        in_specs=[SMEM] + [HBM] * distant + [VMEM] * (len(inputs) - 1 - distant),
        out_specs=[VMEM] * len(outs),
        scratch_shapes=[
            pltpu.VMEM(shape, F32) if isinstance(shape, tuple) else shape for shape in scratch
        ],
        compiler_params=pltpu.CompilerParams(vmem_limit_bytes=limit * 1024 * 1024),
        cost_estimate=pl.CostEstimate(flops=work, bytes_accessed=work, transcendentals=0),
    )(*inputs)


def local(mesh, load, labels, mask, table):
    columns = load.shape[3]
    rows = columns + 2 * PAD
    counts = tuple(lax.axis_size(axis) for axis in ("gx", "gy", "gz"))
    ways = tuple(phases(count) for count in counts)
    sizes = (ways[1], ways[2], ways[1] * ways[2], ways[0])
    pos = jnp.stack([lax.axis_index(axis) for axis in ("gz", "gy", "gx")]).astype(jnp.int32)
    consts = [jnp.asarray(value) for value in tables(columns // BRICK)]
    spectral = (LENGTH, columns // BRICK * LENGTH, LANES)

    def exchange_yz(values, filler=None):
        y, z, yz = groups_of(values, (len(values) - sizes[1] - sizes[2],) + sizes[1:3])
        z = [swap(value, mesh, {"gz": phase}, filler) for phase, value in enumerate(z)]
        y = [swap(value, mesh, {"gy": n % ways[1]}, None) for n, value in enumerate(y)]
        yz = [
            swap(value, mesh, {"gy": number // ways[2], "gz": number % ways[2]}, filler)
            for number, value in enumerate(yz)
        ]
        return [*y, *z, *yz]

    def exchange_x(values, filler=None):
        return [swap(value, mesh, {"gx": phase}, filler) for phase, value in enumerate(values)]

    def message_shapes(width, height, count=LENGTH):
        groups = WIDE // width
        return (
            [(count // groups, height, LANES)] * sizes[0]
            + [(width, height, LANES)] * sizes[1]
            + [(-(-3 * width // (LANES // width)), height, LANES)] * sizes[2]
        )

    bind = lambda kernel, *first: functools.partial(kernel, *first, counts, sizes)
    thick = along(columns)
    thin = (LENGTH, thick, LANES)
    tall = (LENGTH, rows, LANES)
    wide = (WIDE, rows, LANES)
    near = len(planes_of(REACH))

    modulus_core, *out = call(
        bind(prepare_kernel),
        [pos, table, load, labels, mask],
        [(BRICK, BRICK, columns)]
        + [(2 * BRICK + BRICK // 8, 8, columns)] * sizes[0]
        + [(3 * INTERSECTION + REACH, BRICK, columns)] * sizes[1]
        + [(6 + REACH, 8, columns)] * sizes[2],
        [
            pltpu.SMEM(table.shape, F32),
            pltpu.VMEM(labels.shape, jnp.int32),
            pltpu.VMEM(mask.shape, jnp.int32),
            pltpu.VMEM(load.shape, F32),
            pltpu.SemaphoreType.DMA((4,)),
        ],
        distant=4,
        limit=61,
    )
    margins = exchange_yz(out, "gx")
    residual, *out = call(
        bind(gather_kernel),
        [pos, load, *margins],
        [tall] + [(LENGTH, PAD, LANES)] * sizes[3],
        [(LENGTH, LANES, columns)],
    )
    from_x = exchange_x(out)
    modulus, beside = call(
        bind(modulus_kernel),
        [pos, modulus_core, *margins],
        [wide, wide],
        [(WIDE, LANES, columns)],
        work=8000000,
    )
    part = (LENGTH // 2, thick, LANES)
    first_shapes = message_shapes(FOLD, thick)
    outer, mid, *out = call(
        bind(first_kernel), [pos, residual, *from_x, *consts], [part, spectral] + first_shapes[sizes[0] :]
    )
    inner, *late = call(
        bind(inner_kernel),
        [pos, outer, mid, *consts[6:8]],
        [part] + first_shapes[: sizes[0]],
        work=8000000,
    )
    solved = [outer, inner]
    margins = exchange_yz([*late, *out])
    first_edges = exchange_x(
        call(
            bind(edge_kernel, FOLD),
            [pos, *solved, *margins, modulus],
            [(THIRD + WIDE // 3, 8, LANES)] * sizes[3],
            [(WIDE, 16, LANES)],
        ),
        "gy",
    )
    (partial,) = call(
        bind(fold_kernel, FOLD), [pos, *solved, *margins], [wide], work=8000000
    )
    solved, moved, left, *out = call(
        bind(second_kernel),
        [pos, partial, residual, modulus, *from_x, *first_edges, *consts],
        [thin, wide, tall] + message_shapes(REACH, thick),
        [spectral],
        limit=32,
    )
    margins = exchange_yz(out, "gx")
    edges = exchange_x(
        call(
            bind(edge_kernel, REACH), [pos, solved, *margins], [(near, 8, LANES)] * sizes[3]
        ),
        "gy",
    )
    (partial,) = call(
        bind(fold_kernel, REACH), [pos, solved, *margins], [(near, rows, LANES)], work=8000000
    )
    displacement, residual = call(
        bind(last_kernel),
        [pos, partial, modulus, beside, moved, left, *edges, *first_edges],
        [load.shape, load.shape],
        [(near, rows, LANES)],
        limit=32,
    )
    return displacement, residual


def solution(mesh):
    placed = (P(None, "gz", "gy", "gx"), P("gz", "gy", "gx"), P("gz", "gy", "gx"), P())
    return jax.shard_map(
        functools.partial(local, mesh),
        mesh=mesh,
        in_specs=placed,
        out_specs=(P(None, "gz", "gy", "gx"), P(None, "gz", "gy", "gx")),
        check_vma=False,
    )
```
